32 devices in a mesh: dp: 8 (over z, x), mp: 4 (over y, core).
Axes of the slice: x: 2, y: 2, z: 4, core: 2. Of those that a mesh axis runs over, the one named last changes fastest.
Arguments:
- text_rows: bfloat16 [8192, 768], P(('dp', 'mp')), may hold values from -6 to 6
- segment_ids: int32 [8, 1024], P('dp'), may hold values from 0 to 7, as said below
- vocab_ids: int32 [100], replicated, may hold values from 0 to 32127
- embed_table: bfloat16 [32128, 768], P('dp'), may hold values from -6 to 6
- gain_one: float32 [768], replicated, may hold values from 0.25 to 1.75
- gain_two: float32 [768], replicated, may hold values from 0.25 to 1.75
- qkv_weight: bfloat16 [768, 3, 768], P(None, None, 'mp'), may hold values from -0.078125 to 0.078125
- out_weight: bfloat16 [768, 768], P('mp'), may hold values from -3.5 to 3.5
- ffn_in_weight: bfloat16 [768, 3072], P(None, 'mp'), may hold values from -0.21875 to 0.21875
- ffn_out_weight: bfloat16 [3072, 768], P('mp'), may hold values from -0.15625 to 0.15625
- rel_table: bfloat16 [32, 12], P(None, 'mp'), may hold values from -4 to 4
- cotangent: bfloat16 [8192, 768], P(('dp', 'mp')), may hold values from -12 to 12
- left_state: float32 [100, 100], replicated, as said below
- right_state: float32 [768, 768], P('dp'), as said below
Outputs:
- activations: bfloat16 [8192, 768], P(('dp', 'mp'))
- input_grad: float32 [8192, 768], P(('dp', 'mp'))
- prompt_grad: float32 [100, 768], replicated
- left_stat: float32 [100, 100], replicated
- right_stat: float32 [768, 768], P('dp')
- new_prompt: float32 [100, 768], replicated
The draws below stay inside these ranges and needn't reach their ends.
Inputs may be any that keep to these rules, and one draw needn't show every extreme that they name: `segment_ids`: within a pack, segment numbers start at 0 and rise by one at each new segment; a new segment begins only at a row j * 128 + s with 1 <= j <= 7 and 0 <= s < 14. Some pack has eight segments. `left_state`: symmetric and positive definite. `right_state`: symmetric and positive definite.
All inputs are finite; a program needn't handle non-finite values.
Results may differ from the reference program's by a relative error of at most 0.015.
The reference program's roundings to bfloat16 on the way count: a program that leaves them out, or rounds other values in their place, can miss the bound.
Values may be sent and summed in bfloat16 or wider, within the bound.
No kernel may reach another device: no remote copies, remote signals or barrier semaphores. Data moves between devices by JAX's collectives and lax.ppermute only.
A program may use at most 832 MiB of HBM per device.

```python
import jax
import jax.numpy as jnp
from jax import lax

D = 768
H = 12
DH = 64
FF = 3072
VOCAB = 32128
BUCKETS = 32
PROMPT = 100
PACK_LEN = 1024
ROOT_STEPS = 5
PACKS = 8
TOKENS = 8192


def stat_matrix(key, dim_size, level):
    key_diag, key_noise = jax.random.split(key)
    diagonal = jax.random.uniform(key_diag, (dim_size,), jnp.float32, 1.0, 4.0) * level
    noise_draw = jax.random.uniform(key_noise, (dim_size, dim_size), jnp.float32, -1.0, 1.0)
    coupling = (noise_draw + noise_draw.T) * (0.4 * level / dim_size)
    return coupling + jnp.diag(diagonal)


def draw_segment_ids(key, part):
    key = jax.random.fold_in(key, 11)
    key_cut, key_shift, key_pick = jax.random.split(key, 3)
    slot_rows = PACK_LEN // 8
    spread = (slot_rows - PROMPT) // 2
    cut_flags = jax.random.randint(key_cut, (PACKS, 7), 0, 2)
    chosen = jax.random.randint(key_pick, (), 0, PACKS)
    cut_flags = jnp.where(jnp.arange(PACKS, dtype=jnp.int32)[:, None] == chosen, 1, cut_flags)
    cut_shift = jax.random.randint(key_shift, (PACKS, 7), 0, spread)
    cut_rows = slot_rows * jnp.arange(1, 8, dtype=jnp.int32)[None, :] + cut_shift
    positions = jnp.arange(PACK_LEN, dtype=jnp.int32)
    passed = (positions[None, None, :] >= cut_rows[:, :, None]).astype(jnp.int32) * cut_flags[:, :, None]
    return jnp.sum(passed, axis=1).astype(jnp.int32)


def draw_cotangent(key, part):
    key = jax.random.fold_in(key, 12)
    fraction = jnp.arange(TOKENS, dtype=jnp.float32) / max(TOKENS - 1, 1)
    base_draw = jax.random.truncated_normal(key, -4.0, 4.0, (TOKENS, D), jnp.float32)
    row_scale = 1.0 + 2.0 * fraction
    return (base_draw * row_scale[:, None]).astype(jnp.bfloat16)


def draw_left_state(key, part):
    key = jax.random.fold_in(key, 13)
    return stat_matrix(key, PROMPT, 20.0 * PACKS * D)


def draw_right_state(key, part):
    key = jax.random.fold_in(key, 14)
    return stat_matrix(key, D, 20.0 * PACKS * PROMPT)


def with_ends(entries, stream_key, smallest, largest):
    index_at = [jax.random.randint(jax.random.fold_in(stream_key, axis), (), 0, length) for axis, length in enumerate(entries.shape)]
    main_axis = entries.shape.index(max(entries.shape))
    neighbour = index_at[:main_axis] + [(index_at[main_axis] + 1) % entries.shape[main_axis]] + index_at[main_axis + 1:]
    return entries.at[tuple(index_at)].set(smallest).at[tuple(neighbour)].set(largest)


def shard_levels(own_key, extent, shards, smallest, high):
    factor_of = 1.0
    for position, shards_of in shards:
        heights = jax.random.uniform(jax.random.fold_in(jax.random.fold_in(own_key, 6), position), (shards_of,), jnp.float32, smallest / len(shards), high / len(shards))
        factor_of = factor_of * jnp.repeat(jnp.exp(heights), extent[position] // shards_of).reshape((-1,) + (1,) * (len(extent) - 1 - position))
    return factor_of


def noise(stream_key, dims, scale, limit, shards=(), kind=jnp.bfloat16):
    result = jax.random.normal(stream_key, dims, jnp.float32) * scale
    if len(shards) > 0:
        result = shard_levels(stream_key, dims, shards, -0.22, 0.18) * result
    return jnp.clip(result, min=-limit, max=limit).astype(kind)


def setup_inputs(seed: int = 0) -> dict:
    seeds = jax.random.split(jax.random.key(seed), 15)
    return {
        "text_rows": noise(seeds[0], (TOKENS, D), 1.0, 6.0, ((0, 32),)),
        "segment_ids": draw_segment_ids(jax.random.fold_in(seeds[14], 71), 0),
        "vocab_ids": with_ends(jax.random.randint(seeds[2], (PROMPT,), 0, VOCAB), jax.random.fold_in(seeds[2], 1), 0, VOCAB - 1).astype(jnp.int32),
        "embed_table": noise(seeds[3], (VOCAB, D), 1.0, 6.0, ((0, 8),)),
        "gain_one": jnp.clip(1.0 + 0.15 * jax.random.normal(seeds[4], (D,), jnp.float32), 0.25, 1.75),
        "gain_two": jnp.clip(1.0 + 0.15 * jax.random.normal(seeds[5], (D,), jnp.float32), 0.25, 1.75),
        "qkv_weight": noise(seeds[6], (D, 3, H * DH), (8 * D) ** -0.5, 0.078125, ((2, 4),)),
        "out_weight": noise(seeds[7], (H * DH, D), (max(1, H * DH // 256)) ** -0.5, 3.5, ((0, 4),)),
        "ffn_in_weight": noise(seeds[8], (D, FF), D ** -0.5, 0.21875, ((1, 4),)),
        "ffn_out_weight": noise(seeds[9], (FF, D), (FF // 2) ** -0.5, 0.15625, ((0, 4),)),
        "rel_table": noise(seeds[10], (BUCKETS, H), 1.0, 4.0, ((1, 4),)),
        "cotangent": draw_cotangent(jax.random.fold_in(seeds[14], 71), 0),
        "left_state": draw_left_state(jax.random.fold_in(seeds[14], 71), 0),
        "right_state": draw_right_state(jax.random.fold_in(seeds[14], 71), 0),
    }


@jax.custom_vjp
def low(v):
    return lax.optimization_barrier(v.astype(jnp.bfloat16)).astype(jnp.float32)

@jax.custom_vjp
def low_back(v):
    return v

def low_keep(v):
    return (low(v), None)

def low_pass(kept, grad):
    return (grad,)

def back_keep(v):
    return (v, None)

def back_low(kept, grad):
    return (low(grad),)
low.defvjp(low_keep, low_pass)
low_back.defvjp(back_keep, back_low)
norm_epsilon = 1e-06
step_rate = 0.5
bucket_edges = (12, 16, 23, 32, 46, 64, 91)
highest = lax.Precision.HIGHEST

def relative_buckets(length):
    positions = jnp.arange(length, dtype=jnp.int32)
    relative = positions[None, :] - positions[:, None]
    distance = jnp.abs(relative)
    far_bucket = 8 + sum(((distance >= threshold).astype(jnp.int32) for threshold in bucket_edges))
    bucket = jnp.where(distance < 8, distance, far_bucket)
    return bucket + 16 * (relative > 0).astype(jnp.int32)

def prompt_offsets(segments):
    positions = jnp.arange(segments.shape[1], dtype=jnp.int32)
    begins = jnp.concatenate([jnp.ones_like(segments[:, :1]), (segments[:, 1:] != segments[:, :-1]).astype(jnp.int32)], axis=1)
    first_rows = lax.cummax(jnp.where(begins == 1, positions[None, :], 0), axis=1)
    return positions[None, :] - first_rows

def normalize(values, gain_row):
    return values * lax.rsqrt(lax.optimization_barrier(jnp.mean(values * values, axis=-1, keepdims=True)) + norm_epsilon) * gain_row

def layer_forward(text_pack, prompt, segment, offset, rel_bias, weights):
    qkv_mat, out_mat, up_mat, down_mat, gain_one, gain_two = weights
    inside = offset < PROMPT
    layer_in = jnp.where(inside[:, None], jnp.take(prompt, jnp.minimum(offset, PROMPT - 1), axis=0), text_pack)
    first_in = low(normalize(layer_in, gain_one))
    projected = jnp.einsum('td,dcf->tcf', first_in, qkv_mat, precision=highest)
    projected = low_back(low(projected)).reshape(PACK_LEN, 3, H, DH)
    scores = jnp.einsum('qhd,khd->hqk', projected[:, 0], projected[:, 1], precision=highest) + rel_bias
    scores = low_back(scores)
    same_doc = segment[:, None] == segment[None, :]
    scores = jnp.where(same_doc[None], scores, -1000000000.0)
    row_max = lax.optimization_barrier(jnp.max(scores, axis=-1, keepdims=True))
    exponent = jnp.exp(scores - row_max)
    attn_probs = exponent / lax.optimization_barrier(jnp.sum(exponent, axis=-1, keepdims=True))
    context = jnp.einsum('hqk,khd->qhd', low(attn_probs), projected[:, 2], precision=highest)
    context = low_back(low(context.reshape(PACK_LEN, H * DH)))
    middle = layer_in + low_back(jnp.dot(context, out_mat, precision=highest))
    second_in = low(normalize(middle, gain_two))
    hidden = low_back(jnp.dot(second_in, up_mat, precision=highest))
    active = low(jax.nn.gelu(hidden))
    return middle + low_back(jnp.dot(active, down_mat, precision=highest))

def inverse_root(matrix):
    dim_size = matrix.shape[0]
    identity = jnp.eye(dim_size, dtype=jnp.float32)
    scale_norm = 1.25 / jnp.sqrt(jnp.sum(matrix * matrix))
    current = matrix * scale_norm
    root_mat = identity * jnp.sqrt(jnp.sqrt(scale_norm))
    for repeat in range(ROOT_STEPS):
        factor = 1.25 * identity - 0.25 * current
        root_mat = jnp.dot(root_mat, factor, precision=highest)
        square = jnp.dot(factor, factor, precision=highest)
        current = jnp.dot(jnp.dot(square, square, precision=highest), current, precision=highest)
    return root_mat

def reference(text_rows, segment_ids, vocab_ids, embed_table, gain_one, gain_two, qkv_weight, out_weight, ffn_in_weight, ffn_out_weight, rel_table, cotangent, left_state, right_state):
    prompt = jnp.take(embed_table, vocab_ids, axis=0).astype(jnp.float32)
    weights = (qkv_weight.astype(jnp.float32), out_weight.astype(jnp.float32), ffn_in_weight.astype(jnp.float32), ffn_out_weight.astype(jnp.float32), gain_one, gain_two)
    rel_bias = jnp.transpose(jnp.take(rel_table.astype(jnp.float32), relative_buckets(PACK_LEN), axis=0), (2, 0, 1))
    offsets = prompt_offsets(segment_ids)
    text_packs = text_rows.reshape(PACKS, PACK_LEN, D)
    cot_packs = cotangent.reshape(PACKS, PACK_LEN, D)

    def one_pack(running, inputs):
        text_pack, cot_pack, segment, offset = inputs

        def forward(values, prompt_in):
            return layer_forward(values, prompt_in, segment, offset, rel_bias, weights)
        layer_out, pullback = jax.vjp(forward, text_pack.astype(jnp.float32), prompt)
        grad_text, grad_prompt = pullback(cot_pack.astype(jnp.float32))
        return (running + grad_prompt, (layer_out.astype(jnp.bfloat16), grad_text))
    prompt_grad, (outputs, grad_rows) = lax.scan(one_pack, jnp.zeros((PROMPT, D), jnp.float32), (text_packs, cot_packs, segment_ids, offsets))
    left_stat = 0.5 * left_state + 0.5 * jnp.dot(prompt_grad, prompt_grad.T, precision=highest)
    right_stat = 0.5 * right_state + 0.5 * jnp.dot(prompt_grad.T, prompt_grad, precision=highest)
    direction = jnp.dot(jnp.dot(inverse_root(left_stat), prompt_grad, precision=highest), inverse_root(right_stat), precision=highest)
    step_ratio = jnp.sqrt(jnp.mean(prompt * prompt) + norm_epsilon) / jnp.sqrt(jnp.mean(direction * direction) + norm_epsilon)
    new_prompt = prompt - step_rate * step_ratio * direction
    return (outputs.reshape(TOKENS, D), grad_rows.reshape(TOKENS, D), prompt_grad, left_stat, right_stat, new_prompt)
```

```python
import functools

import jax
import jax.numpy as jnp
from jax import lax
from jax.experimental import pallas as pl
from jax.experimental.pallas import tpu as pltpu
from jax.sharding import PartitionSpec as P

ROOT_STEPS = 5
HEAD = 64
SEGMENTS = 8
PENALTY = -1000000000.0

norm_epsilon = 1e-06
step_rate = 0.5
bucket_edges = (12, 16, 23, 32, 46, 64, 91)
bf16 = jnp.bfloat16
f32 = jnp.float32
MIB = 1024 * 1024

VMEM = pl.BlockSpec(memory_space=pltpu.VMEM)
SMEM = pl.BlockSpec(memory_space=pltpu.SMEM)
ANY = pl.BlockSpec(memory_space=pl.ANY)


def dot(left, right):
    return lax.dot_general(left, right, (((1,), (0,)), ((), ())), preferred_element_type=f32)


def dot_t(left, right):
    return lax.dot_general(left, right, (((1,), (1,)), ((), ())), preferred_element_type=f32)


def split(values):
    high = values.astype(bf16)
    return high, (values - high.astype(f32)).astype(bf16)


def swap(array, axis, count, bit):
    return lax.ppermute(array, axis, [(i, i ^ bit) for i in range(count)])


def rms_scale(values):
    return lax.rsqrt(jnp.mean(values * values, axis=-1, keepdims=True) + norm_epsilon)


def norm_back(values, gain, grad):
    scale = rms_scale(values)
    inner = gain * grad
    mean = jnp.mean(values * inner, axis=-1, keepdims=True)
    return scale * inner - values * (scale * scale * scale * mean)


def params(limit=56):
    return pltpu.CompilerParams(vmem_limit_bytes=limit * MIB)


def cost(flops, nbytes, trans=0):
    return pl.CostEstimate(flops=int(flops), bytes_accessed=int(nbytes), transcendentals=int(trans))


def qkv_kernel(member, x0, x1, x2, x3, gain, weight, out):
    me = member[0]
    rows = x0.shape[0]
    for step, ref in enumerate((x0, x1, x2, x3)):
        values = ref[...].astype(f32)
        normed = (values * rms_scale(values) * gain[...]).astype(bf16)
        place = pl.ds(pl.multiple_of((me ^ step) * rows, rows), rows)
        for part in range(3):
            out[part, place, :] = dot(normed, weight[part]).astype(bf16)


def merge_kernel(prompt, gain, weight, onehot, text, out):
    values = prompt[...].astype(f32)
    normed = (values * rms_scale(values) * gain[...]).astype(bf16)
    inside = jnp.max(onehot[...].astype(f32), axis=-1, keepdims=True) > 0.0
    for part in range(3):
        projected = dot(normed, weight[part]).astype(bf16)
        placed = dot(onehot[...], projected)
        out[part] = jnp.where(inside, placed, text[part].astype(f32)).astype(bf16)


def lane_head(rows, lanes):
    return lax.broadcasted_iota(jnp.int32, (rows, lanes), 1) // HEAD


def forward_kernel(steps, member, proj, key_mark, query_mark, strip, *refs):
    count = len(steps)
    contexts, exact, log_rows = refs[:count], refs[count : 2 * count], refs[2 * count : 3 * count]
    keys, value_t = refs[3 * count :]
    rows = contexts[0].shape[1]
    heads = contexts[0].shape[0] // HEAD
    length, lanes = proj.shape[1], proj.shape[2]
    keys[...] = proj[1] + key_mark[...]
    value_t[...] = jnp.transpose(proj[2])
    which = lane_head(rows, lanes)
    blocks = length // rows
    for at, step in enumerate(steps):
        block = member[0] ^ step
        place = pl.ds(pl.multiple_of(block * rows, rows), rows)
        queries = proj[0, place, :] + query_mark[place, :]
        shift = pl.ds(pl.multiple_of((blocks - 1 - block) * rows, rows), length)

        @pl.loop(0, heads)
        def _(head):
            mine = jnp.where((which == head) | (which >= heads), queries, jnp.zeros_like(queries))
            scores = dot_t(keys[...], mine) + strip[head, shift, :]
            row_max = jnp.max(scores, axis=0, keepdims=True)
            exponent = jnp.exp(scores - row_max)
            row_sum = jnp.sum(exponent, axis=0, keepdims=True)
            band = pl.ds(pl.multiple_of(head * HEAD, HEAD), HEAD)
            context = dot(value_t[band, :], exponent.astype(bf16)) * (1.0 / row_sum)
            contexts[at][band, :] = context.astype(bf16)
            exact[at][band, :] = context
            log_rows[at][pl.ds(head, 1), :] = row_max + jnp.log(row_sum)


def ffn_kernel(
    member, text, prompt, onehot, gain_two, cotangent, ctx0, ctx1, ctx2, ctx3, *refs
):
    outs_w, ups, downs = refs[:4], refs[4:8], refs[8:12]
    result, grad_middle_out, prompt_part = refs[12:15]
    sends = refs[15:19]
    out_buf, up_buf, down_buf, sems = refs[19:]
    rows = text.shape[0]

    def fetch(step, kind):
        source = (outs_w, ups, downs)[kind][step]
        target = (out_buf, up_buf, down_buf)[kind].at[step]
        return pltpu.make_async_copy(source, target, sems.at[kind, step])

    for step in range(4):
        fetch(step, 0).start()
    for step in range(4):
        fetch(step, 1).start()
        fetch(step, 2).start()

    mine = onehot[pl.ds(pl.multiple_of(member[0] * rows, rows), rows), :]
    inside = jnp.max(mine.astype(f32), axis=-1, keepdims=True) > 0.0
    layer_in = jnp.where(inside, dot(mine, prompt[...]), text[...].astype(f32))
    middle = layer_in
    for step, ref in enumerate((ctx0, ctx1, ctx2, ctx3)):
        fetch(step, 0).wait()
        middle = middle + dot(jnp.transpose(ref[...]), out_buf[step])
    second = (middle * rms_scale(middle) * gain_two[...]).astype(bf16)
    cot = cotangent[...]
    total = jnp.zeros_like(middle)
    grad_second = jnp.zeros_like(middle)
    root = 0.7978845608028654
    for step in range(4):
        fetch(step, 1).wait()
        fetch(step, 2).wait()
        hidden = dot(second, up_buf[step])
        square = hidden * hidden
        tanh = jnp.tanh(root * hidden * (1.0 + 0.044715 * square))
        half = 0.5 + 0.5 * tanh
        active = (hidden * half).astype(bf16)
        slope = half + (0.5 * root) * hidden * (1.0 - tanh * tanh) * (1.0 + 0.134145 * square)
        grad_hidden = (dot_t(cot, down_buf[step]) * slope).astype(bf16)
        total = total + dot(active, down_buf[step])
        grad_second = grad_second + dot_t(grad_hidden, up_buf[step])
    result[...] = (middle + total).astype(bf16)
    grad_middle = cot.astype(f32) + norm_back(middle, gain_two[...], grad_second)
    grad_middle_out[...] = grad_middle
    send = grad_middle.astype(bf16)
    for step in range(4):
        sends[step][...] = dot_t(out_buf[step], send).astype(bf16)
    high, low = split(grad_middle)
    mine_t = jnp.transpose(mine)
    prompt_part[...] = dot(mine_t, high) + dot(mine_t, low)


def backward_kernel(member, proj, key_mark, query_mark, strip, *refs):
    grads, exact, log_rows = refs[0:4], refs[4:8], refs[8:12]
    onehot_t, prompt, gain, weight, prompt_part, out, partial = refs[12:19]
    keys, key_t, key_sum, value_sum, prob_buf, grad_buf, query_all, out_all, query_t = refs[19:]
    rows = grads[0].shape[1]
    heads = grads[0].shape[0] // HEAD
    length, lanes = proj.shape[1], proj.shape[2]
    keys[...] = proj[1] + key_mark[...]
    key_t[...] = jnp.transpose(proj[1])
    query_t[...] = jnp.zeros_like(query_t)
    which = lane_head(rows, lanes)
    blocks = length // rows
    for step in range(4):
        block = member[0] ^ step
        place = pl.ds(pl.multiple_of(block * rows, rows), rows)
        plain = proj[0, place, :]
        queries = plain + query_mark[place, :]
        shift = pl.ds(pl.multiple_of((blocks - 1 - block) * rows, rows), length)
        grad_t = jnp.concatenate(
            [grads[step][...], jnp.zeros((lanes - heads * HEAD, rows), bf16)], axis=0
        )
        grad_out = jnp.transpose(grad_t)

        @pl.loop(0, heads)
        def _(head):
            near = which == head
            mine = jnp.where(near | (which >= heads), queries, jnp.zeros_like(queries))
            own_grad = jnp.where(near, grad_out, jnp.zeros_like(grad_out))
            band = pl.ds(pl.multiple_of(head * HEAD, HEAD), HEAD)
            stack = pl.ds(pl.multiple_of(head * rows, rows), rows)
            query_all[stack, :] = jnp.where(near, plain, jnp.zeros_like(plain))
            out_all[stack, :] = own_grad
            scores = dot_t(keys[...], mine) + strip[head, shift, :]
            probs = jnp.exp(scores - log_rows[step][pl.ds(head, 1), :])
            prob_buf[:, stack] = probs.astype(bf16)
            grad_probs = dot_t(proj[2], own_grad)
            inner = jnp.sum(
                grads[step][band, :].astype(f32) * exact[step][band, :], axis=0, keepdims=True
            )
            grad_scores = (probs * (grad_probs - inner)).astype(bf16)
            grad_buf[:, stack] = grad_scores
            query_t[band, :] = dot(key_t[band, :], grad_scores).astype(bf16)

        out[0, place, :] = jnp.transpose(query_t[...])
        more_keys = dot(grad_buf[...], query_all[...])
        more_values = dot(prob_buf[...], out_all[...])
        if step == 0:
            key_sum[...] = more_keys
            value_sum[...] = more_values
        else:
            key_sum[...] += more_keys
            value_sum[...] += more_values
    out[1] = key_sum[...].astype(bf16)
    out[2] = value_sum[...].astype(bf16)
    grad = jnp.zeros((prompt.shape[0], prompt.shape[1]), f32)
    for part in range(3):
        high, low = split(dot(onehot_t[...], out[part]))
        grad = grad + dot_t(high, weight[part]) + dot_t(low, weight[part])
    total = prompt_part[...] + norm_back(prompt[...].astype(f32), gain[...], grad)
    kept, half = partial.shape[1], partial.shape[2]
    partial[0] = total[:kept, :half]
    partial[1] = total[:kept, half:]


def first_kernel(member, grad_proj, weight, *outs):
    rows = outs[0].shape[0]
    for step, out in enumerate(outs):
        place = pl.ds(pl.multiple_of((member[0] ^ step) * rows, rows), rows)
        total = dot_t(grad_proj[0, place, :], weight[0])
        for part in (1, 2):
            total = total + dot_t(grad_proj[part, place, :], weight[part])
        out[...] = total.astype(out.dtype)


def finish_kernel(member, text, prompt, onehot, gain, grad_middle, own, received, out):
    rows = text.shape[0]
    mine = onehot[pl.ds(pl.multiple_of(member[0] * rows, rows), rows), :]
    inside = jnp.max(mine.astype(f32), axis=-1, keepdims=True) > 0.0
    layer_in = jnp.where(inside, dot(mine, prompt[...]), text[...].astype(f32))
    grad_first = own[...].astype(f32) + received[...].astype(f32)
    start = grad_middle[...] + norm_back(layer_in, gain[...], grad_first)
    out[...] = jnp.where(inside, 0.0, start)


def strip_kernel(table, out):
    heads, total, rows = out.shape
    diagonal = (total - rows) // 2
    first = diagonal - 128
    chunk = 32
    for head in range(heads):
        out[head, :first, :] = jnp.full((first, rows), table[15, head], f32)
        last = total - first - 2 * rows
        out[head, first + 2 * rows :, :] = jnp.full((last, rows), table[31, head], f32)

    @pl.loop(0, 2 * rows // chunk)
    def _(at):
        start = first + at * chunk
        key_pos = lax.broadcasted_iota(jnp.int32, (chunk, rows), 0) + start
        relative = key_pos - diagonal - lax.broadcasted_iota(jnp.int32, (chunk, rows), 1)
        distance = jnp.abs(relative)
        bucket = jnp.full((chunk, rows), 8, jnp.int32)
        for edge in bucket_edges:
            bucket = bucket + jnp.where(distance >= edge, 1, 0)
        bucket = jnp.where(distance < 8, distance, bucket) + jnp.where(relative > 0, 16, 0)
        place = pl.ds(pl.multiple_of(start, chunk), chunk)
        for head in range(heads):
            values = jnp.full((chunk, rows), table[0, head], f32)
            for index in range(1, table.shape[0]):
                values = jnp.where(bucket == index, table[index, head], values)
            out[head, place, :] = values


def newton_step(current):
    low = current.astype(bf16)
    inner = -0.625 * current + 0.0625 * dot(low, low)
    inner_low = inner.astype(bf16)
    outer = 3.125 * inner + dot(inner_low, inner_low)
    return 2.44140625 * current + dot(outer.astype(bf16), low)


def update_kernel(
    place, mine, other, prompt, left, right, band_state, grad_out, left_out, band_out, prompt_out,
    grad, left_pad, matrix,
):
    kept, half = mine.shape
    count, width = prompt_out.shape
    band = band_state.shape[0]
    grad[...] = jnp.zeros_like(grad)
    core = place[0]
    grad[:kept, pl.ds(pl.multiple_of(core * half, half), half)] = mine[...]
    grad[:kept, pl.ds(pl.multiple_of((1 - core) * half, half), half)] = other[...]
    value = grad[...]
    grad_out[...] = value[:count]
    high, low = split(value)
    high_t, low_t = jnp.transpose(high), jnp.transpose(low)
    left_new = 0.5 * left[...] + 0.5 * (dot(high, high_t) + dot(high, low_t) + dot(low, high_t))[:count, :count]
    left_out[...] = left_new
    right_new = 0.5 * right[...].astype(f32) + 0.5 * (
        dot(high_t, high) + dot(high_t, low) + dot(low_t, high)
    )
    pick = (
        lax.broadcasted_iota(jnp.int32, (band, width), 1)
        == lax.broadcasted_iota(jnp.int32, (band, width), 0) + place[1] * band
    )
    pick = jnp.where(pick, 1.0, 0.0).astype(bf16)
    pick_high, pick_low = dot_t(pick, high).astype(bf16), dot_t(pick, low).astype(bf16)
    band_out[...] = 0.5 * band_state[...] + 0.5 * (
        dot(pick_high, high) + dot(pick_high, low) + dot(pick_low, high)
    )
    left_pad[...] = jnp.zeros_like(left_pad)
    left_pad[:count, :count] = left_new
    left_mat = left_pad[...]
    left_scale = 1.25 * lax.rsqrt(jnp.sum(left_mat * left_mat))
    right_scale = 1.25 * lax.rsqrt(jnp.sum(right_new * right_new))
    left_mat = left_mat * left_scale
    matrix[...] = right_new * right_scale
    size = left_mat.shape[0]
    root = jnp.where(
        lax.broadcasted_iota(jnp.int32, (size, size), 0)
        == lax.broadcasted_iota(jnp.int32, (size, size), 1),
        1.0,
        0.0,
    )
    thin = value

    def thin_dot(values):
        return dot(values.astype(bf16), matrix[...].astype(bf16))

    for repeat in range(ROOT_STEPS):
        root = 1.25 * root - 0.25 * dot(root.astype(bf16), left_mat.astype(bf16))
        if repeat < ROOT_STEPS - 1:
            thin = 1.25 * thin - 0.25 * thin_dot(thin)
            left_mat = newton_step(left_mat)
        if repeat < ROOT_STEPS - 2:
            matrix[...] = newton_step(matrix[...])
    power = thin
    for repeat in range(4):
        power = 1.25 * power - 0.25 * thin_dot(power)
    thin = 1.25 * thin - 0.25 * thin_dot(power)
    direction = dot(root.astype(bf16), thin.astype(bf16))
    scale = jnp.sqrt(jnp.sqrt(left_scale)) * jnp.sqrt(jnp.sqrt(right_scale))
    direction = (direction * scale)[:count]
    prompt_value = prompt[...].astype(f32)[:count]
    cells = 1.0 / (count * width)
    ratio = jnp.sqrt(jnp.sum(prompt_value * prompt_value) * cells + norm_epsilon) * lax.rsqrt(
        jnp.sum(direction * direction) * cells + norm_epsilon
    )
    prompt_out[...] = prompt_value - step_rate * ratio * direction


def local(
    text_rows, segment_ids, vocab_ids, embed_table, gain_one, gain_two, qkv_weight, out_weight,
    ffn_in_weight, ffn_out_weight, rel_table, cotangent, left_state, right_state,
    *, dp_size, mp_size,
):
    member = lax.axis_index("mp")
    dp_index = lax.axis_index("dp")
    core = member % 2
    rows, width = text_rows.shape
    length = segment_ids.shape[1]
    prompt_rows = vocab_ids.shape[0]
    table_rows = embed_table.shape[0]
    heads = rel_table.shape[1]
    head_lanes = heads * HEAD
    lanes = -(-(head_lanes + SEGMENTS) // 128) * 128
    slots = 128
    kept = -(-prompt_rows // 8) * 8
    me = jnp.reshape(member, (1,))
    dp_bits = [1 << bit for bit in range(dp_size.bit_length() - 1)]

    text_y = swap(text_rows, "mp", mp_size, 2)
    text_c = swap(text_rows, "mp", mp_size, 1)
    text_d = swap(text_y, "mp", mp_size, 1)

    share = slots // 2
    ids = lax.dynamic_slice_in_dim(jnp.pad(vocab_ids, (0, slots - prompt_rows), constant_values=-1), core * share, share)
    local_ids = ids - dp_index * table_rows
    owned = (local_ids >= 0) & (local_ids < table_rows)
    found = jnp.take(embed_table, jnp.clip(local_ids, 0, table_rows - 1), axis=0)
    found = jnp.where(owned[:, None], found, jnp.zeros_like(found))
    for bit in dp_bits:
        found = found + swap(found, "dp", dp_size, bit)
    beside = swap(found, "mp", mp_size, 1)
    prompt = jnp.where(core == 0, jnp.concatenate([found, beside]), jnp.concatenate([beside, found]))

    def collect(weight):
        far = swap(weight, "mp", mp_size, 2)
        return [weight, swap(weight, "mp", mp_size, 1), far, swap(far, "mp", mp_size, 1)]

    out_all = collect(out_weight)
    up_all = collect(ffn_in_weight)
    down_all = collect(ffn_out_weight)
    right_full = lax.all_gather(right_state.astype(bf16), "dp", axis=0, tiled=True)

    segment = segment_ids.reshape(length)
    numbers = jnp.arange(SEGMENTS, dtype=jnp.int32)
    starts = jnp.sum(segment[None, :] < numbers[:, None], axis=1).astype(jnp.int32)
    same = segment[:, None] == numbers[None, :]
    first_row = jnp.sum(jnp.where(same, starts[None, :], 0), axis=1)
    offset = jnp.arange(length, dtype=jnp.int32) - first_row
    slot = jnp.where(offset < prompt_rows, offset, -1)
    onehot = (slot[:, None] == jnp.arange(slots, dtype=jnp.int32)[None, :]).astype(bf16)
    onehot_t = (slot[None, :] == jnp.arange(slots, dtype=jnp.int32)[:, None]).astype(bf16)
    lane = jnp.arange(lanes, dtype=jnp.int32)[None, :] - head_lanes
    marked = segment[:, None] == lane
    key_mark = ((lane >= 0) & (lane < SEGMENTS) & ~marked).astype(bf16)
    query_mark = jnp.where(marked, PENALTY, 0.0).astype(bf16)
    weight = jnp.pad(jnp.transpose(qkv_weight, (1, 0, 2)), ((0, 0), (0, 0), (0, lanes - head_lanes)))
    gain_a, gain_b = gain_one.reshape(1, width), gain_two.reshape(1, width)

    shape = jax.ShapeDtypeStruct
    strip = pl.pallas_call(
        strip_kernel,
        out_shape=shape((heads, 2 * length - rows, rows), f32),
        in_specs=[SMEM],
        out_specs=VMEM,
        compiler_params=params(),
        name="strip",
    )(rel_table.astype(f32))
    proj_shape = shape((3, length, lanes), bf16)
    text_proj = pl.pallas_call(
        qkv_kernel,
        out_shape=proj_shape,
        in_specs=[SMEM] + [VMEM] * 6,
        out_specs=VMEM,
        compiler_params=params(),
        cost_estimate=cost(2 * length * width * 3 * lanes, 5e6),
        name="qkv",
    )(me, text_rows, text_c, text_y, text_d, gain_a, weight)
    proj = pl.pallas_call(
        merge_kernel,
        out_shape=proj_shape,
        in_specs=[VMEM] * 5,
        out_specs=VMEM,
        compiler_params=params(),
        name="merge",
    )(prompt, gain_a, weight, onehot, text_proj)

    def forward(steps):
        count = len(steps)
        return pl.pallas_call(
            functools.partial(forward_kernel, steps),
            out_shape=[shape((head_lanes, rows), bf16)] * count
            + [shape((head_lanes, rows), f32)] * count
            + [shape((heads, rows), f32)] * count,
            in_specs=[SMEM] + [VMEM] * 4,
            out_specs=[VMEM] * (3 * count),
            scratch_shapes=[pltpu.VMEM((length, lanes), bf16), pltpu.VMEM((lanes, length), bf16)],
            compiler_params=params(),
            cost_estimate=cost(4 * length * rows * count * heads * lanes, 8e6, heads * length * rows * count),
            name="attend",
        )(me, proj, key_mark, query_mark, strip)

    ctx_2, ctx_3, exact_2, exact_3, log_2, log_3 = forward((2, 3))
    got_2, got_3 = swap(ctx_2, "mp", mp_size, 2), swap(ctx_3, "mp", mp_size, 3)
    ctx_1, ctx_0, exact_1, exact_0, log_1, log_0 = forward((1, 0))
    got_1 = swap(ctx_1, "mp", mp_size, 1)

    units = ffn_in_weight.shape[1]
    send_shape = shape((head_lanes, rows), bf16)
    result, grad_middle, prompt_part, send_0, send_1, send_2, send_3 = pl.pallas_call(
        ffn_kernel,
        out_shape=[shape((rows, width), bf16), shape((rows, width), f32), shape((slots, width), f32)]
        + [send_shape] * 4,
        in_specs=[SMEM] + [VMEM] * 9 + [ANY] * 12,
        out_specs=[VMEM] * 7,
        scratch_shapes=[
            pltpu.VMEM((4, head_lanes, width), bf16),
            pltpu.VMEM((4, width, units), bf16),
            pltpu.VMEM((4, units, width), bf16),
            pltpu.SemaphoreType.DMA((3, 4)),
        ],
        compiler_params=params(),
        cost_estimate=cost(8 * rows * width * units * 4, 12e6, rows * units * 4),
        name="ffn",
    )(me, text_rows, prompt, onehot, gain_b, cotangent, ctx_0, got_1, got_2, got_3, *out_all, *up_all, *down_all)

    back_2, back_3 = swap(send_2, "mp", mp_size, 2), swap(send_3, "mp", mp_size, 3)
    back_1 = swap(send_1, "mp", mp_size, 1)
    grad_proj, partial = pl.pallas_call(
        backward_kernel,
        out_shape=[proj_shape, shape((2, kept, width // 2), f32)],
        in_specs=[SMEM] + [VMEM] * 21,
        out_specs=[VMEM] * 2,
        scratch_shapes=[
            pltpu.VMEM((length, lanes), bf16),
            pltpu.VMEM((lanes, length), bf16),
            pltpu.VMEM((length, lanes), f32),
            pltpu.VMEM((length, lanes), f32),
            pltpu.VMEM((length, heads * rows), bf16),
            pltpu.VMEM((length, heads * rows), bf16),
            pltpu.VMEM((heads * rows, lanes), bf16),
            pltpu.VMEM((heads * rows, lanes), bf16),
            pltpu.VMEM((lanes, rows), bf16),
        ],
        compiler_params=params(),
        cost_estimate=cost(10 * length * length * heads * lanes, 14e6, heads * length * length),
        name="attend_back",
    )(
        me, proj, key_mark, query_mark, strip, send_0, back_1, back_2, back_3,
        exact_0, exact_1, exact_2, exact_3, log_0, log_1, log_2, log_3,
        onehot_t, prompt, gain_a, weight, prompt_part,
    )

    part = lax.dynamic_index_in_dim(partial, core, 0, False)
    part = part + swap(lax.dynamic_index_in_dim(partial, 1 - core, 0, False), "mp", mp_size, 1)
    part = part + swap(part, "mp", mp_size, 2)
    after_y = part
    for bit in dp_bits:
        part = part + swap(part, "dp", dp_size, bit)
    part_beside = swap(part, "mp", mp_size, 1)

    first = pl.pallas_call(
        first_kernel,
        out_shape=[shape((rows, width), bf16)] * 4,
        in_specs=[SMEM] + [VMEM] * 2,
        out_specs=[VMEM] * 4,
        compiler_params=params(),
        cost_estimate=cost(6 * length * width * lanes, 5e6),
        name="grad_first",
    )(me, grad_proj, weight)
    near = first[0] + swap(first[1], "mp", mp_size, 1)
    far = first[2] + swap(first[3], "mp", mp_size, 1)
    far, _ = lax.optimization_barrier((far, after_y))
    received = swap(far, "mp", mp_size, 2)
    input_grad = pl.pallas_call(
        finish_kernel,
        out_shape=shape((rows, width), f32),
        in_specs=[SMEM] + [VMEM] * 7,
        out_specs=VMEM,
        compiler_params=params(),
        name="finish",
    )(me, text_rows, prompt, onehot, gain_a, grad_middle, near, received)

    place = jnp.stack([core, dp_index]).astype(jnp.int32)
    band = right_state.shape[0]
    prompt_grad, left_new, right_new, new_prompt = pl.pallas_call(
        update_kernel,
        out_shape=[
            shape((prompt_rows, width), f32),
            shape((prompt_rows, prompt_rows), f32),
            shape((band, width), f32),
            shape((prompt_rows, width), f32),
        ],
        in_specs=[SMEM] + [VMEM] * 6,
        out_specs=[VMEM] * 4,
        scratch_shapes=[
            pltpu.VMEM((slots, width), f32),
            pltpu.VMEM((slots, slots), f32),
            pltpu.VMEM((width, width), f32),
        ],
        compiler_params=params(),
        cost_estimate=cost(20 * width**3, 5e6),
        name="update",
    )(place, part, part_beside, prompt, left_state, right_full, right_state)
    return result, input_grad, prompt_grad, left_new, right_new, new_prompt


def solution(mesh):
    sizes = dict(mesh.shape)
    return jax.shard_map(
        functools.partial(local, dp_size=sizes["dp"], mp_size=sizes["mp"]),
        mesh=mesh,
        in_specs=(
            P(("dp", "mp"), None),
            P("dp", None),
            P(),
            P("dp", None),
            P(),
            P(),
            P(None, None, "mp"),
            P("mp", None),
            P(None, "mp"),
            P("mp", None),
            P(None, "mp"),
            P(("dp", "mp"), None),
            P(),
            P("dp", None),
        ),
        out_specs=(P(("dp", "mp"), None), P(("dp", "mp"), None), P(), P(), P("dp", None), P()),
        check_vma=False,
    )
```

```python
import functools

import jax
import jax.numpy as jnp
from jax import lax
from jax.experimental import pallas as pl
from jax.experimental.pallas import tpu as pltpu
from jax.sharding import PartitionSpec as P

ROOT_STEPS = 5
HEAD = 64
SEGMENTS = 8
PENALTY = -1000000000.0

norm_epsilon = 1e-06
step_rate = 0.5
bucket_edges = (12, 16, 23, 32, 46, 64, 91)
bf16 = jnp.bfloat16
f32 = jnp.float32
MIB = 1024 * 1024

VMEM = pl.BlockSpec(memory_space=pltpu.VMEM)
ANY = pl.BlockSpec(memory_space=pl.ANY)
SMEM = pl.BlockSpec(memory_space=pltpu.SMEM)


def dot(left, right):
    return lax.dot_general(left, right, (((1,), (0,)), ((), ())), preferred_element_type=f32)


def dot_t(left, right):
    return lax.dot_general(left, right, (((1,), (1,)), ((), ())), preferred_element_type=f32)


def split(values):
    high = values.astype(bf16)
    return high, (values - high.astype(f32)).astype(bf16)


def swap(array, axis, count, bit, name):
    with jax.named_scope(name):
        return lax.ppermute(array, axis, [(i, i ^ bit) for i in range(count)])


def rms_scale(values):
    return lax.rsqrt(jnp.mean(values * values, axis=-1, keepdims=True) + norm_epsilon)


def norm_back(values, gain, grad):
    scale = rms_scale(values)
    inner = gain * grad
    mean = jnp.mean(values * inner, axis=-1, keepdims=True)
    return scale * inner - values * (scale * scale * scale * mean)


def params(limit=56):
    return pltpu.CompilerParams(vmem_limit_bytes=limit * MIB)


def cost(time):
    return pl.CostEstimate(flops=int(time), bytes_accessed=int(time * 3.5e6), transcendentals=0)


def relay_kernel(found, received, both, _up, _down, out, text, cotangent):
    rows = text.shape[0]
    out[...] = found[...] + received[...]
    text[...] = both[:rows]
    cotangent[...] = both[rows:]


def prep_kernel(
    member, table, segments, x0, x1, x2, x3, gain, weight,
    onehot, onehot_t, key_mark, query_mark, band, out,
):
    length = segments.shape[1]
    slots = onehot_t.shape[0]
    heads, tall, wide = band.shape
    tile = tall // 4
    segment = segments[...]
    first = jnp.zeros_like(segment)
    for number in range(1, SEGMENTS):
        before = jnp.sum(jnp.where(segment < number, 1.0, 0.0), axis=-1, keepdims=True)
        first = jnp.where(segment == number, before.astype(jnp.int32), first)
    offset = lax.broadcasted_iota(jnp.int32, segment.shape, 1) - first
    slot = jnp.where(offset < table[0, heads].astype(jnp.int32), offset, -1)
    placed = lax.broadcasted_iota(jnp.int32, (slots, length), 0) == slot
    placed = jnp.where(placed, 1.0, 0.0)
    onehot_t[...] = placed.astype(bf16)
    onehot[...] = jnp.transpose(placed).astype(bf16)
    lanes = key_mark.shape[1]
    spare = heads * HEAD % lanes
    segment_t = jnp.transpose(jnp.broadcast_to(segment.astype(f32), (lanes, length)))
    lane = lax.broadcasted_iota(jnp.int32, (length, lanes), 1) - spare
    tile_at = lax.broadcasted_iota(jnp.int32, (length, lanes), 0) // tile
    in_segment = (lane >= 0) & (lane < SEGMENTS)
    in_tile = (lane >= SEGMENTS) & (lane < SEGMENTS + length // tile)
    same = segment_t == lane.astype(f32)
    other_tile = lane - SEGMENTS
    key_mark[...] = jnp.where(
        (in_segment & ~same) | (in_tile & (tile_at == other_tile)), 1.0, 0.0
    ).astype(bf16)
    for head in range(heads):
        values = jnp.where(in_segment & same, PENALTY, 0.0)
        values = jnp.where(in_tile & (other_tile < tile_at - 1), table[15, head], values)
        values = jnp.where(in_tile & (other_tile > tile_at + 1), table[31, head], values)
        query_mark[head] = values.astype(bf16)
    rows = lax.broadcasted_iota(jnp.int32, (tile, tile), 0)
    columns = lax.broadcasted_iota(jnp.int32, (tile, tile), 1)
    zero = jnp.zeros((tile, tile), f32)
    for head in range(heads):
        band[head, :tile, tile:] = zero
        band[head, 3 * tile :, :tile] = zero
    for shift in (-1, 0, 1):
        relative = rows - columns + shift * tile
        distance = jnp.abs(relative)
        bucket = jnp.full((tile, tile), 8, jnp.int32)
        for edge in bucket_edges:
            bucket = bucket + jnp.where(distance >= edge, 1, 0)
        bucket = jnp.where(distance < 8, distance, bucket) + jnp.where(relative > 0, 16, 0)
        numbers = {-1: range(1, 16), 0: (*range(0, 16), *range(17, 32)), 1: range(17, 32)}[shift]
        values = [zero] * heads
        for number in numbers:
            here = bucket == number
            values = [jnp.where(here, table[number, head], values[head]) for head in range(heads)]
        for head in range(heads):
            for half in range(2):
                at = (shift + 1 + half) * tile
                band[head, at : at + tile, half * tile : half * tile + tile] = values[head]

    me = member[0]
    rows = x0.shape[0]
    used = weight.shape[2]
    out[:, :, used:] = jnp.zeros((3, out.shape[1], out.shape[2] - used), bf16)
    for step, ref in enumerate((x0, x1, x2, x3)):
        place = pl.ds(pl.multiple_of((me ^ step) * rows, rows), rows)
        values = ref[...].astype(f32)
        inside = jnp.max(onehot[place, :].astype(f32), axis=-1, keepdims=True) > 0.0
        scale = jnp.where(inside, 0.0, rms_scale(values))
        normed = (values * scale * gain[...].reshape(1, -1)).astype(bf16)
        for part in range(3):
            out[part, place, :used] = dot(normed, weight[part]).astype(bf16)


def lane_head(rows, lanes):
    return lax.broadcasted_iota(jnp.int32, (rows, lanes), 1) // HEAD


def marked_keys(keys, key, key_mark):
    lanes = key_mark.shape[1]
    keys[:, :lanes] = key[:, :lanes]
    keys[:, lanes:] = key[:, lanes:] + key_mark[...]


def block_scores(scores, keys, queries, marks, which, head, band, block):
    rows = queries.shape[0]
    length = keys.shape[0]
    mine = jnp.where(which == head, queries, marks)
    margin = rows // 2
    scores[margin : margin + length, :] = dot_t(keys[...], mine)
    near = pl.ds(pl.multiple_of(block * rows, rows), 2 * rows)
    scores[near, :] += band[head]
    return scores[margin : margin + length, :]


def padded_marks(query_mark, head, place, lanes):
    marks = query_mark[head, place, :]
    return jnp.concatenate([jnp.zeros((marks.shape[0], lanes - marks.shape[1]), bf16), marks], axis=1)


def attend_blocks(steps, member, proj, key_mark, query_mark, band, refs):
    contexts, exact, log_rows, keys, value_t, scores_buf = refs
    rows = contexts.shape[2]
    heads = contexts.shape[1] // HEAD
    lanes = proj.shape[2]
    marked_keys(keys, proj[1], key_mark)
    value_t[...] = jnp.transpose(proj[2])
    which = lane_head(rows, lanes)
    for at, step in enumerate(steps):
        block = member[0] ^ step
        place = pl.ds(pl.multiple_of(block * rows, rows), rows)
        queries = proj[0, place, :]
        for head in range(heads):
            marks = padded_marks(query_mark, head, place, lanes)
            scores = block_scores(
                scores_buf.at[head], keys, queries, marks, which, head, band, block
            )
            row_max = jnp.max(scores, axis=0, keepdims=True)
            exponent = jnp.exp(scores - row_max)
            row_sum = jnp.sum(exponent, axis=0, keepdims=True)
            part = slice(head * HEAD, head * HEAD + HEAD)
            context = dot(value_t[part, :], exponent.astype(bf16)) * (1.0 / row_sum)
            contexts[at, part, :] = context.astype(bf16)
            exact[at, part, :] = context
            log_rows[at, head : head + 1, :] = row_max + jnp.log(row_sum)


def join(near, far, out):
    count = near.shape[0]
    out[:count] = near[...]
    out[count:] = far[...]


def forward_first(
    steps, member, prompt, gain, weight, onehot, text, key_mark, query_mark, band, proj, *refs
):
    values = prompt[...].astype(f32)
    normed = (values * rms_scale(values) * gain[...].reshape(1, -1)).astype(bf16)
    used = weight.shape[2]
    for part in range(3):
        projected = dot(normed, weight[part]).astype(bf16)
        proj[part, :, :used] = text[part, :, :used] + dot(onehot[...], projected).astype(bf16)
    proj[:, :, used:] = text[:, :, used:]
    attend_blocks(steps, member, proj, key_mark, query_mark, band, refs)


def forward_second(steps, member, proj, key_mark, query_mark, band, near, far, joined, *refs):
    join(near, far, joined)
    attend_blocks(steps, member, proj, key_mark, query_mark, band, refs)


def own_input(member, step, text, prompt, onehot):
    rows = text.shape[0]
    mine = onehot[pl.ds(pl.multiple_of((member[0] ^ step) * rows, rows), rows), :]
    inside = jnp.max(mine.astype(f32), axis=-1, keepdims=True) > 0.0
    return mine, inside, jnp.where(inside, dot(mine, prompt[...]), text[...].astype(f32))


def middle_kernel(member, text, text_y, prompt, onehot, left, across, weight_c, weight_d, out, out_y):
    for step, rows, result in ((0, text, out), (2, text_y, out_y)):
        at = step // 2
        layer_in = own_input(member, step, rows, prompt, onehot)[2]
        added = dot(jnp.transpose(left[1 - at]), weight_c[...])
        added = added + dot(jnp.transpose(across[at]), weight_d[...])
        result[...] = layer_in + added


def ffn_kernel(step, start, gain, cotangent, near, far, *refs):
    outs_w, ups, downs = refs[:2], refs[2:4], refs[4:6]
    result, middle_out, grad_outs = refs[6], refs[7], refs[8:]
    at = step // 2
    added = dot(jnp.transpose(near[1 - at]), outs_w[0][...])
    added = added + dot(jnp.transpose(far[at]), outs_w[1][...])
    middle = start[...] + added
    if middle_out is not None:
        middle_out[...] = middle
    second = (middle * rms_scale(middle) * gain[...].reshape(1, -1)).astype(bf16)
    cot = cotangent[...]
    total = jnp.zeros_like(middle)
    grad = jnp.zeros_like(middle)
    root = 0.7978845608028654
    for up, down in zip(ups, downs):
        hidden = dot(second, up[...])
        square = hidden * hidden
        tanh = jnp.tanh(root * hidden * (1.0 + 0.044715 * square))
        half = 0.5 + 0.5 * tanh
        active = (hidden * half).astype(bf16)
        slope = half + (0.5 * root) * hidden * (1.0 - tanh * tanh) * (1.0 + 0.134145 * square)
        grad_hidden = (dot_t(cot, down[...]) * slope).astype(bf16)
        grad = grad + dot_t(grad_hidden, up[...])
        total = total + dot(active, down[...])
    half = grad.shape[0] // len(grad_outs)
    for index, out in enumerate(grad_outs):
        out[...] = grad[index * half : index * half + half].astype(out.dtype)
    result[...] = total.astype(result.dtype)


def post_kernel(member, middle, gain, cotangent, onehot, own, received, received_b, arrived, *refs):
    outs_w, grad_middle_out, prompt_part, sends = refs[:4], refs[4], refs[5], refs[6:]
    rows, half = own.shape[0], received.shape[0]
    received = jnp.concatenate([received[...], received_b[...]]).astype(f32)
    grad_second = own[...] + received
    grad_middle = cotangent[...].astype(f32) + norm_back(middle[...], gain[...].reshape(1, -1), grad_second)
    grad_middle_out[...] = grad_middle
    send = grad_middle.astype(bf16)
    for out, weight in zip(sends, outs_w):
        out[...] = dot_t(weight[...], send).astype(bf16)
    mine_t = jnp.transpose(onehot[pl.ds(pl.multiple_of(member[0] * rows, rows), rows), :])
    high, low = split(grad_middle)
    prompt_part[...] = dot(mine_t, high) + dot(mine_t, low)


def back_blocks(steps, member, proj, key_mark, query_mark, band, grads, exact, log_rows, grad_query, sums, started, buffers):
    keys, key_t, prob_buf, grad_buf, query_all, out_all, query_t, scores_buf = buffers
    key_sum, value_sum = sums
    rows = grads[0].shape[1]
    heads = grads[0].shape[0] // HEAD
    lanes = proj.shape[2]
    marked_keys(keys, proj[1], key_mark)
    key_t[...] = jnp.transpose(proj[1])
    which = lane_head(rows, lanes)
    for at, step in enumerate(steps):
        block = member[0] ^ step
        place = pl.ds(pl.multiple_of(block * rows, rows), rows)
        queries = proj[0, place, :]
        grad_t = jnp.concatenate(
            [grads[at][...], jnp.zeros((lanes - heads * HEAD, rows), bf16)], axis=0
        )
        grad_out = jnp.transpose(grad_t)
        query_t[heads * HEAD :, :] = jnp.zeros((lanes - heads * HEAD, rows), bf16)
        for head in range(heads):
            near = which == head
            own_grad = jnp.where(near, grad_out, jnp.zeros_like(grad_out))
            part = slice(head * HEAD, head * HEAD + HEAD)
            stack = slice(head * rows, head * rows + rows)
            query_all[stack, :] = jnp.where(near, queries, jnp.zeros_like(queries))
            out_all[stack, :] = own_grad
            marks = padded_marks(query_mark, head, place, lanes)
            scores = block_scores(
                scores_buf.at[head], keys, queries, marks, which, head, band, block
            )
            probs = jnp.exp(scores - log_rows[at, head : head + 1, :])
            prob_buf[:, stack] = probs.astype(bf16)
            grad_probs = dot_t(proj[2], own_grad)
            inner = jnp.sum(grads[at][part, :].astype(f32) * exact[at, part, :], axis=0, keepdims=True)
            grad_scores = (probs * (grad_probs - inner)).astype(bf16)
            grad_buf[:, stack] = grad_scores
            query_t[part, :] = dot(key_t[part, :], grad_scores).astype(bf16)
        grad_query(step, place, jnp.transpose(query_t[...]))
        more_keys = dot(grad_buf[...], query_all[...])
        more_values = dot(prob_buf[...], out_all[...])
        if at == 0 and not started:
            key_sum[...] = more_keys
            value_sum[...] = more_values
        else:
            key_sum[...] += more_keys
            value_sum[...] += more_values


def back_first(steps, member, proj, key_mark, query_mark, band, *refs):
    grads, exact, log_rows = refs[0:2], refs[2], refs[3]
    query_out, key_sum, value_sum = refs[4:7]

    def store(step, place, values):
        query_out[steps.index(step)] = values

    back_blocks(steps, member, proj, key_mark, query_mark, band, grads, exact, log_rows, store,
                (key_sum, value_sum), False, refs[7:])


def back_second(steps, member, proj, key_mark, query_mark, band, *refs):
    grads, exact, log_rows = refs[0:2], refs[2], refs[3]
    query_in, key_in, value_in = refs[4:7]
    onehot_t, prompt, gain, weight, prompt_part, out, part_mine, part_other = refs[7:15]
    key_sum, value_sum, total_buf = refs[15:18]
    rows = grads[0].shape[1]
    key_sum[...] = key_in[...]
    value_sum[...] = value_in[...]

    def store(step, place, values):
        out[0, place, :] = values

    for at in range(2):
        out[0, pl.ds(pl.multiple_of((member[0] ^ at) * rows, rows), rows), :] = query_in[at]
    back_blocks(steps, member, proj, key_mark, query_mark, band, grads, exact, log_rows, store,
                (key_sum, value_sum), True, refs[18:])
    out[1] = key_sum[...].astype(bf16)
    out[2] = value_sum[...].astype(bf16)
    grad = jnp.zeros((prompt.shape[0], prompt.shape[1]), f32)
    for part in range(3):
        high, low = split(dot(onehot_t[...], out[part])[:, : weight.shape[2]])
        grad = grad + dot_t(high, weight[part]) + dot_t(low, weight[part])
    total_buf[...] = prompt_part[...] + norm_back(prompt[...].astype(f32), gain[...].reshape(1, -1), grad)
    kept, half = part_mine.shape
    core = member[0] & 1
    part_mine[...] = total_buf[:kept, pl.ds(pl.multiple_of(core * half, half), half)]
    part_other[...] = total_buf[:kept, pl.ds(pl.multiple_of((1 - core) * half, half), half)]


def first_kernel(member, grad_proj, weight, *outs):
    rows = outs[0].shape[0]
    used = weight.shape[2]
    for step, out in enumerate(outs):
        place = pl.ds(pl.multiple_of((member[0] ^ step) * rows, rows), rows)
        total = dot_t(grad_proj[0, place, :used], weight[0])
        for part in (1, 2):
            total = total + dot_t(grad_proj[part, place, :used], weight[part])
        out[...] = total.astype(out.dtype)


def finish_kernel(member, text, prompt, onehot, gain, grad_middle, own, received, middle, own_result, far_result, out, result):
    _, inside, layer_in = own_input(member, 0, text, prompt, onehot)
    grad_first = own[...].astype(f32) + received[...].astype(f32)
    start = grad_middle[...] + norm_back(layer_in, gain[...].reshape(1, -1), grad_first)
    out[...] = jnp.where(inside, 0.0, start)
    result[...] = (middle[...] + own_result[...] + far_result[...].astype(f32)).astype(bf16)


def newton_step(current):
    low = current.astype(bf16)
    inner = -0.625 * current + 0.0625 * dot(low, low)
    inner_low = inner.astype(bf16)
    outer = 3.125 * inner + dot(inner_low, inner_low)
    return 2.44140625 * current + dot(outer.astype(bf16), low)


def update_kernel(
    place, mine, other, prompt, left, near_a, far_a, near_b, far_b, band_state, grad_out, left_out, band_out, prompt_out,
    grad, left_pad, matrix, right,
):
    kept, half = mine.shape
    count, width = prompt_out.shape
    band = band_state.shape[0]
    grad[...] = jnp.zeros_like(grad)
    core = place[0]
    half_rows = width // 2
    for side, pieces in ((core, (near_a, far_a)), (1 - core, (near_b, far_b))):
        columns = pl.ds(pl.multiple_of(side * half, half), half)
        for at in range(width // band):
            source = pieces[at * band // half_rows]
            begin = at * band % half_rows
            target = at * band
            if band % 16 == 0:
                target = pl.multiple_of((place[1] ^ at) * band, 16)
            elif at * band % half_rows:
                continue
            count_rows = band if band % 16 == 0 else half_rows
            right[pl.ds(target, count_rows), columns] = source[begin : begin + count_rows, :]
    grad[:kept, pl.ds(pl.multiple_of(core * half, half), half)] = mine[...]
    grad[:kept, pl.ds(pl.multiple_of((1 - core) * half, half), half)] = other[...]
    value = grad[...]
    grad_out[...] = value[:count]
    high, low = split(value)
    high_t, low_t = jnp.transpose(high), jnp.transpose(low)
    left_new = 0.5 * left[...] + 0.5 * (dot(high, high_t) + dot(high, low_t) + dot(low, high_t))[:count, :count]
    left_out[...] = left_new
    right_new = 0.5 * right[...].astype(f32) + 0.5 * (
        dot(high_t, high) + dot(high_t, low) + dot(low_t, high)
    )
    pick = (
        lax.broadcasted_iota(jnp.int32, (band, width), 1)
        == lax.broadcasted_iota(jnp.int32, (band, width), 0) + place[1] * band
    )
    pick = jnp.where(pick, 1.0, 0.0).astype(bf16)
    pick_high, pick_low = dot_t(pick, high).astype(bf16), dot_t(pick, low).astype(bf16)
    band_out[...] = 0.5 * band_state[...] + 0.5 * (
        dot(pick_high, high) + dot(pick_high, low) + dot(pick_low, high)
    )
    left_pad[...] = jnp.zeros_like(left_pad)
    left_pad[:count, :count] = left_new
    left_mat = left_pad[...]
    left_scale = 1.25 * lax.rsqrt(jnp.sum(left_mat * left_mat))
    right_scale = 1.25 * lax.rsqrt(jnp.sum(right_new * right_new))
    left_mat = left_mat * left_scale
    matrix[...] = right_new * right_scale
    size = left_mat.shape[0]
    root = jnp.where(
        lax.broadcasted_iota(jnp.int32, (size, size), 0)
        == lax.broadcasted_iota(jnp.int32, (size, size), 1),
        1.0,
        0.0,
    )
    thin = value

    def thin_dot(values):
        return dot(values.astype(bf16), matrix[...].astype(bf16))

    for repeat in range(ROOT_STEPS):
        root = 1.25 * root - 0.25 * dot(root.astype(bf16), left_mat.astype(bf16))
        if repeat < ROOT_STEPS - 1:
            thin = 1.25 * thin - 0.25 * thin_dot(thin)
            left_mat = newton_step(left_mat)
        if repeat < ROOT_STEPS - 2:
            matrix[...] = newton_step(matrix[...])
    power = thin
    for repeat in range(4):
        power = 1.25 * power - 0.25 * thin_dot(power)
    thin = 1.25 * thin - 0.25 * thin_dot(power)
    direction = dot(root.astype(bf16), thin.astype(bf16))
    scale = jnp.sqrt(jnp.sqrt(left_scale)) * jnp.sqrt(jnp.sqrt(right_scale))
    direction = (direction * scale)[:count]
    prompt_value = prompt[...].astype(f32)[:count]
    cells = 1.0 / (count * width)
    ratio = jnp.sqrt(jnp.sum(prompt_value * prompt_value) * cells + norm_epsilon) * lax.rsqrt(
        jnp.sum(direction * direction) * cells + norm_epsilon
    )
    prompt_out[...] = prompt_value - step_rate * ratio * direction


def local(
    text_rows, segment_ids, vocab_ids, embed_table, gain_one, gain_two, qkv_weight, out_weight,
    ffn_in_weight, ffn_out_weight, rel_table, cotangent, left_state, right_state,
    *, dp_size, mp_size,
):
    member = lax.axis_index("mp")
    dp_index = lax.axis_index("dp")
    core = member % 2
    rows, width = text_rows.shape
    length = segment_ids.shape[1]
    prompt_rows = vocab_ids.shape[0]
    table_rows = embed_table.shape[0]
    heads = rel_table.shape[1]
    head_lanes = heads * HEAD
    lanes = -(-(head_lanes + SEGMENTS + length // 128) // 128) * 128
    slots = 128
    kept = -(-prompt_rows // 8) * 8
    me = jnp.reshape(member, (1,))
    dp_bits = [1 << bit for bit in range(dp_size.bit_length() - 1)]
    shape = jax.ShapeDtypeStruct

    def to_core(array, name):
        return swap(array, "mp", mp_size, 1, name)

    def to_y(array, name):
        return swap(array, "mp", mp_size, 2, name)

    def to_across(array, name):
        return swap(array, "mp", mp_size, 3, name)

    place = jnp.stack([core, dp_index]).astype(jnp.int32)

    both_y = to_y(jnp.concatenate([text_rows, cotangent]), "text_and_cotangent_y")
    text_c = to_core(text_rows, "text_core")

    share = slots // 2
    padded = jnp.pad(vocab_ids, (0, slots - prompt_rows), constant_values=-1)
    ids = lax.dynamic_slice_in_dim(padded, core * share, share)
    local_ids = jnp.where(ids >= 0, ids - dp_index * table_rows, -1)
    owned = (local_ids >= 0) & (local_ids < table_rows)
    found = jnp.take(embed_table, jnp.clip(local_ids, 0, table_rows - 1), axis=0)
    found = jnp.where(owned[:, None], found, jnp.zeros_like(found))

    table = jnp.concatenate(
        [rel_table.astype(f32), jnp.full((rel_table.shape[0], 1), prompt_rows, f32)], axis=1
    )
    found = found + swap(found, "dp", dp_size, dp_bits[0], "prompt_x")
    found = found + swap(found, "dp", dp_size, dp_bits[1], "prompt_z")
    for bit in dp_bits[2:-1]:
        found = found + swap(found, "dp", dp_size, bit, "prompt_far")
    up_c = to_core(ffn_in_weight, "up_core")
    down_c = to_core(ffn_out_weight, "down_core")
    found, text_y, cot_y = pl.pallas_call(
        relay_kernel,
        out_shape=[shape(found.shape, bf16)] + [shape((rows, width), bf16)] * 2,
        in_specs=[VMEM] * 3 + [ANY] * 2,
        out_specs=[VMEM] * 3,
        compiler_params=params(8),
        cost_estimate=cost(0.5),
        name="relay",
    )(found, swap(found, "dp", dp_size, dp_bits[-1], "prompt_far"), both_y, up_c, down_c)
    text_d = to_core(text_y, "text_across")
    out_y = to_y(out_weight, "out_y")
    out_c = to_core(out_weight, "out_core")

    weight = jnp.transpose(qkv_weight, (1, 0, 2))
    proj_shape = shape((3, length, lanes), bf16)
    onehot, onehot_t, key_mark, query_mark, band, text_proj = pl.pallas_call(
        prep_kernel,
        out_shape=[
            shape((length, slots), bf16),
            shape((slots, length), bf16),
            shape((length, 128), bf16),
            shape((heads, length, 128), bf16),
            shape((heads, 512, 256), f32),
            proj_shape,
        ],
        in_specs=[SMEM, SMEM] + [VMEM] * 7,
        out_specs=[VMEM] * 6,
        compiler_params=params(16),
        cost_estimate=cost(3.5),
        name="project",
    )(me, table, segment_ids, text_rows, text_c, text_y, text_d, gain_one, weight)

    right_near = lax.dynamic_slice_in_dim(right_state, core * (width // 2), width // 2, 1)
    right_near = right_near.astype(bf16)
    right_x = swap(right_near, "dp", dp_size, dp_bits[0], "right_x")
    right_near = jnp.concatenate([right_near, right_x])
    right_far = swap(right_near, "dp", dp_size, dp_bits[1], "right_z")
    beside = to_core(found, "prompt_core")
    prompt = jnp.where(core == 0, jnp.concatenate([found, beside]), jnp.concatenate([beside, found]))
    out_d = to_core(out_y, "out_across")

    context_shapes = [shape((2, head_lanes, rows), bf16), shape((2, head_lanes, rows), f32), shape((2, heads, rows), f32)]
    score_buffer = pltpu.VMEM((heads, length + rows, rows), f32)
    forward_scratch = [pltpu.VMEM((length, lanes), bf16), pltpu.VMEM((lanes, length), bf16), score_buffer]
    proj, ctx_near, exact_near, log_near = pl.pallas_call(
        functools.partial(forward_first, (3, 1)),
        out_shape=[proj_shape] + context_shapes,
        in_specs=[SMEM] + [VMEM] * 8,
        out_specs=[VMEM] * 4,
        scratch_shapes=forward_scratch,
        compiler_params=params(24),
        cost_estimate=cost(4.5),
        name="attend",
    )(
        me, prompt, gain_one, weight, onehot, text_proj, key_mark, query_mark, band,
    )
    got_d = to_across(ctx_near, "context_across")
    got_c = to_core(ctx_near, "context_core")
    right_near, ctx_far, exact_far, log_far = pl.pallas_call(
        functools.partial(forward_second, (2, 0)),
        out_shape=[shape((2 * right_near.shape[0], width // 2), bf16)] + context_shapes,
        in_specs=[SMEM] + [VMEM] * 6,
        out_specs=[VMEM] * 4,
        scratch_shapes=forward_scratch,
        compiler_params=params(24),
        cost_estimate=cost(4.5),
        name="attend",
    )(me, proj, key_mark, query_mark, band, right_near, right_far)
    got_y = to_y(ctx_far, "context_y")

    units = ffn_in_weight.shape[1]
    wide = (rows, width)

    def ffn(step, start, cot, out_shape):
        body = functools.partial(ffn_kernel, step)
        if step:
            body = lambda *refs: ffn_kernel(step, *refs[:12], None, *refs[12:])
        return pl.pallas_call(
            body,
            out_shape=out_shape,
            in_specs=[VMEM] * 11,
            out_specs=[VMEM] * 3,
            compiler_params=params(24),
            cost_estimate=cost(4.5),
            name="ffn",
        )(
            start, gain_two, cot, ctx_far, got_y, out_weight, out_y,
            ffn_in_weight, up_c, ffn_out_weight, down_c,
        )

    start, start_y = pl.pallas_call(
        middle_kernel,
        out_shape=[shape(wide, f32)] * 2,
        in_specs=[SMEM] + [VMEM] * 8,
        out_specs=[VMEM] * 2,
        compiler_params=params(16),
        cost_estimate=cost(2),
        name="middle",
    )(me, text_rows, text_y, prompt, onehot, got_c, got_d, out_c, out_d)
    right_far = swap(right_near, "dp", dp_size, dp_bits[2], "right_far")
    half_rows = shape((rows // 2, width), bf16)
    far_result, *far_grad = ffn(2, start_y, cot_y, [shape(wide, bf16), half_rows, half_rows])
    got_grad = [to_y(piece, "grad_second_y") for piece in far_grad]
    own_result, middle, own_grad = ffn(0, start, cotangent, [shape(wide, f32)] * 3)

    send_shape = shape((head_lanes, rows), bf16)
    grad_middle, prompt_part, send_0, send_1, send_2, send_3 = pl.pallas_call(
        post_kernel,
        out_shape=[shape(wide, f32), shape((slots, width), f32)] + [send_shape] * 4,
        in_specs=[SMEM] + [VMEM] * 12,
        out_specs=[VMEM] * 6,
        compiler_params=params(16),
        cost_estimate=cost(2.2),
        name="post",
    )(me, middle, gain_two, cotangent, onehot, own_grad, *got_grad, right_far, out_weight, out_c, out_y, out_d)
    back_2, back_3 = to_y(send_2, "grad_context_y"), to_across(send_3, "grad_context_across")
    back_1 = to_core(send_1, "grad_context_core")
    got_result = to_y(far_result, "result_y")

    back_scratch = [
        pltpu.VMEM((length, lanes), bf16),
        pltpu.VMEM((lanes, length), bf16),
        pltpu.VMEM((length, heads * rows), bf16),
        pltpu.VMEM((length, heads * rows), bf16),
        pltpu.VMEM((heads * rows, lanes), bf16),
        pltpu.VMEM((heads * rows, lanes), bf16),
        pltpu.VMEM((lanes, rows), bf16),
        score_buffer,
    ]
    sum_shape = shape((length, lanes), f32)
    exact_a, log_a = jnp.stack([exact_far[1], exact_near[1]]), jnp.stack([log_far[1], log_near[1]])
    exact_b, log_b = jnp.stack([exact_far[0], exact_near[0]]), jnp.stack([log_far[0], log_near[0]])
    query_a, key_a, value_a = pl.pallas_call(
        functools.partial(back_first, (0, 1)),
        out_shape=[shape((2, rows, lanes), bf16), sum_shape, sum_shape],
        in_specs=[SMEM] + [VMEM] * 8,
        out_specs=[VMEM] * 3,
        scratch_shapes=back_scratch,
        compiler_params=params(32),
        cost_estimate=cost(6.5),
        name="attend_back",
    )(me, proj, key_mark, query_mark, band, send_0, back_1, exact_a, log_a)
    grad_proj, part, part_other = pl.pallas_call(
        functools.partial(back_second, (2, 3)),
        out_shape=[proj_shape] + [shape((kept, width // 2), f32)] * 2,
        in_specs=[SMEM] + [VMEM] * 16,
        out_specs=[VMEM] * 3,
        scratch_shapes=[pltpu.VMEM((length, lanes), f32)] * 2 + [pltpu.VMEM((slots, width), f32)] + back_scratch,
        compiler_params=params(36),
        cost_estimate=cost(6.5),
        name="attend_back",
    )(
        me, proj, key_mark, query_mark, band, back_2, back_3, exact_b, log_b, query_a, key_a, value_a,
        onehot_t, prompt, gain_one, weight, prompt_part,
    )

    for bit in dp_bits[3:]:
        right_near = jnp.concatenate([right_near, right_far])
        right_far = swap(right_near, "dp", dp_size, bit, "right_far")
    if right_state.shape[0] % 16:
        blocks = jnp.concatenate([right_near, right_far]).reshape(dp_size, -1, width // 2)
        blocks = jnp.take(blocks, jnp.arange(dp_size) ^ dp_index, axis=0).reshape(width, width // 2)
        right_near, right_far = blocks[: width // 2], blocks[width // 2 :]
    right_beside = [to_core(right_near, "right_core"), to_core(right_far, "right_core")]

    part = part + to_core(part_other, "prompt_grad_core")

    def add_pair(values, axis, size, bit):
        sent = values.astype(bf16)
        return sent.astype(f32) + swap(sent, axis, size, bit, "prompt_grad_sum").astype(f32)

    part = add_pair(part, "mp", mp_size, 2)
    for bit in dp_bits:
        part = add_pair(part, "dp", dp_size, bit)
    part_beside = to_core(part, "prompt_grad_other")

    first = pl.pallas_call(
        first_kernel,
        out_shape=[shape(wide, bf16)] * 4,
        in_specs=[SMEM] + [VMEM] * 2,
        out_specs=[VMEM] * 4,
        compiler_params=params(16),
        cost_estimate=cost(1.5),
        name="grad_first",
    )(me, grad_proj, weight)
    near = first[0] + to_core(first[1], "grad_first_core")
    far = first[2] + to_core(first[3], "grad_first_across")
    received = to_y(far, "grad_first_y")
    input_grad, result = pl.pallas_call(
        finish_kernel,
        out_shape=[shape(wide, f32), shape(wide, bf16)],
        in_specs=[SMEM] + [VMEM] * 10,
        out_specs=[VMEM] * 2,
        compiler_params=params(16),
        cost_estimate=cost(1.5),
        name="finish",
    )(me, text_rows, prompt, onehot, gain_one, grad_middle, near, received, middle, own_result, got_result)

    band_rows = right_state.shape[0]
    prompt_grad, left_new, right_new, new_prompt = pl.pallas_call(
        update_kernel,
        out_shape=[
            shape((prompt_rows, width), f32),
            shape((prompt_rows, prompt_rows), f32),
            shape((band_rows, width), f32),
            shape((prompt_rows, width), f32),
        ],
        in_specs=[SMEM] + [VMEM] * 9,
        out_specs=[VMEM] * 4,
        scratch_shapes=[
            pltpu.VMEM((slots, width), f32),
            pltpu.VMEM((slots, slots), f32),
            pltpu.VMEM((width, width), f32),
            pltpu.VMEM((width, width), bf16),
        ],
        compiler_params=params(32),
        cost_estimate=cost(16),
        name="update",
    )(
        place, part, part_beside, prompt, left_state, right_near, right_far, *right_beside,
        right_state,
    )
    return result, input_grad, prompt_grad, left_new, right_new, new_prompt


def solution(mesh):
    sizes = dict(mesh.shape)
    return jax.shard_map(
        functools.partial(local, dp_size=sizes["dp"], mp_size=sizes["mp"]),
        mesh=mesh,
        in_specs=(
            P(("dp", "mp"), None),
            P("dp", None),
            P(),
            P("dp", None),
            P(),
            P(),
            P(None, None, "mp"),
            P("mp", None),
            P(None, "mp"),
            P("mp", None),
            P(None, "mp"),
            P(("dp", "mp"), None),
            P(),
            P("dp", None),
        ),
        out_specs=(P(("dp", "mp"), None), P(("dp", "mp"), None), P(), P(), P("dp", None), P()),
        check_vma=False,
    )
```

```python
import functools

import jax
import jax.numpy as jnp
from jax import lax
from jax.experimental import pallas as pl
from jax.experimental.pallas import tpu as pltpu
from jax.sharding import PartitionSpec as P

ROOT_STEPS = 5
HEAD = 64
SEGMENTS = 8
PENALTY = -1000000000.0

norm_epsilon = 1e-06
step_rate = 0.5
bucket_edges = (12, 16, 23, 32, 46, 64, 91)
bf16 = jnp.bfloat16
f32 = jnp.float32
MIB = 1024 * 1024
TILE = 256

VMEM = pl.BlockSpec(memory_space=pltpu.VMEM)
ANY = pl.BlockSpec(memory_space=pl.ANY)
SMEM = pl.BlockSpec(memory_space=pltpu.SMEM)


def dot(left, right):
    return lax.dot_general(left, right, (((1,), (0,)), ((), ())), preferred_element_type=f32)


def dot_t(left, right):
    return lax.dot_general(left, right, (((1,), (1,)), ((), ())), preferred_element_type=f32)


def dot_rows(left, right):
    return lax.dot_general(left, right, (((0,), (0,)), ((), ())), preferred_element_type=f32)


def split(values):
    high = values.astype(bf16)
    return high, (values - high.astype(f32)).astype(bf16)


def swap(array, axis, count, bit, name):
    with jax.named_scope(name):
        return lax.ppermute(array, axis, [(i, i ^ bit) for i in range(count)])


def rms_scale(values):
    return lax.rsqrt(jnp.mean(values * values, axis=-1, keepdims=True) + norm_epsilon)


def norm_back(values, gain, grad):
    scale = rms_scale(values)
    inner = gain * grad
    mean = jnp.mean(values * inner, axis=-1, keepdims=True)
    return scale * inner - values * (scale * scale * scale * mean)


def params(limit=56):
    return pltpu.CompilerParams(vmem_limit_bytes=limit * MIB)


def cost(time):
    return pl.CostEstimate(flops=int(time), bytes_accessed=int(time * 3.5e6), transcendentals=0)


def stage_kernel(found, received, _text, _weight, out):
    out[...] = found[...] + received[...]


def relay_kernel(
    table, found, received, text, right, _cotangent, _up, _down, out, text_out
):
    out[...] = found[...] + received[...]
    text_out[...] = text[...]


def prep_kernel(
    member, table, segments, x0, x1, x2, x3, gain, weight,
    onehot, onehot_t, key_mark, query_mark, band, out,
):
    length = segments.shape[1]
    slots = onehot_t.shape[0]
    heads, tall, wide = band.shape
    tile = tall // 4
    segment = segments[...]
    first = jnp.zeros_like(segment)
    for number in range(1, SEGMENTS):
        before = jnp.sum(jnp.where(segment < number, 1.0, 0.0), axis=-1, keepdims=True)
        first = jnp.where(segment == number, before.astype(jnp.int32), first)
    offset = lax.broadcasted_iota(jnp.int32, segment.shape, 1) - first
    slot = jnp.where(offset < table[0, heads].astype(jnp.int32), offset, -1)
    placed = lax.broadcasted_iota(jnp.int32, (slots, length), 0) == slot
    placed = jnp.where(placed, 1.0, 0.0)
    onehot_t[...] = placed.astype(bf16)
    onehot[...] = jnp.transpose(placed).astype(bf16)
    lanes = key_mark.shape[1]
    spare = heads * HEAD % lanes
    segment_t = jnp.transpose(jnp.broadcast_to(segment.astype(f32), (lanes, length)))
    lane = lax.broadcasted_iota(jnp.int32, (length, lanes), 1) - spare
    tile_at = lax.broadcasted_iota(jnp.int32, (length, lanes), 0) // tile
    in_segment = (lane >= 0) & (lane < SEGMENTS)
    in_tile = (lane >= SEGMENTS) & (lane < SEGMENTS + length // tile)
    same = segment_t == lane.astype(f32)
    other_tile = lane - SEGMENTS
    key_mark[...] = jnp.where(
        (in_segment & ~same) | (in_tile & (tile_at == other_tile)), 1.0, 0.0
    ).astype(bf16)
    for head in range(heads):
        values = jnp.where(in_segment & same, PENALTY, 0.0)
        values = jnp.where(in_tile & (other_tile < tile_at - 1), table[15, head], values)
        values = jnp.where(in_tile & (other_tile > tile_at + 1), table[31, head], values)
        query_mark[head] = values.astype(bf16)
    rows = lax.broadcasted_iota(jnp.int32, (tile, tile), 0)
    columns = lax.broadcasted_iota(jnp.int32, (tile, tile), 1)
    zero = jnp.zeros((tile, tile), f32)
    for head in range(heads):
        band[head, :tile, tile:] = zero
        band[head, 3 * tile :, :tile] = zero
    for shift in (-1, 0, 1):
        relative = rows - columns + shift * tile
        distance = jnp.abs(relative)
        bucket = jnp.full((tile, tile), 8, jnp.int32)
        for edge in bucket_edges:
            bucket = bucket + jnp.where(distance >= edge, 1, 0)
        bucket = jnp.where(distance < 8, distance, bucket) + jnp.where(relative > 0, 16, 0)
        numbers = {-1: range(1, 16), 0: (*range(0, 16), *range(17, 32)), 1: range(17, 32)}[shift]
        values = [zero] * heads
        for number in numbers:
            here = bucket == number
            values = [jnp.where(here, table[number, head], values[head]) for head in range(heads)]
        for head in range(heads):
            for half in range(2):
                at = (shift + 1 + half) * tile
                band[head, at : at + tile, half * tile : half * tile + tile] = values[head]

    me = member[0]
    rows = x0.shape[0]
    used = weight.shape[2]
    out[:, :, used:] = jnp.zeros((3, out.shape[1], out.shape[2] - used), bf16)
    for step, ref in enumerate((x0, x1, x2, x3)):
        place = pl.ds(pl.multiple_of((me ^ step) * rows, rows), rows)
        values = ref[...].astype(f32)
        inside = jnp.max(onehot[place, :].astype(f32), axis=-1, keepdims=True) > 0.0
        scale = jnp.where(inside, 0.0, rms_scale(values))
        normed = (values * scale * gain[...].reshape(1, -1)).astype(bf16)
        for part in range(3):
            out[part, place, :used] = dot(normed, weight[part]).astype(bf16)


def lane_head(rows, lanes):
    return lax.broadcasted_iota(jnp.int32, (rows, lanes), 1) // HEAD


def marked_keys(keys, key, key_mark):
    lanes = key_mark.shape[1]
    keys[:, :lanes] = key[:, :lanes]
    keys[:, lanes:] = key[:, lanes:] + key_mark[...]


def block_scores(scores, keys, queries, marks, which, head, band, block):
    rows = queries.shape[0]
    length = keys.shape[0]
    mine = jnp.where(which == head, queries, marks)
    margin = rows // 2
    scores[margin : margin + length, :] = dot_t(keys[...], mine)
    near = pl.ds(pl.multiple_of(block * rows, rows), 2 * rows)
    scores[near, :] += band[head]
    return scores[margin : margin + length, :]


def padded_marks(query_mark, head, place, lanes):
    marks = query_mark[head, place, :]
    return jnp.concatenate([jnp.zeros((marks.shape[0], lanes - marks.shape[1]), bf16), marks], axis=1)


def attend_blocks(steps, member, proj, key_mark, query_mark, band, refs):
    contexts, exact, log_rows, keys, scores_buf = refs
    rows = contexts.shape[2]
    used = contexts.shape[1]
    heads = used // HEAD
    lanes = proj.shape[2]
    marked_keys(keys, proj[1], key_mark)
    which = lane_head(rows, lanes)
    for at, step in enumerate(steps):
        block = member[0] ^ step
        place = pl.ds(pl.multiple_of(block * rows, rows), rows)
        queries = proj[0, place, :]
        mixed = jnp.zeros((rows, lanes), f32)
        sums = []
        for head in range(heads):
            marks = padded_marks(query_mark, head, place, lanes)
            scores = block_scores(
                scores_buf.at[head], keys, queries, marks, which, head, band, block
            )
            row_max = jnp.max(scores, axis=0, keepdims=True)
            exponent = jnp.exp(scores - row_max)
            row_sum = jnp.sum(exponent, axis=0, keepdims=True)
            mixed = jnp.where(which == head, dot_rows(exponent.astype(bf16), proj[2]), mixed)
            log_rows[at, head : head + 1, :] = row_max + jnp.log(row_sum)
            sums.append(jnp.broadcast_to(1.0 / row_sum, (HEAD, rows)))
        context = jnp.transpose(mixed)[:used] * jnp.concatenate(sums, axis=0)
        contexts[at] = context.astype(bf16)
        exact[at] = context


def join(near, far, out):
    count = near.shape[0]
    out[:count] = near[...]
    out[count:] = far[...]


def forward_first(
    steps, member, found, beside, gain, weight, onehot, text, key_mark, query_mark, band,
    near, far, prompt, proj, joined, *refs
):
    join(near, far, joined)
    share = found.shape[0]
    core = member[0] & 1
    prompt[pl.ds(pl.multiple_of(core * share, share), share), :] = found[...]
    prompt[pl.ds(pl.multiple_of((1 - core) * share, share), share), :] = beside[...]
    values = prompt[...].astype(f32)
    normed = (values * rms_scale(values) * gain[...].reshape(1, -1)).astype(bf16)
    used = weight.shape[2]
    for part in range(3):
        projected = dot(normed, weight[part]).astype(bf16)
        proj[part, :, :used] = text[part, :, :used] + dot(onehot[...], projected).astype(bf16)
    proj[:, :, used:] = text[:, :, used:]
    attend_blocks(steps, member, proj, key_mark, query_mark, band, refs)


def forward_second(steps, member, proj, key_mark, query_mark, band, near, far, joined, *refs):
    join(near, far, joined)
    attend_blocks(steps, member, proj, key_mark, query_mark, band, refs)


def own_input(member, step, text, prompt, onehot):
    rows = text.shape[0]
    mine = onehot[pl.ds(pl.multiple_of((member[0] ^ step) * rows, rows), rows), :]
    inside = jnp.max(mine.astype(f32), axis=-1, keepdims=True) > 0.0
    return mine, inside, jnp.where(inside, dot(mine, prompt[...]), text[...].astype(f32))


def middle_kernel(
    member, text, text_y, prompt, onehot, left, across, weights, cotangent, out, out_y, cot_out
):
    cot_out[...] = cotangent[...]
    for step, rows, result in ((0, text, out), (2, text_y, out_y)):
        at = step // 2
        layer_in = own_input(member, step, rows, prompt, onehot)[2]
        part = left.shape[1]
        added = dot(jnp.transpose(left[1 - at]), weights[:part])
        added = added + dot(jnp.transpose(across[at]), weights[part:])
        result[...] = layer_in + added


def ffn_kernel(step, start, gain, cotangent, near, far, *refs):
    outs_w, ups, downs = refs[:2], refs[2:4], refs[4:6]
    result, middle_out, grad_outs = refs[6], refs[7], refs[8:]
    at = step // 2
    added = dot(jnp.transpose(near[1 - at]), outs_w[0][...])
    added = added + dot(jnp.transpose(far[at]), outs_w[1][...])
    middle = start[...] + added
    if middle_out is not None:
        middle_out[...] = middle
    second = (middle * rms_scale(middle) * gain[...].reshape(1, -1)).astype(bf16)
    cot = cotangent[...]
    total = jnp.zeros_like(middle)
    grad = jnp.zeros_like(middle)
    root = 0.7978845608028654
    for up, down in zip(ups, downs):
        hidden = dot(second, up[...])
        square = hidden * hidden
        tanh = jnp.tanh(root * hidden * (1.0 + 0.044715 * square))
        half = 0.5 + 0.5 * tanh
        active = (hidden * half).astype(bf16)
        slope = half + (0.5 * root) * hidden * (1.0 - tanh * tanh) * (1.0 + 0.134145 * square)
        grad_hidden = (dot_t(cot, down[...]) * slope).astype(bf16)
        grad = grad + dot_t(grad_hidden, up[...])
        total = total + dot(active, down[...])
    half = grad.shape[0] // len(grad_outs)
    for index, out in enumerate(grad_outs):
        out[...] = grad[index * half : index * half + half].astype(out.dtype)
    result[...] = total.astype(result.dtype)


def post_kernel(member, middle, gain, cotangent, onehot, own, received, received_b, *refs):
    weight, weight_y, pair, grad_middle_out, prompt_part = refs[:5]
    sends = refs[5:]
    part = weight.shape[0]
    outs_w = (weight, pair.at[:part], weight_y, pair.at[part:])
    rows, half = own.shape[0], received.shape[0]
    received = jnp.concatenate([received[...], received_b[...]]).astype(f32)
    grad_second = own[...] + received
    grad_middle = cotangent[...].astype(f32) + norm_back(middle[...], gain[...].reshape(1, -1), grad_second)
    grad_middle_out[...] = grad_middle
    send = grad_middle.astype(bf16)
    for out, weight in zip(sends, outs_w):
        out[...] = dot_t(weight[...], send).astype(bf16)
    mine_t = jnp.transpose(onehot[pl.ds(pl.multiple_of(member[0] * rows, rows), rows), :])
    high, low = split(grad_middle)
    prompt_part[...] = dot(mine_t, high) + dot(mine_t, low)


def back_blocks(steps, member, proj, key_mark, query_mark, band, grads, exact, log_rows, grad_query, sums, started, buffers):
    keys, prob_buf, grad_buf, query_all, out_all, scores_buf = buffers
    key_sum, value_sum = sums
    rows = grads[0].shape[1]
    heads = grads[0].shape[0] // HEAD
    lanes = proj.shape[2]
    marked_keys(keys, proj[1], key_mark)
    which = lane_head(rows, lanes)
    for at, step in enumerate(steps):
        block = member[0] ^ step
        place = pl.ds(pl.multiple_of(block * rows, rows), rows)
        queries = proj[0, place, :]
        grad_t = jnp.concatenate(
            [grads[at][...], jnp.zeros((lanes - heads * HEAD, rows), bf16)], axis=0
        )
        grad_out = jnp.transpose(grad_t)
        mixed = jnp.zeros((rows, lanes), f32)
        for head in range(heads):
            near = which == head
            own_grad = jnp.where(near, grad_out, jnp.zeros_like(grad_out))
            part = slice(head * HEAD, head * HEAD + HEAD)
            stack = slice(head * rows, head * rows + rows)
            query_all[stack, :] = jnp.where(near, queries, jnp.zeros_like(queries))
            out_all[stack, :] = own_grad
            marks = padded_marks(query_mark, head, place, lanes)
            scores = block_scores(
                scores_buf.at[head], keys, queries, marks, which, head, band, block
            )
            probs = jnp.exp(scores - log_rows[at, head : head + 1, :])
            prob_buf[:, stack] = probs.astype(bf16)
            grad_probs = dot_t(proj[2], own_grad)
            inner = jnp.sum(grads[at][part, :].astype(f32) * exact[at, part, :], axis=0, keepdims=True)
            grad_scores = (probs * (grad_probs - inner)).astype(bf16)
            grad_buf[:, stack] = grad_scores
            mixed = jnp.where(near, dot_rows(grad_scores, proj[1]), mixed)
        grad_query(step, place, mixed.astype(bf16))
        more_keys = dot(grad_buf[...], query_all[...])
        more_values = dot(prob_buf[...], out_all[...])
        if at == 0 and not started:
            key_sum[...] = more_keys
            value_sum[...] = more_values
        else:
            key_sum[...] += more_keys
            value_sum[...] += more_values


def back_first(steps, member, proj, key_mark, query_mark, band, *refs):
    grads, exact, log_rows = refs[0:2], refs[2], refs[3]
    query_out, key_sum, value_sum = refs[4:7]

    def store(step, place, values):
        query_out[steps.index(step)] = values

    back_blocks(steps, member, proj, key_mark, query_mark, band, grads, exact, log_rows, store,
                (key_sum, value_sum), False, refs[7:])


def back_second(steps, member, proj, key_mark, query_mark, band, *refs):
    grads, exact, log_rows = refs[0:2], refs[2], refs[3]
    query_in, key_in, value_in = refs[4:7]
    onehot_t, prompt, gain, weight, prompt_part, _, out, part_mine, part_other = refs[7:16]
    key_sum, value_sum, total_buf = refs[16:19]
    rows = grads[0].shape[1]
    key_sum[...] = key_in[...]
    value_sum[...] = value_in[...]

    def store(step, place, values):
        out[0, place, :] = values

    for at in range(2):
        out[0, pl.ds(pl.multiple_of((member[0] ^ at) * rows, rows), rows), :] = query_in[at]
    back_blocks(steps, member, proj, key_mark, query_mark, band, grads, exact, log_rows, store,
                (key_sum, value_sum), True, refs[19:])
    out[1] = key_sum[...].astype(bf16)
    out[2] = value_sum[...].astype(bf16)
    grad = jnp.zeros((prompt.shape[0], prompt.shape[1]), f32)
    for part in range(3):
        high, low = split(dot(onehot_t[...], out[part])[:, : weight.shape[2]])
        grad = grad + dot_t(high, weight[part]) + dot_t(low, weight[part])
    total_buf[...] = prompt_part[...] + norm_back(prompt[...].astype(f32), gain[...].reshape(1, -1), grad)
    kept, half = part_mine.shape
    core = member[0] & 1
    part_mine[...] = total_buf[:kept, pl.ds(pl.multiple_of(core * half, half), half)]
    part_other[...] = total_buf[:kept, pl.ds(pl.multiple_of((1 - core) * half, half), half)]


def first_kernel(member, grad_proj, weight, _near, _far, *outs):
    rows = outs[0].shape[0]
    used = weight.shape[2]
    for step, out in enumerate(outs):
        place = pl.ds(pl.multiple_of((member[0] ^ step) * rows, rows), rows)
        total = dot_t(grad_proj[0, place, :used], weight[0])
        for part in (1, 2):
            total = total + dot_t(grad_proj[part, place, :used], weight[part])
        out[...] = total.astype(out.dtype)


def finish_kernel(member, text, prompt, onehot, gain, grad_middle, own, received, middle, own_result, far_result, out, result):
    _, inside, layer_in = own_input(member, 0, text, prompt, onehot)
    grad_first = own[...].astype(f32) + received[...].astype(f32)
    start = grad_middle[...] + norm_back(layer_in, gain[...].reshape(1, -1), grad_first)
    out[...] = jnp.where(inside, 0.0, start)
    result[...] = (middle[...] + own_result[...] + far_result[...].astype(f32)).astype(bf16)


def newton_step(current):
    low = current.astype(bf16)
    inner = -0.625 * current + 0.0625 * dot(low, low)
    inner_low = inner.astype(bf16)
    outer = 3.125 * inner + dot(inner_low, inner_low)
    return 2.44140625 * current + dot(outer.astype(bf16), low)


def put_columns(target, first, block, values):
    low = values.astype(bf16)
    begin = block * TILE
    lanes = slice(begin, begin + TILE)
    target[first : first + begin + TILE, lanes] = low
    if block:
        target[first + begin : first + begin + TILE, :begin] = jnp.transpose(low[:begin])


def update_kernel(
    place, mine, other, prompt, left, near_a, far_a, near_b, far_b, band_state,
    grad_out, left_out, band_out, prompt_out, grad, left_pad, right, matrix, inner_buf, outer_buf,
):
    kept, half = mine.shape
    count, width = prompt_out.shape
    band = band_state.shape[0]
    size = grad.shape[0]
    core = place[0]
    half_rows = width // 2
    grad[...] = jnp.zeros_like(grad)
    for side, pieces in ((core, (near_a, far_a)), (1 - core, (near_b, far_b))):
        columns = pl.ds(pl.multiple_of(side * half, half), half)
        for at in range(width // band):
            source = pieces[at * band // half_rows]
            begin = at * band % half_rows
            target = at * band
            if band % 16 == 0:
                target = pl.multiple_of((place[1] ^ at) * band, 16)
            elif at * band % half_rows:
                continue
            count_rows = band if band % 16 == 0 else half_rows
            right[pl.ds(target, count_rows), columns] = source[begin : begin + count_rows, :]
    grad[:kept, pl.ds(pl.multiple_of(core * half, half), half)] = mine[...]
    grad[:kept, pl.ds(pl.multiple_of((1 - core) * half, half), half)] = other[...]
    value = grad[...]
    grad_out[...] = value[:count]
    high, low = split(value)
    high_t, low_t = jnp.transpose(high), jnp.transpose(low)
    left_gram = dot(high, high_t) + dot(high, low_t) + dot(low, high_t)
    left_new = 0.5 * left[...] + 0.5 * left_gram[:count, :count]
    left_out[...] = left_new

    tops = [begin + TILE for begin in range(0, width, TILE)]
    columns = []
    total = 0.0
    for top in tops:
        lanes = slice(top - TILE, top)
        values = 0.5 * right[:top, lanes].astype(f32) + 0.5 * dot(high_t[:top], high[:, lanes])
        squares = values * values
        if top > TILE:
            total = total + 2.0 * jnp.sum(squares[: top - TILE])
        total = total + jnp.sum(squares[top - TILE :])
        columns.append(values)
    right_scale = 1.25 * lax.rsqrt(total)
    pick = (
        lax.broadcasted_iota(jnp.int32, (band, width), 1)
        == lax.broadcasted_iota(jnp.int32, (band, width), 0) + place[1] * band
    )
    pick = jnp.where(pick, 1.0, 0.0).astype(bf16)
    pick_high, pick_low = dot_t(pick, high).astype(bf16), dot_t(pick, low).astype(bf16)
    band_out[...] = 0.5 * band_state[...] + 0.5 * (
        dot(pick_high, high) + dot(pick_high, low) + dot(pick_low, high)
    )

    left_pad[...] = jnp.zeros_like(left_pad)
    left_pad[:count, :count] = left_new
    left_mat = left_pad[...]
    left_scale = 1.25 * lax.rsqrt(jnp.sum(left_mat * left_mat))
    left_mat = left_mat * left_scale
    root = jnp.where(
        lax.broadcasted_iota(jnp.int32, (size, size), 0)
        == lax.broadcasted_iota(jnp.int32, (size, size), 1),
        1.0,
        0.0,
    )
    thin = value
    columns = [values * right_scale for values in columns]
    for block, values in enumerate(columns):
        put_columns(matrix, size, block, values)
    for repeat in range(ROOT_STEPS - 2):
        matrix[:size, :] = thin.astype(bf16)
        inner, thin_parts = [], []
        for block, top in enumerate(tops):
            lanes = slice(top - TILE, top)
            product = dot(matrix[: size + top, :], matrix[size:, lanes])
            thin_parts.append(product[:size])
            inner.append(-0.625 * columns[block] + 0.0625 * product[size:])
            put_columns(inner_buf, 0, block, inner[block])
        thin = 1.25 * thin - 0.25 * jnp.concatenate(thin_parts, axis=1)
        root = 1.25 * root - 0.25 * dot(root.astype(bf16), left_mat.astype(bf16))
        left_mat = newton_step(left_mat)
        for block, top in enumerate(tops):
            lanes = slice(top - TILE, top)
            outer = 3.125 * inner[block] + dot(inner_buf[:top, :], inner_buf[:, lanes])
            put_columns(outer_buf, 0, block, outer)
        for block, top in enumerate(tops):
            lanes = slice(top - TILE, top)
            columns[block] = 2.44140625 * columns[block] + dot(
                outer_buf[:top, :], matrix[size:, lanes]
            )
        for block, values in enumerate(columns):
            put_columns(matrix, size, block, values)

    def thin_dot(values):
        return dot(values.astype(bf16), matrix[size:, :])

    root = 1.25 * root - 0.25 * dot(root.astype(bf16), left_mat.astype(bf16))
    left_mat = newton_step(left_mat)
    thin = 1.25 * thin - 0.25 * thin_dot(thin)
    power = thin
    for repeat in range(4):
        power = 1.25 * power - 0.25 * thin_dot(power)
    thin = 1.25 * thin - 0.25 * thin_dot(power)
    root = 1.25 * root - 0.25 * dot(root.astype(bf16), left_mat.astype(bf16))
    direction = dot(root.astype(bf16), thin.astype(bf16))
    scale = jnp.sqrt(jnp.sqrt(left_scale)) * jnp.sqrt(jnp.sqrt(right_scale))
    direction = (direction * scale)[:count]
    prompt_value = prompt[...].astype(f32)[:count]
    cells = 1.0 / (count * width)
    ratio = jnp.sqrt(jnp.sum(prompt_value * prompt_value) * cells + norm_epsilon) * lax.rsqrt(
        jnp.sum(direction * direction) * cells + norm_epsilon
    )
    prompt_out[...] = prompt_value - step_rate * ratio * direction


def local(
    text_rows, segment_ids, vocab_ids, embed_table, gain_one, gain_two, qkv_weight, out_weight,
    ffn_in_weight, ffn_out_weight, rel_table, cotangent, left_state, right_state,
    *, dp_size, mp_size,
):
    member = lax.axis_index("mp")
    dp_index = lax.axis_index("dp")
    core = member % 2
    rows, width = text_rows.shape
    length = segment_ids.shape[1]
    prompt_rows = vocab_ids.shape[0]
    table_rows = embed_table.shape[0]
    heads = rel_table.shape[1]
    head_lanes = heads * HEAD
    lanes = -(-(head_lanes + SEGMENTS + length // 128) // 128) * 128
    slots = 128
    kept = -(-prompt_rows // 8) * 8
    me = jnp.reshape(member, (1,))
    dp_bits = [1 << bit for bit in range(dp_size.bit_length() - 1)]
    shape = jax.ShapeDtypeStruct

    def to_core(array, name):
        return swap(array, "mp", mp_size, 1, name)

    def to_y(array, name):
        return swap(array, "mp", mp_size, 2, name)

    def to_across(array, name):
        return swap(array, "mp", mp_size, 3, name)

    place = jnp.stack([core, dp_index]).astype(jnp.int32)

    text_y, cot_y = to_y(text_rows, "text_y"), to_y(cotangent, "cotangent_y")
    up_c = to_core(ffn_in_weight, "up_core")
    down_c = to_core(ffn_out_weight, "down_core")
    right_near = lax.dynamic_slice_in_dim(right_state, core * (width // 2), width // 2, 1)
    right_near = right_near.astype(bf16)
    right_far = swap(right_near, "dp", dp_size, dp_bits[0], "right_x")
    text_c = to_core(text_rows, "text_core")

    share = slots // 2
    padded = jnp.pad(vocab_ids, (0, slots - prompt_rows), constant_values=-1)
    ids = lax.dynamic_slice_in_dim(padded, core * share, share)
    local_ids = jnp.where(ids >= 0, ids - dp_index * table_rows, -1)
    owned = (local_ids >= 0) & (local_ids < table_rows)
    found = jnp.take(embed_table, jnp.clip(local_ids, 0, table_rows - 1), axis=0)
    found = jnp.where(owned[:, None], found, jnp.zeros_like(found))

    table = jnp.concatenate(
        [rel_table.astype(f32), jnp.full((rel_table.shape[0], 1), prompt_rows, f32)], axis=1
    )
    weight = jnp.transpose(qkv_weight, (1, 0, 2))
    found = pl.pallas_call(
        stage_kernel,
        out_shape=shape(found.shape, bf16),
        in_specs=[VMEM] * 2 + [ANY] * 2,
        out_specs=VMEM,
        compiler_params=params(4),
        cost_estimate=cost(0.5),
        name="stage",
    )(found, swap(found, "dp", dp_size, dp_bits[0], "prompt_x"), text_y, weight)
    found = found + swap(found, "dp", dp_size, dp_bits[1], "prompt_z")
    for bit in dp_bits[2:-1]:
        found = found + swap(found, "dp", dp_size, bit, "prompt_far")
    found, text_y = pl.pallas_call(
        relay_kernel,
        out_shape=[
            shape(found.shape, bf16),
            shape((rows, width), bf16),
        ],
        in_specs=[SMEM] + [VMEM] * 4 + [ANY] * 3,
        out_specs=[VMEM] * 2,
        compiler_params=params(8),
        cost_estimate=cost(0.5),
        name="relay",
    )(
        table, found, swap(found, "dp", dp_size, dp_bits[-1], "prompt_far"), text_y,
        right_far, cot_y, up_c, down_c,
    )
    text_d = to_core(text_y, "text_across")
    out_y = to_y(out_weight, "out_y")

    proj_shape = shape((3, length, lanes), bf16)
    onehot, onehot_t, key_mark, query_mark, band, text_proj = pl.pallas_call(
        prep_kernel,
        out_shape=[
            shape((length, slots), bf16),
            shape((slots, length), bf16),
            shape((length, 128), bf16),
            shape((heads, length, 128), bf16),
            shape((heads, 512, 256), f32),
            proj_shape,
        ],
        in_specs=[SMEM, SMEM] + [VMEM] * 7,
        out_specs=[VMEM] * 6,
        compiler_params=params(16),
        cost_estimate=cost(3.5),
        name="project",
    )(me, table, segment_ids, text_rows, text_c, text_y, text_d, gain_one, weight)

    beside = to_core(found, "prompt_core")

    context_shapes = [shape((2, head_lanes, rows), bf16), shape((2, head_lanes, rows), f32), shape((2, heads, rows), f32)]
    score_buffer = pltpu.VMEM((heads, length + rows, rows), f32)
    forward_scratch = [pltpu.VMEM((length, lanes), bf16), score_buffer]
    joined = shape((2 * right_state.shape[0], width // 2), bf16)
    prompt, proj, right_near, ctx_near, exact_near, log_near = pl.pallas_call(
        functools.partial(forward_first, (3, 1)),
        out_shape=[shape((slots, width), bf16), proj_shape, joined] + context_shapes,
        in_specs=[SMEM] + [VMEM] * 11,
        out_specs=[VMEM] * 6,
        scratch_shapes=forward_scratch,
        compiler_params=params(24),
        cost_estimate=cost(4.5),
        name="attend",
    )(
        me, found, beside, gain_one, weight, onehot, text_proj, key_mark, query_mark, band,
        right_near, right_far,
    )
    got_d = to_across(ctx_near, "context_across")
    got_c = to_core(ctx_near, "context_core")
    out_pair, ctx_far, exact_far, log_far = pl.pallas_call(
        functools.partial(forward_second, (2, 0)),
        out_shape=[shape((2 * head_lanes, width), bf16)] + context_shapes,
        in_specs=[SMEM] + [VMEM] * 6,
        out_specs=[VMEM] * 4,
        scratch_shapes=forward_scratch,
        compiler_params=params(24),
        cost_estimate=cost(4.5),
        name="attend",
    )(me, proj, key_mark, query_mark, band, out_weight, out_y)
    out_pair = to_core(out_pair, "out_core")
    got_y = to_y(ctx_far, "context_y")
    right_far = swap(right_near, "dp", dp_size, dp_bits[1], "right_z")

    units = ffn_in_weight.shape[1]
    wide = (rows, width)

    def far_body(*refs):
        join(refs[11], refs[12], refs[16])
        ffn_kernel(2, *refs[:11], refs[13], None, *refs[14:16])

    def ffn(step, start, cot, out_shape, *extra):
        body = functools.partial(ffn_kernel, step)
        if step:
            body = far_body
        return pl.pallas_call(
            body,
            out_shape=out_shape,
            in_specs=[VMEM] * (11 + len(extra)),
            out_specs=[VMEM] * len(out_shape),
            compiler_params=params(24),
            cost_estimate=cost(4.5),
            name="ffn",
        )(
            start, gain_two, cot, ctx_far, got_y, out_weight, out_y,
            ffn_in_weight, up_c, ffn_out_weight, down_c, *extra,
        )

    start, start_y, cot_y = pl.pallas_call(
        middle_kernel,
        out_shape=[shape(wide, f32)] * 2 + [shape(wide, bf16)],
        in_specs=[SMEM] + [VMEM] * 8,
        out_specs=[VMEM] * 3,
        compiler_params=params(16),
        cost_estimate=cost(2),
        name="middle",
    )(me, text_rows, text_y, prompt, onehot, got_c, got_d, out_pair, cot_y)
    half_rows = shape((rows // 2, width), bf16)
    joined = shape((4 * right_state.shape[0], width // 2), bf16)
    far_result, *far_grad, right_near = ffn(
        2, start_y, cot_y, [shape(wide, bf16), half_rows, half_rows, joined], right_near, right_far
    )
    right_far = swap(right_near, "dp", dp_size, dp_bits[2], "right_far")
    got_grad = [to_y(piece, "grad_second_y") for piece in far_grad]
    own_result, middle, own_grad = ffn(0, start, cotangent, [shape(wide, f32)] * 3)

    send_shape = shape((head_lanes, rows), bf16)
    grad_middle, prompt_part, send_0, send_1, send_2, send_3 = pl.pallas_call(
        post_kernel,
        out_shape=[shape(wide, f32), shape((slots, width), f32)] + [send_shape] * 4,
        in_specs=[SMEM] + [VMEM] * 10,
        out_specs=[VMEM] * 6,
        compiler_params=params(16),
        cost_estimate=cost(2.2),
        name="post",
    )(me, middle, gain_two, cotangent, onehot, own_grad, *got_grad, out_weight, out_y, out_pair)
    back_2, back_3 = to_y(send_2, "grad_context_y"), to_across(send_3, "grad_context_across")
    back_1 = to_core(send_1, "grad_context_core")
    got_result = to_y(far_result, "result_y")

    back_scratch = [
        pltpu.VMEM((length, lanes), bf16),
        pltpu.VMEM((length, heads * rows), bf16),
        pltpu.VMEM((length, heads * rows), bf16),
        pltpu.VMEM((heads * rows, lanes), bf16),
        pltpu.VMEM((heads * rows, lanes), bf16),
        score_buffer,
    ]
    sum_shape = shape((length, lanes), f32)
    exact_a, log_a = jnp.stack([exact_far[1], exact_near[1]]), jnp.stack([log_far[1], log_near[1]])
    exact_b, log_b = jnp.stack([exact_far[0], exact_near[0]]), jnp.stack([log_far[0], log_near[0]])
    query_a, key_a, value_a = pl.pallas_call(
        functools.partial(back_first, (0, 1)),
        out_shape=[shape((2, rows, lanes), bf16), sum_shape, sum_shape],
        in_specs=[SMEM] + [VMEM] * 8,
        out_specs=[VMEM] * 3,
        scratch_shapes=back_scratch,
        compiler_params=params(32),
        cost_estimate=cost(6.5),
        name="attend_back",
    )(me, proj, key_mark, query_mark, band, send_0, back_1, exact_a, log_a)
    grad_proj, part, part_other = pl.pallas_call(
        functools.partial(back_second, (2, 3)),
        out_shape=[proj_shape] + [shape((kept, width // 2), f32)] * 2,
        in_specs=[SMEM] + [VMEM] * 17,
        out_specs=[VMEM] * 3,
        scratch_shapes=[pltpu.VMEM((length, lanes), f32)] * 2 + [pltpu.VMEM((slots, width), f32)] + back_scratch,
        compiler_params=params(36),
        cost_estimate=cost(6.5),
        name="attend_back",
    )(
        me, proj, key_mark, query_mark, band, back_2, back_3, exact_b, log_b, query_a, key_a, value_a,
        onehot_t, prompt, gain_one, weight, prompt_part, right_far,
    )

    for bit in dp_bits[3:]:
        right_near = jnp.concatenate([right_near, right_far])
        right_far = swap(right_near, "dp", dp_size, bit, "right_far")
    if right_state.shape[0] % 16:
        blocks = jnp.concatenate([right_near, right_far]).reshape(dp_size, -1, width // 2)
        blocks = jnp.take(blocks, jnp.arange(dp_size) ^ dp_index, axis=0).reshape(width, width // 2)
        right_near, right_far = blocks[: width // 2], blocks[width // 2 :]
    right_beside = [to_core(right_near, "right_core"), to_core(right_far, "right_core")]

    part = part + to_core(part_other, "prompt_grad_core")

    def add_pair(values, axis, size, bit):
        sent = values.astype(bf16)
        return sent.astype(f32) + swap(sent, axis, size, bit, "prompt_grad_sum").astype(f32)

    sent = part.astype(bf16)
    beyond = lax.ppermute(
        sent, ("dp", "mp"),
        [(i, i ^ (mp_size + 2)) for i in range(dp_size * mp_size)],
    ).astype(f32)
    over_y = swap(sent, "mp", mp_size, 2, "prompt_grad_y").astype(f32)
    over_x = swap(sent, "dp", dp_size, dp_bits[0], "prompt_grad_x").astype(f32)
    part = (sent.astype(f32) + over_y) + (over_x + beyond)
    for bit in dp_bits[1:]:
        part = add_pair(part, "dp", dp_size, bit)
    part_beside = to_core(part, "prompt_grad_other")

    first = pl.pallas_call(
        first_kernel,
        out_shape=[shape(wide, bf16)] * 4,
        in_specs=[SMEM] + [VMEM] * 2 + [ANY] * 2,
        out_specs=[VMEM] * 4,
        compiler_params=params(16),
        cost_estimate=cost(1.5),
        name="grad_first",
    )(me, grad_proj, weight, *right_beside)
    near = first[0] + to_core(first[1], "grad_first_core")
    far = first[2] + to_core(first[3], "grad_first_across")
    received = to_y(far, "grad_first_y")
    input_grad, result = pl.pallas_call(
        finish_kernel,
        out_shape=[shape(wide, f32), shape(wide, bf16)],
        in_specs=[SMEM] + [VMEM] * 10,
        out_specs=[VMEM] * 2,
        compiler_params=params(16),
        cost_estimate=cost(1.5),
        name="finish",
    )(me, text_rows, prompt, onehot, gain_one, grad_middle, near, received, middle, own_result, got_result)

    band_rows = right_state.shape[0]
    prompt_grad, left_new, right_new, new_prompt = pl.pallas_call(
        update_kernel,
        out_shape=[
            shape((prompt_rows, width), f32),
            shape((prompt_rows, prompt_rows), f32),
            shape((band_rows, width), f32),
            shape((prompt_rows, width), f32),
        ],
        in_specs=[SMEM] + [VMEM] * 9,
        out_specs=[VMEM] * 4,
        scratch_shapes=[
            pltpu.VMEM((slots, width), f32),
            pltpu.VMEM((slots, slots), f32),
            pltpu.VMEM((width, width), bf16),
            pltpu.VMEM((slots + width, width), bf16),
            pltpu.VMEM((width, width), bf16),
            pltpu.VMEM((width, width), bf16),
        ],
        compiler_params=params(40),
        cost_estimate=cost(16),
        name="update",
    )(
        place, part, part_beside, prompt, left_state, right_near, right_far, *right_beside,
        right_state,
    )
    return result, input_grad, prompt_grad, left_new, right_new, new_prompt


def solution(mesh):
    sizes = dict(mesh.shape)
    return jax.shard_map(
        functools.partial(local, dp_size=sizes["dp"], mp_size=sizes["mp"]),
        mesh=mesh,
        in_specs=(
            P(("dp", "mp"), None),
            P("dp", None),
            P(),
            P("dp", None),
            P(),
            P(),
            P(None, None, "mp"),
            P("mp", None),
            P(None, "mp"),
            P("mp", None),
            P(None, "mp"),
            P(("dp", "mp"), None),
            P(),
            P("dp", None),
        ),
        out_specs=(P(("dp", "mp"), None), P(("dp", "mp"), None), P(), P(), P("dp", None), P()),
        check_vma=False,
    )
```

```python
import functools

import jax
import jax.numpy as jnp
from jax import lax
from jax.experimental import pallas as pl
from jax.experimental.pallas import tpu as pltpu
from jax.sharding import PartitionSpec as P

ROOT_STEPS = 5
HEAD = 64
SEGMENTS = 8
PENALTY = -1000000000.0

norm_epsilon = 1e-06
step_rate = 0.5
bucket_edges = (12, 16, 23, 32, 46, 64, 91)
bf16 = jnp.bfloat16
f32 = jnp.float32
MIB = 1024 * 1024
TILE = 256

VMEM = pl.BlockSpec(memory_space=pltpu.VMEM)
ANY = pl.BlockSpec(memory_space=pl.ANY)
SMEM = pl.BlockSpec(memory_space=pltpu.SMEM)


def dot(left, right):
    return lax.dot_general(left, right, (((1,), (0,)), ((), ())), preferred_element_type=f32)


def dot_t(left, right):
    return lax.dot_general(left, right, (((1,), (1,)), ((), ())), preferred_element_type=f32)


def dot_rows(left, right):
    return lax.dot_general(left, right, (((0,), (0,)), ((), ())), preferred_element_type=f32)


def split(values):
    high = values.astype(bf16)
    return high, (values - high.astype(f32)).astype(bf16)


def swap(array, axis, count, bit, name):
    with jax.named_scope(name):
        return lax.ppermute(array, axis, [(i, i ^ bit) for i in range(count)])


def rms_scale(values):
    return lax.rsqrt(jnp.mean(values * values, axis=-1, keepdims=True) + norm_epsilon)


def norm_back(values, gain, grad):
    scale = rms_scale(values)
    inner = gain * grad
    mean = jnp.mean(values * inner, axis=-1, keepdims=True)
    return scale * inner - values * (scale * scale * scale * mean)


def params(limit=56):
    return pltpu.CompilerParams(vmem_limit_bytes=limit * MIB)


def cost(time):
    return pl.CostEstimate(flops=int(time), bytes_accessed=int(time * 3.5e6), transcendentals=0)


def stage_kernel(found, received, _text, out):
    out[...] = found[...] + received[...]


def relay_kernel(
    table, found, received, text, right, _cotangent, _up, _down, out, text_out
):
    out[...] = found[...] + received[...]
    text_out[...] = text[...]


def prep_kernel(
    member, table, segments, x0, x1, x2, x3, gain, weight,
    onehot, onehot_t, key_mark, query_mark, band, out,
):
    length = segments.shape[1]
    slots = onehot_t.shape[0]
    heads, tall, wide = band.shape
    tile = tall // 4
    segment = segments[...]
    first = jnp.zeros_like(segment)
    for number in range(1, SEGMENTS):
        before = jnp.sum(jnp.where(segment < number, 1.0, 0.0), axis=-1, keepdims=True)
        first = jnp.where(segment == number, before.astype(jnp.int32), first)
    offset = lax.broadcasted_iota(jnp.int32, segment.shape, 1) - first
    slot = jnp.where(offset < table[0, heads].astype(jnp.int32), offset, -1)
    placed = lax.broadcasted_iota(jnp.int32, (slots, length), 0) == slot
    placed = jnp.where(placed, 1.0, 0.0)
    onehot_t[...] = placed.astype(bf16)
    onehot[...] = jnp.transpose(placed).astype(bf16)
    lanes = key_mark.shape[1]
    spare = heads * HEAD % lanes
    segment_t = jnp.transpose(jnp.broadcast_to(segment.astype(f32), (lanes, length)))
    lane = lax.broadcasted_iota(jnp.int32, (length, lanes), 1) - spare
    tile_at = lax.broadcasted_iota(jnp.int32, (length, lanes), 0) // tile
    in_segment = (lane >= 0) & (lane < SEGMENTS)
    in_tile = (lane >= SEGMENTS) & (lane < SEGMENTS + length // tile)
    same = segment_t == lane.astype(f32)
    other_tile = lane - SEGMENTS
    key_mark[...] = jnp.where(
        (in_segment & ~same) | (in_tile & (tile_at == other_tile)), 1.0, 0.0
    ).astype(bf16)
    for head in range(heads):
        values = jnp.where(in_segment & same, PENALTY, 0.0)
        values = jnp.where(in_tile & (other_tile < tile_at - 1), table[15, head], values)
        values = jnp.where(in_tile & (other_tile > tile_at + 1), table[31, head], values)
        query_mark[head] = values.astype(bf16)
    rows = lax.broadcasted_iota(jnp.int32, (tile, tile), 0)
    columns = lax.broadcasted_iota(jnp.int32, (tile, tile), 1)
    zero = jnp.zeros((tile, tile), f32)
    for head in range(heads):
        band[head, :tile, tile:] = zero
        band[head, 3 * tile :, :tile] = zero
    for shift in (-1, 0, 1):
        relative = rows - columns + shift * tile
        distance = jnp.abs(relative)
        bucket = jnp.full((tile, tile), 8, jnp.int32)
        for edge in bucket_edges:
            bucket = bucket + jnp.where(distance >= edge, 1, 0)
        bucket = jnp.where(distance < 8, distance, bucket) + jnp.where(relative > 0, 16, 0)
        numbers = {-1: range(1, 16), 0: (*range(0, 16), *range(17, 32)), 1: range(17, 32)}[shift]
        values = [zero] * heads
        for number in numbers:
            here = bucket == number
            values = [jnp.where(here, table[number, head], values[head]) for head in range(heads)]
        for head in range(heads):
            for half in range(2):
                at = (shift + 1 + half) * tile
                band[head, at : at + tile, half * tile : half * tile + tile] = values[head]

    me = member[0]
    rows = x0.shape[0]
    used = weight.shape[1]
    out[:, :, used:] = jnp.zeros((3, out.shape[1], out.shape[2] - used), bf16)
    for step, ref in enumerate((x0, x1, x2, x3)):
        place = pl.ds(pl.multiple_of((me ^ step) * rows, rows), rows)
        values = ref[...].astype(f32)
        inside = jnp.max(onehot[place, :].astype(f32), axis=-1, keepdims=True) > 0.0
        scale = jnp.where(inside, 0.0, rms_scale(values))
        normed = (values * scale * gain[...].reshape(1, -1)).astype(bf16)
        for part in range(3):
            out[part, place, :used] = dot_t(normed, weight[part]).astype(bf16)


def lane_head(rows, lanes):
    return lax.broadcasted_iota(jnp.int32, (rows, lanes), 1) // HEAD


def marked_keys(keys, key, key_mark):
    lanes = key_mark.shape[1]
    keys[:, :lanes] = key[:, :lanes]
    keys[:, lanes:] = key[:, lanes:] + key_mark[...]


def block_scores(scores, keys, queries, marks, which, head, band, block):
    rows = queries.shape[0]
    length = keys.shape[0]
    mine = jnp.where(which == head, queries, marks)
    margin = rows // 2
    scores[margin : margin + length, :] = dot_t(keys[...], mine)
    near = pl.ds(pl.multiple_of(block * rows, rows), 2 * rows)
    scores[near, :] += band[head]
    return scores[margin : margin + length, :]


def padded_marks(query_mark, head, place, lanes):
    marks = query_mark[head, place, :]
    return jnp.concatenate([jnp.zeros((marks.shape[0], lanes - marks.shape[1]), bf16), marks], axis=1)


def attend_blocks(steps, member, proj, key_mark, query_mark, band, refs):
    contexts, exact, log_rows, keys, scores_buf = refs
    rows = contexts.shape[2]
    used = contexts.shape[1]
    heads = used // HEAD
    lanes = proj.shape[2]
    marked_keys(keys, proj[1], key_mark)
    which = lane_head(rows, lanes)
    for at, step in enumerate(steps):
        block = member[0] ^ step
        place = pl.ds(pl.multiple_of(block * rows, rows), rows)
        queries = proj[0, place, :]
        mixed = jnp.zeros((rows, lanes), f32)
        sums = []
        for head in range(heads):
            marks = padded_marks(query_mark, head, place, lanes)
            scores = block_scores(
                scores_buf.at[head], keys, queries, marks, which, head, band, block
            )
            row_max = jnp.max(scores, axis=0, keepdims=True)
            exponent = jnp.exp(scores - row_max)
            row_sum = jnp.sum(exponent, axis=0, keepdims=True)
            mixed = jnp.where(which == head, dot_rows(exponent.astype(bf16), proj[2]), mixed)
            log_rows[at, head : head + 1, :] = row_max + jnp.log(row_sum)
            sums.append(jnp.broadcast_to(1.0 / row_sum, (HEAD, rows)))
        context = jnp.transpose(mixed)[:used] * jnp.concatenate(sums, axis=0)
        contexts[at] = context.astype(bf16)
        exact[at] = context


def join(near, far, out):
    count = near.shape[0]
    out[:count] = near[...]
    out[count:] = far[...]


def forward_first(
    steps, member, found, beside, gain, weight, onehot, text, key_mark, query_mark, band,
    near, far, prompt, proj, joined, *refs
):
    join(near, far, joined)
    share = found.shape[0]
    core = member[0] & 1
    prompt[pl.ds(pl.multiple_of(core * share, share), share), :] = found[...]
    prompt[pl.ds(pl.multiple_of((1 - core) * share, share), share), :] = beside[...]
    values = prompt[...].astype(f32)
    normed = (values * rms_scale(values) * gain[...].reshape(1, -1)).astype(bf16)
    used = weight.shape[1]
    for part in range(3):
        projected = dot_t(normed, weight[part]).astype(bf16)
        proj[part, :, :used] = text[part, :, :used] + dot(onehot[...], projected).astype(bf16)
    proj[:, :, used:] = text[:, :, used:]
    attend_blocks(steps, member, proj, key_mark, query_mark, band, refs)


def forward_second(steps, member, proj, key_mark, query_mark, band, near, far, joined, *refs):
    join(near, far, joined)
    attend_blocks(steps, member, proj, key_mark, query_mark, band, refs)


def own_input(member, step, text, prompt, onehot):
    rows = text.shape[0]
    mine = onehot[pl.ds(pl.multiple_of((member[0] ^ step) * rows, rows), rows), :]
    inside = jnp.max(mine.astype(f32), axis=-1, keepdims=True) > 0.0
    return mine, inside, jnp.where(inside, dot(mine, prompt[...]), text[...].astype(f32))


def middle_kernel(
    member, text, text_y, prompt, onehot, left, across, weights, cotangent, out, out_y, cot_out
):
    cot_out[...] = cotangent[...]
    for step, rows, result in ((0, text, out), (2, text_y, out_y)):
        at = step // 2
        layer_in = own_input(member, step, rows, prompt, onehot)[2]
        part = left.shape[1]
        added = dot(jnp.transpose(left[1 - at]), weights[:part])
        added = added + dot(jnp.transpose(across[at]), weights[part:])
        result[...] = layer_in + added


def ffn_kernel(step, start, gain, cotangent, near, far, *refs):
    outs_w, ups, downs = refs[:2], refs[2:4], refs[4:6]
    result, middle_out, grad_outs = refs[6], refs[7], refs[8:]
    at = step // 2
    added = dot(jnp.transpose(near[1 - at]), outs_w[0][...])
    added = added + dot(jnp.transpose(far[at]), outs_w[1][...])
    middle = start[...] + added
    if middle_out is not None:
        middle_out[...] = middle
    second = (middle * rms_scale(middle) * gain[...].reshape(1, -1)).astype(bf16)
    cot = cotangent[...]
    total = jnp.zeros_like(middle)
    grad = jnp.zeros_like(middle)
    root = 0.7978845608028654
    for up, down in zip(ups, downs):
        hidden = dot(second, up[...])
        square = hidden * hidden
        tanh = jnp.tanh(root * hidden * (1.0 + 0.044715 * square))
        half = 0.5 + 0.5 * tanh
        active = (hidden * half).astype(bf16)
        slope = half + (0.5 * root) * hidden * (1.0 - tanh * tanh) * (1.0 + 0.134145 * square)
        grad_hidden = (dot_t(cot, down[...]) * slope).astype(bf16)
        grad = grad + dot_t(grad_hidden, up[...])
        total = total + dot(active, down[...])
    half = grad.shape[0] // len(grad_outs)
    for index, out in enumerate(grad_outs):
        out[...] = grad[index * half : index * half + half].astype(out.dtype)
    result[...] = total.astype(result.dtype)


def post_kernel(member, middle, gain, cotangent, onehot, own, received, received_b, *refs):
    weight, weight_y, pair, grad_middle_out, prompt_part = refs[:5]
    sends = refs[5:]
    part = weight.shape[0]
    outs_w = (weight, pair.at[:part], weight_y, pair.at[part:])
    rows, half = own.shape[0], received.shape[0]
    received = jnp.concatenate([received[...], received_b[...]]).astype(f32)
    grad_second = own[...] + received
    grad_middle = cotangent[...].astype(f32) + norm_back(middle[...], gain[...].reshape(1, -1), grad_second)
    grad_middle_out[...] = grad_middle
    send = grad_middle.astype(bf16)
    for out, weight in zip(sends, outs_w):
        out[...] = dot_t(weight[...], send).astype(bf16)
    mine_t = jnp.transpose(onehot[pl.ds(pl.multiple_of(member[0] * rows, rows), rows), :])
    high, low = split(grad_middle)
    prompt_part[...] = dot(mine_t, high) + dot(mine_t, low)


def back_blocks(steps, member, proj, key_mark, query_mark, band, grads, exact, log_rows, grad_query, sums, started, buffers):
    keys, prob_buf, grad_buf, query_all, out_all, scores_buf = buffers
    key_sum, value_sum = sums
    rows = grads[0].shape[1]
    heads = grads[0].shape[0] // HEAD
    lanes = proj.shape[2]
    marked_keys(keys, proj[1], key_mark)
    which = lane_head(rows, lanes)
    for at, step in enumerate(steps):
        block = member[0] ^ step
        place = pl.ds(pl.multiple_of(block * rows, rows), rows)
        queries = proj[0, place, :]
        grad_t = jnp.concatenate(
            [grads[at][...], jnp.zeros((lanes - heads * HEAD, rows), bf16)], axis=0
        )
        grad_out = jnp.transpose(grad_t)
        mixed = jnp.zeros((rows, lanes), f32)
        for head in range(heads):
            near = which == head
            own_grad = jnp.where(near, grad_out, jnp.zeros_like(grad_out))
            part = slice(head * HEAD, head * HEAD + HEAD)
            stack = slice(head * rows, head * rows + rows)
            query_all[stack, :] = jnp.where(near, queries, jnp.zeros_like(queries))
            out_all[stack, :] = own_grad
            marks = padded_marks(query_mark, head, place, lanes)
            scores = block_scores(
                scores_buf.at[head], keys, queries, marks, which, head, band, block
            )
            probs = jnp.exp(scores - log_rows[at, head : head + 1, :])
            prob_buf[:, stack] = probs.astype(bf16)
            grad_probs = dot_t(proj[2], own_grad)
            inner = jnp.sum(grads[at][part, :].astype(f32) * exact[at, part, :], axis=0, keepdims=True)
            grad_scores = (probs * (grad_probs - inner)).astype(bf16)
            grad_buf[:, stack] = grad_scores
            mixed = jnp.where(near, dot_rows(grad_scores, proj[1]), mixed)
        grad_query(step, place, mixed.astype(bf16))
        more_keys = dot(grad_buf[...], query_all[...])
        more_values = dot(prob_buf[...], out_all[...])
        if at == 0 and not started:
            key_sum[...] = more_keys
            value_sum[...] = more_values
        else:
            key_sum[...] += more_keys
            value_sum[...] += more_values


def back_first(steps, member, proj, key_mark, query_mark, band, *refs):
    grads, exact, log_rows = refs[0:2], refs[2], refs[3]
    query_out, key_sum, value_sum = refs[4:7]

    def store(step, place, values):
        query_out[steps.index(step)] = values

    back_blocks(steps, member, proj, key_mark, query_mark, band, grads, exact, log_rows, store,
                (key_sum, value_sum), False, refs[7:])


def back_second(steps, member, proj, key_mark, query_mark, band, *refs):
    grads, exact, log_rows = refs[0:2], refs[2], refs[3]
    query_in, key_in, value_in = refs[4:7]
    onehot_t, prompt, gain, weight, prompt_part, far, out, part_mine, part_other, far_out = refs[7:17]
    key_sum, value_sum, total_buf = refs[17:20]
    rows = grads[0].shape[1]
    far_out[...] = far[...]
    key_sum[...] = key_in[...]
    value_sum[...] = value_in[...]

    def store(step, place, values):
        out[0, place, :] = values

    for at in range(2):
        out[0, pl.ds(pl.multiple_of((member[0] ^ at) * rows, rows), rows), :] = query_in[at]
    back_blocks(steps, member, proj, key_mark, query_mark, band, grads, exact, log_rows, store,
                (key_sum, value_sum), True, refs[20:])
    out[1] = key_sum[...].astype(bf16)
    out[2] = value_sum[...].astype(bf16)
    grad = jnp.zeros((prompt.shape[0], prompt.shape[1]), f32)
    for part in range(3):
        high, low = split(dot(onehot_t[...], out[part])[:, : weight.shape[1]])
        grad = grad + dot(high, weight[part]) + dot(low, weight[part])
    total_buf[...] = prompt_part[...] + norm_back(prompt[...].astype(f32), gain[...].reshape(1, -1), grad)
    kept, half = part_mine.shape
    core = member[0] & 1
    part_mine[...] = total_buf[:kept, pl.ds(pl.multiple_of(core * half, half), half)]
    part_other[...] = total_buf[:kept, pl.ds(pl.multiple_of((1 - core) * half, half), half)]


def first_kernel(member, grad_proj, weight, *outs):
    rows = outs[0].shape[0]
    used = weight.shape[1]
    for step, out in enumerate(outs):
        place = pl.ds(pl.multiple_of((member[0] ^ step) * rows, rows), rows)
        total = dot(grad_proj[0, place, :used], weight[0])
        for part in (1, 2):
            total = total + dot(grad_proj[part, place, :used], weight[part])
        out[...] = total.astype(out.dtype)


def outgoing_kernel(result, own, other, _near, _far, out):
    rows = result.shape[0]
    out[:rows] = result[...]
    out[rows:] = own[...] + other[...]


def finish_kernel(
    member, text, prompt, onehot, gain, grad_middle, own, received, middle, own_result, out, result
):
    rows = text.shape[0]
    _, inside, layer_in = own_input(member, 0, text, prompt, onehot)
    grad_first = own[...].astype(f32) + received[rows:].astype(f32)
    start = grad_middle[...] + norm_back(layer_in, gain[...].reshape(1, -1), grad_first)
    out[...] = jnp.where(inside, 0.0, start)
    result[...] = (middle[...] + own_result[...] + received[:rows].astype(f32)).astype(bf16)


def newton_step(current):
    low = current.astype(bf16)
    inner = -0.625 * current + 0.0625 * dot(low, low)
    inner_low = inner.astype(bf16)
    outer = 3.125 * inner + dot(inner_low, inner_low)
    return 2.44140625 * current + dot(outer.astype(bf16), low)


def put_columns(target, first, block, values):
    low = values.astype(bf16)
    begin = block * TILE
    lanes = slice(begin, begin + TILE)
    target[first : first + begin + TILE, lanes] = low
    if block:
        target[first + begin : first + begin + TILE, :begin] = jnp.transpose(low[:begin])


def update_kernel(
    place, mine, other, prompt, left, near_a, far_a, near_b, far_b, band_state,
    grad_out, left_out, band_out, prompt_out, grad, left_pad, right, matrix, inner_buf, outer_buf,
):
    kept, half = mine.shape
    count, width = prompt_out.shape
    band = band_state.shape[0]
    size = grad.shape[0]
    core = place[0]
    half_rows = width // 2
    grad[...] = jnp.zeros_like(grad)
    for side, pieces in ((core, (near_a, far_a)), (1 - core, (near_b, far_b))):
        columns = pl.ds(pl.multiple_of(side * half, half), half)
        for at in range(width // band):
            source = pieces[at * band // half_rows]
            begin = at * band % half_rows
            target = at * band
            if band % 16 == 0:
                target = pl.multiple_of((place[1] ^ at) * band, 16)
            elif at * band % half_rows:
                continue
            count_rows = band if band % 16 == 0 else half_rows
            right[pl.ds(target, count_rows), columns] = source[begin : begin + count_rows, :]
    grad[:kept, pl.ds(pl.multiple_of(core * half, half), half)] = mine[...]
    grad[:kept, pl.ds(pl.multiple_of((1 - core) * half, half), half)] = other[...]
    value = grad[...]
    grad_out[...] = value[:count]
    high, low = split(value)
    high_t, low_t = jnp.transpose(high), jnp.transpose(low)
    left_gram = dot(high, high_t) + dot(high, low_t) + dot(low, high_t)
    left_new = 0.5 * left[...] + 0.5 * left_gram[:count, :count]
    left_out[...] = left_new

    tops = [begin + TILE for begin in range(0, width, TILE)]
    columns = []
    total = 0.0
    for top in tops:
        lanes = slice(top - TILE, top)
        values = 0.5 * right[:top, lanes].astype(f32) + 0.5 * dot(high_t[:top], high[:, lanes])
        squares = values * values
        if top > TILE:
            total = total + 2.0 * jnp.sum(squares[: top - TILE])
        total = total + jnp.sum(squares[top - TILE :])
        columns.append(values)
    right_scale = 1.25 * lax.rsqrt(total)
    pick = (
        lax.broadcasted_iota(jnp.int32, (band, width), 1)
        == lax.broadcasted_iota(jnp.int32, (band, width), 0) + place[1] * band
    )
    pick = jnp.where(pick, 1.0, 0.0).astype(bf16)
    pick_high, pick_low = dot_t(pick, high).astype(bf16), dot_t(pick, low).astype(bf16)
    band_out[...] = 0.5 * band_state[...] + 0.5 * (
        dot(pick_high, high) + dot(pick_high, low) + dot(pick_low, high)
    )

    left_pad[...] = jnp.zeros_like(left_pad)
    left_pad[:count, :count] = left_new
    left_mat = left_pad[...]
    left_scale = 1.25 * lax.rsqrt(jnp.sum(left_mat * left_mat))
    left_mat = left_mat * left_scale
    root = jnp.where(
        lax.broadcasted_iota(jnp.int32, (size, size), 0)
        == lax.broadcasted_iota(jnp.int32, (size, size), 1),
        1.0,
        0.0,
    )
    thin = value
    columns = [values * right_scale for values in columns]
    for block, values in enumerate(columns):
        put_columns(matrix, size, block, values)
    for repeat in range(ROOT_STEPS - 2):
        matrix[:size, :] = thin.astype(bf16)
        inner, thin_parts = [], []
        for block, top in enumerate(tops):
            lanes = slice(top - TILE, top)
            product = dot(matrix[: size + top, :], matrix[size:, lanes])
            thin_parts.append(product[:size])
            inner.append(-0.625 * columns[block] + 0.0625 * product[size:])
            put_columns(inner_buf, 0, block, inner[block])
        thin = 1.25 * thin - 0.25 * jnp.concatenate(thin_parts, axis=1)
        root = 1.25 * root - 0.25 * dot(root.astype(bf16), left_mat.astype(bf16))
        left_mat = newton_step(left_mat)
        for block, top in enumerate(tops):
            lanes = slice(top - TILE, top)
            outer = 3.125 * inner[block] + dot(inner_buf[:top, :], inner_buf[:, lanes])
            put_columns(outer_buf, 0, block, outer)
        for block, top in enumerate(tops):
            lanes = slice(top - TILE, top)
            columns[block] = 2.44140625 * columns[block] + dot(
                outer_buf[:top, :], matrix[size:, lanes]
            )
        for block, values in enumerate(columns):
            put_columns(matrix, size, block, values)

    def thin_dot(values):
        return dot(values.astype(bf16), matrix[size:, :])

    root = 1.25 * root - 0.25 * dot(root.astype(bf16), left_mat.astype(bf16))
    left_mat = newton_step(left_mat)
    thin = 1.25 * thin - 0.25 * thin_dot(thin)
    power = thin
    for repeat in range(4):
        power = 1.25 * power - 0.25 * thin_dot(power)
    thin = 1.25 * thin - 0.25 * thin_dot(power)
    root = 1.25 * root - 0.25 * dot(root.astype(bf16), left_mat.astype(bf16))
    direction = dot(root.astype(bf16), thin.astype(bf16))
    scale = jnp.sqrt(jnp.sqrt(left_scale)) * jnp.sqrt(jnp.sqrt(right_scale))
    direction = (direction * scale)[:count]
    prompt_value = prompt[...].astype(f32)[:count]
    cells = 1.0 / (count * width)
    ratio = jnp.sqrt(jnp.sum(prompt_value * prompt_value) * cells + norm_epsilon) * lax.rsqrt(
        jnp.sum(direction * direction) * cells + norm_epsilon
    )
    prompt_out[...] = prompt_value - step_rate * ratio * direction


def local(
    text_rows, segment_ids, vocab_ids, embed_table, gain_one, gain_two, qkv_weight, out_weight,
    ffn_in_weight, ffn_out_weight, rel_table, cotangent, left_state, right_state,
    *, dp_size, mp_size,
):
    member = lax.axis_index("mp")
    dp_index = lax.axis_index("dp")
    core = member % 2
    rows, width = text_rows.shape
    length = segment_ids.shape[1]
    prompt_rows = vocab_ids.shape[0]
    table_rows = embed_table.shape[0]
    heads = rel_table.shape[1]
    head_lanes = heads * HEAD
    lanes = -(-(head_lanes + SEGMENTS + length // 128) // 128) * 128
    slots = 128
    kept = -(-prompt_rows // 8) * 8
    me = jnp.reshape(member, (1,))
    dp_bits = [1 << bit for bit in range(dp_size.bit_length() - 1)]
    shape = jax.ShapeDtypeStruct

    def to_core(array, name):
        return swap(array, "mp", mp_size, 1, name)

    def to_y(array, name):
        return swap(array, "mp", mp_size, 2, name)

    def to_across(array, name):
        return swap(array, "mp", mp_size, 3, name)

    place = jnp.stack([core, dp_index]).astype(jnp.int32)

    text_y, cot_y = to_y(text_rows, "text_y"), to_y(cotangent, "cotangent_y")
    up_c = to_core(ffn_in_weight, "up_core")
    down_c = to_core(ffn_out_weight, "down_core")
    right_near = lax.dynamic_slice_in_dim(right_state, core * (width // 2), width // 2, 1)
    right_near = right_near.astype(bf16)
    right_far = swap(right_near, "dp", dp_size, dp_bits[0], "right_x")
    text_c = to_core(text_rows, "text_core")

    share = slots // 2
    padded = jnp.pad(vocab_ids, (0, slots - prompt_rows), constant_values=-1)
    ids = lax.dynamic_slice_in_dim(padded, core * share, share)
    local_ids = jnp.where(ids >= 0, ids - dp_index * table_rows, -1)
    picked = local_ids[:, None] == jnp.arange(table_rows, dtype=jnp.int32)[None, :]
    found = dot(picked.astype(bf16), embed_table).astype(bf16)

    table = jnp.concatenate(
        [rel_table.astype(f32), jnp.full((rel_table.shape[0], 1), prompt_rows, f32)], axis=1
    )
    weight = jnp.transpose(qkv_weight, (1, 2, 0))
    found = pl.pallas_call(
        stage_kernel,
        out_shape=shape(found.shape, bf16),
        in_specs=[VMEM] * 2 + [ANY],
        out_specs=VMEM,
        compiler_params=params(4),
        cost_estimate=cost(0.5),
        name="stage",
    )(found, swap(found, "dp", dp_size, dp_bits[0], "prompt_x"), text_y)
    found = found + swap(found, "dp", dp_size, dp_bits[1], "prompt_z")
    for bit in dp_bits[2:-1]:
        found = found + swap(found, "dp", dp_size, bit, "prompt_far")
    found, text_y = pl.pallas_call(
        relay_kernel,
        out_shape=[
            shape(found.shape, bf16),
            shape((rows, width), bf16),
        ],
        in_specs=[SMEM] + [VMEM] * 4 + [ANY] * 3,
        out_specs=[VMEM] * 2,
        compiler_params=params(8),
        cost_estimate=cost(0.5),
        name="relay",
    )(
        table, found, swap(found, "dp", dp_size, dp_bits[-1], "prompt_far"), text_y,
        right_far, cot_y, up_c, down_c,
    )
    text_d = to_core(text_y, "text_across")
    out_y = to_y(out_weight, "out_y")

    proj_shape = shape((3, length, lanes), bf16)
    onehot, onehot_t, key_mark, query_mark, band, text_proj = pl.pallas_call(
        prep_kernel,
        out_shape=[
            shape((length, slots), bf16),
            shape((slots, length), bf16),
            shape((length, 128), bf16),
            shape((heads, length, 128), bf16),
            shape((heads, 512, 256), f32),
            proj_shape,
        ],
        in_specs=[SMEM, SMEM] + [VMEM] * 7,
        out_specs=[VMEM] * 6,
        compiler_params=params(16),
        cost_estimate=cost(3.5),
        name="project",
    )(me, table, segment_ids, text_rows, text_c, text_y, text_d, gain_one, weight)

    beside = to_core(found, "prompt_core")

    context_shapes = [shape((2, head_lanes, rows), bf16), shape((2, head_lanes, rows), f32), shape((2, heads, rows), f32)]
    score_buffer = pltpu.VMEM((heads, length + rows, rows), f32)
    forward_scratch = [pltpu.VMEM((length, lanes), bf16), score_buffer]
    joined = shape((2 * right_state.shape[0], width // 2), bf16)
    prompt, proj, right_near, ctx_near, exact_near, log_near = pl.pallas_call(
        functools.partial(forward_first, (3, 1)),
        out_shape=[shape((slots, width), bf16), proj_shape, joined] + context_shapes,
        in_specs=[SMEM] + [VMEM] * 11,
        out_specs=[VMEM] * 6,
        scratch_shapes=forward_scratch,
        compiler_params=params(24),
        cost_estimate=cost(4.5),
        name="attend",
    )(
        me, found, beside, gain_one, weight, onehot, text_proj, key_mark, query_mark, band,
        right_near, right_far,
    )
    got_d = to_across(ctx_near, "context_across")
    got_c = to_core(ctx_near, "context_core")
    out_pair, ctx_far, exact_far, log_far = pl.pallas_call(
        functools.partial(forward_second, (2, 0)),
        out_shape=[shape((2 * head_lanes, width), bf16)] + context_shapes,
        in_specs=[SMEM] + [VMEM] * 6,
        out_specs=[VMEM] * 4,
        scratch_shapes=forward_scratch,
        compiler_params=params(24),
        cost_estimate=cost(4.5),
        name="attend",
    )(me, proj, key_mark, query_mark, band, out_weight, out_y)
    out_pair = to_core(out_pair, "out_core")
    got_y = to_y(ctx_far, "context_y")
    right_far = swap(right_near, "dp", dp_size, dp_bits[1], "right_z")

    units = ffn_in_weight.shape[1]
    wide = (rows, width)

    def far_body(*refs):
        join(refs[11], refs[12], refs[16])
        ffn_kernel(2, *refs[:11], refs[13], None, *refs[14:16])

    def ffn(step, start, cot, out_shape, *extra):
        body = functools.partial(ffn_kernel, step)
        if step:
            body = far_body
        return pl.pallas_call(
            body,
            out_shape=out_shape,
            in_specs=[VMEM] * (11 + len(extra)),
            out_specs=[VMEM] * len(out_shape),
            compiler_params=params(24),
            cost_estimate=cost(4.5),
            name="ffn",
        )(
            start, gain_two, cot, ctx_far, got_y, out_weight, out_y,
            ffn_in_weight, up_c, ffn_out_weight, down_c, *extra,
        )

    start, start_y, cot_y = pl.pallas_call(
        middle_kernel,
        out_shape=[shape(wide, f32)] * 2 + [shape(wide, bf16)],
        in_specs=[SMEM] + [VMEM] * 8,
        out_specs=[VMEM] * 3,
        compiler_params=params(16),
        cost_estimate=cost(2),
        name="middle",
    )(me, text_rows, text_y, prompt, onehot, got_c, got_d, out_pair, cot_y)
    half_rows = shape((rows // 2, width), bf16)
    joined = shape((4 * right_state.shape[0], width // 2), bf16)
    far_result, *far_grad, right_near = ffn(
        2, start_y, cot_y, [shape(wide, bf16), half_rows, half_rows, joined], right_near, right_far
    )
    right_far = swap(right_near, "dp", dp_size, dp_bits[2], "right_far")
    got_grad = [to_y(piece, "grad_second_y") for piece in far_grad]
    own_result, middle, own_grad = ffn(0, start, cotangent, [shape(wide, f32)] * 3)

    send_shape = shape((head_lanes, rows), bf16)
    grad_middle, prompt_part, send_0, send_1, send_2, send_3 = pl.pallas_call(
        post_kernel,
        out_shape=[shape(wide, f32), shape((slots, width), f32)] + [send_shape] * 4,
        in_specs=[SMEM] + [VMEM] * 10,
        out_specs=[VMEM] * 6,
        compiler_params=params(16),
        cost_estimate=cost(2.2),
        name="post",
    )(me, middle, gain_two, cotangent, onehot, own_grad, *got_grad, out_weight, out_y, out_pair)
    back_2, back_3 = to_y(send_2, "grad_context_y"), to_across(send_3, "grad_context_across")
    back_1 = to_core(send_1, "grad_context_core")

    back_scratch = [
        pltpu.VMEM((length, lanes), bf16),
        pltpu.VMEM((length, heads * rows), bf16),
        pltpu.VMEM((length, heads * rows), bf16),
        pltpu.VMEM((heads * rows, lanes), bf16),
        pltpu.VMEM((heads * rows, lanes), bf16),
        score_buffer,
    ]
    sum_shape = shape((length, lanes), f32)
    exact_a, log_a = jnp.stack([exact_far[1], exact_near[1]]), jnp.stack([log_far[1], log_near[1]])
    exact_b, log_b = jnp.stack([exact_far[0], exact_near[0]]), jnp.stack([log_far[0], log_near[0]])
    query_a, key_a, value_a = pl.pallas_call(
        functools.partial(back_first, (0, 1)),
        out_shape=[shape((2, rows, lanes), bf16), sum_shape, sum_shape],
        in_specs=[SMEM] + [VMEM] * 8,
        out_specs=[VMEM] * 3,
        scratch_shapes=back_scratch,
        compiler_params=params(32),
        cost_estimate=cost(6.5),
        name="attend_back",
    )(me, proj, key_mark, query_mark, band, send_0, back_1, exact_a, log_a)
    grad_proj, part, part_other, right_far = pl.pallas_call(
        functools.partial(back_second, (2, 3)),
        out_shape=[proj_shape] + [shape((kept, width // 2), f32)] * 2 + [shape(right_far.shape, bf16)],
        in_specs=[SMEM] + [VMEM] * 17,
        out_specs=[VMEM] * 4,
        scratch_shapes=[pltpu.VMEM((length, lanes), f32)] * 2 + [pltpu.VMEM((slots, width), f32)] + back_scratch,
        compiler_params=params(36),
        cost_estimate=cost(6.5),
        name="attend_back",
    )(
        me, proj, key_mark, query_mark, band, back_2, back_3, exact_b, log_b, query_a, key_a, value_a,
        onehot_t, prompt, gain_one, weight, prompt_part, right_far,
    )

    for bit in dp_bits[3:]:
        right_near = jnp.concatenate([right_near, right_far])
        right_far = swap(right_near, "dp", dp_size, bit, "right_far")
    if right_state.shape[0] % 16:
        blocks = jnp.concatenate([right_near, right_far]).reshape(dp_size, -1, width // 2)
        blocks = jnp.take(blocks, jnp.arange(dp_size) ^ dp_index, axis=0).reshape(width, width // 2)
        right_near, right_far = blocks[: width // 2], blocks[width // 2 :]
    right_beside = [to_core(right_near, "right_core"), to_core(right_far, "right_core")]

    part = part + to_core(part_other, "prompt_grad_core")

    def add_pair(values, axis, size, bit):
        sent = values.astype(bf16)
        return sent.astype(f32) + swap(sent, axis, size, bit, "prompt_grad_sum").astype(f32)

    sent = part.astype(bf16)
    beyond = lax.ppermute(
        sent, ("dp", "mp"),
        [(i, i ^ (mp_size + 2)) for i in range(dp_size * mp_size)],
    ).astype(f32)
    over_y = swap(sent, "mp", mp_size, 2, "prompt_grad_y").astype(f32)
    over_x = swap(sent, "dp", dp_size, dp_bits[0], "prompt_grad_x").astype(f32)
    part = (sent.astype(f32) + over_y) + (over_x + beyond)
    for bit in dp_bits[1:]:
        part = add_pair(part, "dp", dp_size, bit)
    part_beside = to_core(part, "prompt_grad_other")

    first = pl.pallas_call(
        first_kernel,
        out_shape=[shape(wide, bf16)] * 4,
        in_specs=[SMEM] + [VMEM] * 2,
        out_specs=[VMEM] * 4,
        compiler_params=params(16),
        cost_estimate=cost(1.5),
        name="grad_first",
    )(me, grad_proj, weight)
    near = first[0] + to_core(first[1], "grad_first_core")
    outgoing = pl.pallas_call(
        outgoing_kernel,
        out_shape=shape((2 * rows, width), bf16),
        in_specs=[VMEM] * 3 + [ANY] * 2,
        out_specs=VMEM,
        compiler_params=params(8),
        cost_estimate=cost(0.5),
        name="outgoing",
    )(far_result, first[2], to_core(first[3], "grad_first_across"), *right_beside)
    received = to_y(outgoing, "result_and_grad_first_y")
    input_grad, result = pl.pallas_call(
        finish_kernel,
        out_shape=[shape(wide, f32), shape(wide, bf16)],
        in_specs=[SMEM] + [VMEM] * 9,
        out_specs=[VMEM] * 2,
        compiler_params=params(16),
        cost_estimate=cost(1.5),
        name="finish",
    )(me, text_rows, prompt, onehot, gain_one, grad_middle, near, received, middle, own_result)

    band_rows = right_state.shape[0]
    prompt_grad, left_new, right_new, new_prompt = pl.pallas_call(
        update_kernel,
        out_shape=[
            shape((prompt_rows, width), f32),
            shape((prompt_rows, prompt_rows), f32),
            shape((band_rows, width), f32),
            shape((prompt_rows, width), f32),
        ],
        in_specs=[SMEM] + [VMEM] * 9,
        out_specs=[VMEM] * 4,
        scratch_shapes=[
            pltpu.VMEM((slots, width), f32),
            pltpu.VMEM((slots, slots), f32),
            pltpu.VMEM((width, width), bf16),
            pltpu.VMEM((slots + width, width), bf16),
            pltpu.VMEM((width, width), bf16),
            pltpu.VMEM((width, width), bf16),
        ],
        compiler_params=params(40),
        cost_estimate=cost(16),
        name="update",
    )(
        place, part, part_beside, prompt, left_state, right_near, right_far, *right_beside,
        right_state,
    )
    return result, input_grad, prompt_grad, left_new, right_new, new_prompt


def solution(mesh):
    sizes = dict(mesh.shape)
    return jax.shard_map(
        functools.partial(local, dp_size=sizes["dp"], mp_size=sizes["mp"]),
        mesh=mesh,
        in_specs=(
            P(("dp", "mp"), None),
            P("dp", None),
            P(),
            P("dp", None),
            P(),
            P(),
            P(None, None, "mp"),
            P("mp", None),
            P(None, "mp"),
            P("mp", None),
            P(None, "mp"),
            P(("dp", "mp"), None),
            P(),
            P("dp", None),
        ),
        out_specs=(P(("dp", "mp"), None), P(("dp", "mp"), None), P(), P(), P("dp", None), P()),
        check_vma=False,
    )
```

```python
import functools

import jax
import jax.numpy as jnp
from jax import lax
from jax.experimental import pallas as pl
from jax.experimental.pallas import tpu as pltpu
from jax.sharding import PartitionSpec as P

ROOT_STEPS = 5
HEAD = 64
SEGMENTS = 8
PENALTY = -1000000000.0

norm_epsilon = 1e-06
step_rate = 0.5
bucket_edges = (12, 16, 23, 32, 46, 64, 91)
bf16 = jnp.bfloat16
f32 = jnp.float32
MIB = 1024 * 1024
TILE = 256

VMEM = pl.BlockSpec(memory_space=pltpu.VMEM)
ANY = pl.BlockSpec(memory_space=pl.ANY)
SMEM = pl.BlockSpec(memory_space=pltpu.SMEM)


def dot(left, right):
    return lax.dot_general(left, right, (((1,), (0,)), ((), ())), preferred_element_type=f32)


def dot_t(left, right):
    return lax.dot_general(left, right, (((1,), (1,)), ((), ())), preferred_element_type=f32)


def dot_rows(left, right):
    return lax.dot_general(left, right, (((0,), (0,)), ((), ())), preferred_element_type=f32)


def split(values):
    high = values.astype(bf16)
    return high, (values - high.astype(f32)).astype(bf16)


def swap(array, axis, count, bit, name):
    with jax.named_scope(name):
        return lax.ppermute(array, axis, [(i, i ^ bit) for i in range(count)])


def rms_scale(values):
    return lax.rsqrt(jnp.mean(values * values, axis=-1, keepdims=True) + norm_epsilon)


def norm_back(values, gain, grad):
    scale = rms_scale(values)
    inner = gain * grad
    mean = jnp.mean(values * inner, axis=-1, keepdims=True)
    return scale * inner - values * (scale * scale * scale * mean)


def params(limit=56):
    return pltpu.CompilerParams(vmem_limit_bytes=limit * MIB)


def cost(time):
    return pl.CostEstimate(flops=int(time), bytes_accessed=int(time * 3.5e6), transcendentals=0)


def stage_kernel(found, received, _text, out):
    out[...] = found[...] + received[...]


def relay_kernel(
    table, found, received, text, right, _cotangent, _up, _down, out, text_out
):
    out[...] = found[...] + received[...]
    text_out[...] = text[...]


def prep_kernel(
    member, table, segments, x0, x1, x2, x3, gain, weight,
    onehot, onehot_t, key_mark, query_mark, band, out,
):
    length = segments.shape[1]
    slots = onehot_t.shape[0]
    heads, tall, wide = band.shape
    tile = tall // 4
    segment = segments[...]
    first = jnp.zeros_like(segment)
    for number in range(1, SEGMENTS):
        before = jnp.sum(jnp.where(segment < number, 1.0, 0.0), axis=-1, keepdims=True)
        first = jnp.where(segment == number, before.astype(jnp.int32), first)
    offset = lax.broadcasted_iota(jnp.int32, segment.shape, 1) - first
    slot = jnp.where(offset < table[0, heads].astype(jnp.int32), offset, -1)
    placed = lax.broadcasted_iota(jnp.int32, (slots, length), 0) == slot
    placed = jnp.where(placed, 1.0, 0.0)
    onehot_t[...] = placed.astype(bf16)
    onehot[...] = jnp.transpose(placed).astype(bf16)
    lanes = key_mark.shape[1]
    spare = heads * HEAD % lanes
    segment_t = jnp.transpose(jnp.broadcast_to(segment.astype(f32), (lanes, length)))
    lane = lax.broadcasted_iota(jnp.int32, (length, lanes), 1) - spare
    tile_at = lax.broadcasted_iota(jnp.int32, (length, lanes), 0) // tile
    in_segment = (lane >= 0) & (lane < SEGMENTS)
    in_tile = (lane >= SEGMENTS) & (lane < SEGMENTS + length // tile)
    same = segment_t == lane.astype(f32)
    other_tile = lane - SEGMENTS
    key_mark[...] = jnp.where(
        (in_segment & ~same) | (in_tile & (tile_at == other_tile)), 1.0, 0.0
    ).astype(bf16)
    for head in range(heads):
        values = jnp.where(in_segment & same, PENALTY, 0.0)
        values = jnp.where(in_tile & (other_tile < tile_at - 1), table[15, head], values)
        values = jnp.where(in_tile & (other_tile > tile_at + 1), table[31, head], values)
        query_mark[head] = values.astype(bf16)
    rows = lax.broadcasted_iota(jnp.int32, (tile, tile), 0)
    columns = lax.broadcasted_iota(jnp.int32, (tile, tile), 1)
    zero = jnp.zeros((tile, tile), f32)
    for head in range(heads):
        band[head, :tile, tile:] = zero
        band[head, 3 * tile :, :tile] = zero
    for shift in (-1, 0, 1):
        relative = rows - columns + shift * tile
        distance = jnp.abs(relative)
        bucket = jnp.full((tile, tile), 8, jnp.int32)
        for edge in bucket_edges:
            bucket = bucket + jnp.where(distance >= edge, 1, 0)
        bucket = jnp.where(distance < 8, distance, bucket) + jnp.where(relative > 0, 16, 0)
        numbers = {-1: range(1, 16), 0: (*range(0, 16), *range(17, 32)), 1: range(17, 32)}[shift]
        values = [zero] * heads
        for number in numbers:
            here = bucket == number
            values = [jnp.where(here, table[number, head], values[head]) for head in range(heads)]
        for head in range(heads):
            for half in range(2):
                at = (shift + 1 + half) * tile
                band[head, at : at + tile, half * tile : half * tile + tile] = values[head]

    me = member[0]
    rows = x0.shape[0]
    used = weight.shape[1]
    out[:, :, used:] = jnp.zeros((3, out.shape[1], out.shape[2] - used), bf16)
    for step, ref in enumerate((x0, x1, x2, x3)):
        place = pl.ds(pl.multiple_of((me ^ step) * rows, rows), rows)
        values = ref[...].astype(f32)
        inside = jnp.max(onehot[place, :].astype(f32), axis=-1, keepdims=True) > 0.0
        scale = jnp.where(inside, 0.0, rms_scale(values))
        normed = (values * scale * gain[...].reshape(1, -1)).astype(bf16)
        for part in range(3):
            out[part, place, :used] = dot_t(normed, weight[part]).astype(bf16)


def lane_head(rows, lanes):
    return lax.broadcasted_iota(jnp.int32, (rows, lanes), 1) // HEAD


def marked_keys(keys, key, key_mark):
    lanes = key_mark.shape[1]
    keys[:, :lanes] = key[:, :lanes]
    keys[:, lanes:] = key[:, lanes:] + key_mark[...]


def block_scores(scores, keys, queries, marks, which, head, band, block):
    rows = queries.shape[0]
    length = keys.shape[0]
    mine = jnp.where(which == head, queries, marks)
    margin = rows // 2
    scores[margin : margin + length, :] = dot_t(keys[...], mine)
    near = pl.ds(pl.multiple_of(block * rows, rows), 2 * rows)
    scores[near, :] += band[head]
    return scores[margin : margin + length, :]


def padded_marks(query_mark, head, place, lanes):
    marks = query_mark[head, place, :]
    return jnp.concatenate([jnp.zeros((marks.shape[0], lanes - marks.shape[1]), bf16), marks], axis=1)


def attend_blocks(steps, member, proj, key_mark, query_mark, band, refs):
    contexts, exact, log_rows, keys, scores_buf = refs
    rows = contexts.shape[2]
    used = contexts.shape[1]
    heads = used // HEAD
    lanes = proj.shape[2]
    marked_keys(keys, proj[1], key_mark)
    which = lane_head(rows, lanes)
    for at, step in enumerate(steps):
        block = member[0] ^ step
        place = pl.ds(pl.multiple_of(block * rows, rows), rows)
        queries = proj[0, place, :]
        mixed = jnp.zeros((rows, lanes), f32)
        sums = []
        for head in range(heads):
            marks = padded_marks(query_mark, head, place, lanes)
            scores = block_scores(
                scores_buf.at[head], keys, queries, marks, which, head, band, block
            )
            row_max = jnp.max(scores, axis=0, keepdims=True)
            exponent = jnp.exp(scores - row_max)
            row_sum = jnp.sum(exponent, axis=0, keepdims=True)
            mixed = jnp.where(which == head, dot_rows(exponent.astype(bf16), proj[2]), mixed)
            log_rows[at, head : head + 1, :] = row_max + jnp.log(row_sum)
            sums.append(jnp.broadcast_to(1.0 / row_sum, (HEAD, rows)))
        context = jnp.transpose(mixed)[:used] * jnp.concatenate(sums, axis=0)
        contexts[at] = context.astype(bf16)
        exact[at] = context


def join(near, far, out):
    count = near.shape[0]
    out[:count] = near[...]
    out[count:] = far[...]


def forward_first(
    steps, member, found, beside, gain, weight, onehot, text, key_mark, query_mark, band,
    near, far, prompt, proj, joined, *refs
):
    join(near, far, joined)
    share = found.shape[0]
    core = member[0] & 1
    prompt[pl.ds(pl.multiple_of(core * share, share), share), :] = found[...]
    prompt[pl.ds(pl.multiple_of((1 - core) * share, share), share), :] = beside[...]
    values = prompt[...].astype(f32)
    normed = (values * rms_scale(values) * gain[...].reshape(1, -1)).astype(bf16)
    used = weight.shape[1]
    for part in range(3):
        projected = dot_t(normed, weight[part]).astype(bf16)
        proj[part, :, :used] = text[part, :, :used] + dot(onehot[...], projected).astype(bf16)
    proj[:, :, used:] = text[:, :, used:]
    attend_blocks(steps, member, proj, key_mark, query_mark, band, refs)


def forward_second(steps, member, proj, key_mark, query_mark, band, near, far, joined, *refs):
    join(near, far, joined)
    attend_blocks(steps, member, proj, key_mark, query_mark, band, refs)


def own_input(member, step, text, prompt, onehot):
    rows = text.shape[0]
    mine = onehot[pl.ds(pl.multiple_of((member[0] ^ step) * rows, rows), rows), :]
    inside = jnp.max(mine.astype(f32), axis=-1, keepdims=True) > 0.0
    return mine, inside, jnp.where(inside, dot(mine, prompt[...]), text[...].astype(f32))


def middle_kernel(
    member, text, text_y, prompt, onehot, left, across, weights, cotangent, out, out_y, cot_out
):
    cot_out[...] = cotangent[...]
    for step, rows, result in ((0, text, out), (2, text_y, out_y)):
        at = step // 2
        layer_in = own_input(member, step, rows, prompt, onehot)[2]
        part = left.shape[1]
        added = dot(jnp.transpose(left[1 - at]), weights[:part])
        added = added + dot(jnp.transpose(across[at]), weights[part:])
        result[...] = layer_in + added


def ffn_kernel(step, place, start, gain, cotangent, near, far, *refs):
    outs_w, ups, downs = refs[:2], refs[2:4], refs[4:6]
    result, middle_out, grad_second = refs[6:9]
    at = step // 2
    added = dot(jnp.transpose(near[1 - at, :, place]), outs_w[0][...])
    added = added + dot(jnp.transpose(far[at, :, place]), outs_w[1][...])
    middle = start[place, :] + added
    if middle_out is not None:
        middle_out[...] = middle
    second = (middle * rms_scale(middle) * gain[...].reshape(1, -1)).astype(bf16)
    cot = cotangent[place, :]
    total = jnp.zeros_like(middle)
    grad = jnp.zeros_like(middle)
    root = 0.7978845608028654
    for up, down in zip(ups, downs):
        hidden = dot(second, up[...])
        square = hidden * hidden
        tanh = jnp.tanh(root * hidden * (1.0 + 0.044715 * square))
        half = 0.5 + 0.5 * tanh
        active = (hidden * half).astype(bf16)
        slope = half + (0.5 * root) * hidden * (1.0 - tanh * tanh) * (1.0 + 0.134145 * square)
        grad_hidden = (dot_t(cot, down[...]) * slope).astype(bf16)
        grad = grad + dot_t(grad_hidden, up[...])
        total = total + dot(active, down[...])
    grad_second[...] = grad.astype(grad_second.dtype)
    result[...] = total.astype(result.dtype)


def post_kernel(member, middle, gain, cotangent, onehot, own, received, received_b, *refs):
    weight, weight_y, pair, grad_middle_out, prompt_part = refs[:5]
    sends = refs[5:]
    part = weight.shape[0]
    outs_w = (weight, pair.at[:part], weight_y, pair.at[part:])
    rows, half = own.shape[0], received.shape[0]
    received = jnp.concatenate([received[...], received_b[...]]).astype(f32)
    grad_second = own[...] + received
    grad_middle = cotangent[...].astype(f32) + norm_back(middle[...], gain[...].reshape(1, -1), grad_second)
    grad_middle_out[...] = grad_middle
    send = grad_middle.astype(bf16)
    for out, weight in zip(sends, outs_w):
        out[...] = dot_t(weight[...], send).astype(bf16)
    mine_t = jnp.transpose(onehot[pl.ds(pl.multiple_of(member[0] * rows, rows), rows), :])
    high, low = split(grad_middle)
    prompt_part[...] = dot(mine_t, high) + dot(mine_t, low)


def back_blocks(steps, member, proj, key_mark, query_mark, band, grads, exact, log_rows, grad_query, sums, started, buffers):
    keys, prob_buf, grad_buf, query_all, out_all, scores_buf = buffers
    key_sum, value_sum = sums
    rows = grads[0].shape[1]
    heads = grads[0].shape[0] // HEAD
    lanes = proj.shape[2]
    marked_keys(keys, proj[1], key_mark)
    which = lane_head(rows, lanes)
    for at, step in enumerate(steps):
        block = member[0] ^ step
        place = pl.ds(pl.multiple_of(block * rows, rows), rows)
        queries = proj[0, place, :]
        grad_t = jnp.concatenate(
            [grads[at][...], jnp.zeros((lanes - heads * HEAD, rows), bf16)], axis=0
        )
        grad_out = jnp.transpose(grad_t)
        mixed = jnp.zeros((rows, lanes), f32)
        for head in range(heads):
            near = which == head
            own_grad = jnp.where(near, grad_out, jnp.zeros_like(grad_out))
            part = slice(head * HEAD, head * HEAD + HEAD)
            stack = slice(head * rows, head * rows + rows)
            query_all[stack, :] = jnp.where(near, queries, jnp.zeros_like(queries))
            out_all[stack, :] = own_grad
            marks = padded_marks(query_mark, head, place, lanes)
            scores = block_scores(
                scores_buf.at[head], keys, queries, marks, which, head, band, block
            )
            probs = jnp.exp(scores - log_rows[at, head : head + 1, :])
            prob_buf[:, stack] = probs.astype(bf16)
            grad_probs = dot_t(proj[2], own_grad)
            inner = jnp.sum(grads[at][part, :].astype(f32) * exact[at, part, :], axis=0, keepdims=True)
            grad_scores = (probs * (grad_probs - inner)).astype(bf16)
            grad_buf[:, stack] = grad_scores
            mixed = jnp.where(near, dot_rows(grad_scores, proj[1]), mixed)
        grad_query(step, place, mixed.astype(bf16))
        more_keys = dot(grad_buf[...], query_all[...])
        more_values = dot(prob_buf[...], out_all[...])
        if at == 0 and not started:
            key_sum[...] = more_keys
            value_sum[...] = more_values
        else:
            key_sum[...] += more_keys
            value_sum[...] += more_values


def back_first(steps, member, proj, key_mark, query_mark, band, *refs):
    grads, exact, log_rows = refs[0:2], refs[2], refs[3]
    query_out, key_sum, value_sum = refs[4:7]

    def store(step, place, values):
        query_out[steps.index(step)] = values

    back_blocks(steps, member, proj, key_mark, query_mark, band, grads, exact, log_rows, store,
                (key_sum, value_sum), False, refs[7:])


def back_second(steps, member, proj, key_mark, query_mark, band, *refs):
    grads, exact, log_rows = refs[0:2], refs[2], refs[3]
    query_in, key_in, value_in = refs[4:7]
    onehot_t, prompt, gain, weight, prompt_part, far, out, part_mine, part_other, far_out = refs[7:17]
    key_sum, value_sum, total_buf = refs[17:20]
    rows = grads[0].shape[1]
    far_out[...] = far[...]
    key_sum[...] = key_in[...]
    value_sum[...] = value_in[...]

    def store(step, place, values):
        out[0, place, :] = values

    for at in range(2):
        out[0, pl.ds(pl.multiple_of((member[0] ^ at) * rows, rows), rows), :] = query_in[at]
    back_blocks(steps, member, proj, key_mark, query_mark, band, grads, exact, log_rows, store,
                (key_sum, value_sum), True, refs[20:])
    out[1] = key_sum[...].astype(bf16)
    out[2] = value_sum[...].astype(bf16)
    grad = jnp.zeros((prompt.shape[0], prompt.shape[1]), f32)
    for part in range(3):
        high, low = split(dot(onehot_t[...], out[part])[:, : weight.shape[1]])
        grad = grad + dot(high, weight[part]) + dot(low, weight[part])
    total_buf[...] = prompt_part[...] + norm_back(prompt[...].astype(f32), gain[...].reshape(1, -1), grad)
    kept, half = part_mine.shape
    core = member[0] & 1
    part_mine[...] = total_buf[:kept, pl.ds(pl.multiple_of(core * half, half), half)]
    part_other[...] = total_buf[:kept, pl.ds(pl.multiple_of((1 - core) * half, half), half)]


def first_kernel(member, grad_proj, weight, *outs):
    rows = outs[0].shape[0]
    used = weight.shape[1]
    for step, out in enumerate(outs):
        place = pl.ds(pl.multiple_of((member[0] ^ step) * rows, rows), rows)
        total = dot(grad_proj[0, place, :used], weight[0])
        for part in (1, 2):
            total = total + dot(grad_proj[part, place, :used], weight[part])
        out[...] = total.astype(out.dtype)


def outgoing_kernel(result_a, result_b, own, other, _near, _far, out):
    rows = own.shape[0]
    out[: rows // 2] = result_a[...]
    out[rows // 2 : rows] = result_b[...]
    out[rows:] = own[...] + other[...]


def finish_kernel(
    member, text, prompt, onehot, gain, grad_middle, own, received, middle, own_result, out, result
):
    rows = text.shape[0]
    _, inside, layer_in = own_input(member, 0, text, prompt, onehot)
    grad_first = own[...].astype(f32) + received[rows:].astype(f32)
    start = grad_middle[...] + norm_back(layer_in, gain[...].reshape(1, -1), grad_first)
    out[...] = jnp.where(inside, 0.0, start)
    result[...] = (middle[...] + own_result[...] + received[:rows].astype(f32)).astype(bf16)


def newton_step(current):
    low = current.astype(bf16)
    inner = -0.625 * current + 0.0625 * dot(low, low)
    inner_low = inner.astype(bf16)
    outer = 3.125 * inner + dot(inner_low, inner_low)
    return 2.44140625 * current + dot(outer.astype(bf16), low)


def put_columns(target, first, block, values):
    low = values.astype(bf16)
    begin = block * TILE
    lanes = slice(begin, begin + TILE)
    target[first : first + begin + TILE, lanes] = low
    if block:
        target[first + begin : first + begin + TILE, :begin] = jnp.transpose(low[:begin])


def update_kernel(
    place, mine, other, prompt, left, near_a, far_a, near_b, far_b, band_state,
    grad_out, left_out, band_out, prompt_out, grad, left_pad, right, matrix, inner_buf, outer_buf,
):
    kept, half = mine.shape
    count, width = prompt_out.shape
    band = band_state.shape[0]
    size = grad.shape[0]
    core = place[0]
    half_rows = width // 2
    grad[...] = jnp.zeros_like(grad)
    for side, pieces in ((core, (near_a, far_a)), (1 - core, (near_b, far_b))):
        columns = pl.ds(pl.multiple_of(side * half, half), half)
        for at in range(width // band):
            source = pieces[at * band // half_rows]
            begin = at * band % half_rows
            target = at * band
            if band % 16 == 0:
                target = pl.multiple_of((place[1] ^ at) * band, 16)
            elif at * band % half_rows:
                continue
            count_rows = band if band % 16 == 0 else half_rows
            right[pl.ds(target, count_rows), columns] = source[begin : begin + count_rows, :]
    grad[:kept, pl.ds(pl.multiple_of(core * half, half), half)] = mine[...]
    grad[:kept, pl.ds(pl.multiple_of((1 - core) * half, half), half)] = other[...]
    value = grad[...]
    grad_out[...] = value[:count]
    high, low = split(value)
    high_t, low_t = jnp.transpose(high), jnp.transpose(low)
    left_gram = dot(high, high_t) + dot(high, low_t) + dot(low, high_t)
    left_new = 0.5 * left[...] + 0.5 * left_gram[:count, :count]
    left_out[...] = left_new

    tops = [begin + TILE for begin in range(0, width, TILE)]
    columns = []
    total = 0.0
    for top in tops:
        lanes = slice(top - TILE, top)
        values = 0.5 * right[:top, lanes].astype(f32) + 0.5 * dot(high_t[:top], high[:, lanes])
        squares = values * values
        if top > TILE:
            total = total + 2.0 * jnp.sum(squares[: top - TILE])
        total = total + jnp.sum(squares[top - TILE :])
        columns.append(values)
    right_scale = 1.25 * lax.rsqrt(total)
    pick = (
        lax.broadcasted_iota(jnp.int32, (band, width), 1)
        == lax.broadcasted_iota(jnp.int32, (band, width), 0) + place[1] * band
    )
    pick = jnp.where(pick, 1.0, 0.0).astype(bf16)
    pick_high, pick_low = dot_t(pick, high).astype(bf16), dot_t(pick, low).astype(bf16)
    band_out[...] = 0.5 * band_state[...] + 0.5 * (
        dot(pick_high, high) + dot(pick_high, low) + dot(pick_low, high)
    )

    left_pad[...] = jnp.zeros_like(left_pad)
    left_pad[:count, :count] = left_new
    left_mat = left_pad[...]
    left_scale = 1.25 * lax.rsqrt(jnp.sum(left_mat * left_mat))
    left_mat = left_mat * left_scale
    root = jnp.where(
        lax.broadcasted_iota(jnp.int32, (size, size), 0)
        == lax.broadcasted_iota(jnp.int32, (size, size), 1),
        1.0,
        0.0,
    )
    thin = value
    columns = [values * right_scale for values in columns]
    for block, values in enumerate(columns):
        put_columns(matrix, size, block, values)
    for repeat in range(ROOT_STEPS - 2):
        matrix[:size, :] = thin.astype(bf16)
        inner, thin_parts = [], []
        for block, top in enumerate(tops):
            lanes = slice(top - TILE, top)
            product = dot(matrix[: size + top, :], matrix[size:, lanes])
            thin_parts.append(product[:size])
            inner.append(-0.625 * columns[block] + 0.0625 * product[size:])
            put_columns(inner_buf, 0, block, inner[block])
        thin = 1.25 * thin - 0.25 * jnp.concatenate(thin_parts, axis=1)
        root = 1.25 * root - 0.25 * dot(root.astype(bf16), left_mat.astype(bf16))
        left_mat = newton_step(left_mat)
        for block, top in enumerate(tops):
            lanes = slice(top - TILE, top)
            outer = 3.125 * inner[block] + dot(inner_buf[:top, :], inner_buf[:, lanes])
            put_columns(outer_buf, 0, block, outer)
        for block, top in enumerate(tops):
            lanes = slice(top - TILE, top)
            columns[block] = 2.44140625 * columns[block] + dot(
                outer_buf[:top, :], matrix[size:, lanes]
            )
        for block, values in enumerate(columns):
            put_columns(matrix, size, block, values)

    def thin_dot(values):
        return dot(values.astype(bf16), matrix[size:, :])

    root = 1.25 * root - 0.25 * dot(root.astype(bf16), left_mat.astype(bf16))
    left_mat = newton_step(left_mat)
    thin = 1.25 * thin - 0.25 * thin_dot(thin)
    power = thin
    for repeat in range(4):
        power = 1.25 * power - 0.25 * thin_dot(power)
    thin = 1.25 * thin - 0.25 * thin_dot(power)
    root = 1.25 * root - 0.25 * dot(root.astype(bf16), left_mat.astype(bf16))
    direction = dot(root.astype(bf16), thin.astype(bf16))
    scale = jnp.sqrt(jnp.sqrt(left_scale)) * jnp.sqrt(jnp.sqrt(right_scale))
    direction = (direction * scale)[:count]
    prompt_value = prompt[...].astype(f32)[:count]
    cells = 1.0 / (count * width)
    ratio = jnp.sqrt(jnp.sum(prompt_value * prompt_value) * cells + norm_epsilon) * lax.rsqrt(
        jnp.sum(direction * direction) * cells + norm_epsilon
    )
    prompt_out[...] = prompt_value - step_rate * ratio * direction


def local(
    text_rows, segment_ids, vocab_ids, embed_table, gain_one, gain_two, qkv_weight, out_weight,
    ffn_in_weight, ffn_out_weight, rel_table, cotangent, left_state, right_state,
    *, dp_size, mp_size,
):
    member = lax.axis_index("mp")
    dp_index = lax.axis_index("dp")
    core = member % 2
    rows, width = text_rows.shape
    length = segment_ids.shape[1]
    prompt_rows = vocab_ids.shape[0]
    table_rows = embed_table.shape[0]
    heads = rel_table.shape[1]
    head_lanes = heads * HEAD
    lanes = -(-(head_lanes + SEGMENTS + length // 128) // 128) * 128
    slots = 128
    kept = -(-prompt_rows // 8) * 8
    me = jnp.reshape(member, (1,))
    dp_bits = [1 << bit for bit in range(dp_size.bit_length() - 1)]
    shape = jax.ShapeDtypeStruct

    def to_core(array, name):
        return swap(array, "mp", mp_size, 1, name)

    def to_y(array, name):
        return swap(array, "mp", mp_size, 2, name)

    def to_across(array, name):
        return swap(array, "mp", mp_size, 3, name)

    place = jnp.stack([core, dp_index]).astype(jnp.int32)

    text_y, cot_y = to_y(text_rows, "text_y"), to_y(cotangent, "cotangent_y")
    up_c = to_core(ffn_in_weight, "up_core")
    down_c = to_core(ffn_out_weight, "down_core")
    right_near = lax.dynamic_slice_in_dim(right_state, core * (width // 2), width // 2, 1)
    right_near = right_near.astype(bf16)
    right_far = swap(right_near, "dp", dp_size, dp_bits[0], "right_x")
    text_c = to_core(text_rows, "text_core")

    share = slots // 2
    padded = jnp.pad(vocab_ids, (0, slots - prompt_rows), constant_values=-1)
    ids = lax.dynamic_slice_in_dim(padded, core * share, share)
    local_ids = jnp.where(ids >= 0, ids - dp_index * table_rows, -1)
    picked = local_ids[:, None] == jnp.arange(table_rows, dtype=jnp.int32)[None, :]
    found = dot(picked.astype(bf16), embed_table).astype(bf16)

    table = jnp.concatenate(
        [rel_table.astype(f32), jnp.full((rel_table.shape[0], 1), prompt_rows, f32)], axis=1
    )
    weight = jnp.transpose(qkv_weight, (1, 2, 0))
    found = pl.pallas_call(
        stage_kernel,
        out_shape=shape(found.shape, bf16),
        in_specs=[VMEM] * 2 + [ANY],
        out_specs=VMEM,
        compiler_params=params(4),
        cost_estimate=cost(0.5),
        name="stage",
    )(found, swap(found, "dp", dp_size, dp_bits[0], "prompt_x"), text_y)
    found = found + swap(found, "dp", dp_size, dp_bits[1], "prompt_z")
    for bit in dp_bits[2:-1]:
        found = found + swap(found, "dp", dp_size, bit, "prompt_far")
    found, text_y = pl.pallas_call(
        relay_kernel,
        out_shape=[
            shape(found.shape, bf16),
            shape((rows, width), bf16),
        ],
        in_specs=[SMEM] + [VMEM] * 4 + [ANY] * 3,
        out_specs=[VMEM] * 2,
        compiler_params=params(8),
        cost_estimate=cost(0.5),
        name="relay",
    )(
        table, found, swap(found, "dp", dp_size, dp_bits[-1], "prompt_far"), text_y,
        right_far, cot_y, up_c, down_c,
    )
    text_d = to_core(text_y, "text_across")
    out_y = to_y(out_weight, "out_y")

    proj_shape = shape((3, length, lanes), bf16)
    onehot, onehot_t, key_mark, query_mark, band, text_proj = pl.pallas_call(
        prep_kernel,
        out_shape=[
            shape((length, slots), bf16),
            shape((slots, length), bf16),
            shape((length, 128), bf16),
            shape((heads, length, 128), bf16),
            shape((heads, 512, 256), f32),
            proj_shape,
        ],
        in_specs=[SMEM, SMEM] + [VMEM] * 7,
        out_specs=[VMEM] * 6,
        compiler_params=params(16),
        cost_estimate=cost(3.5),
        name="project",
    )(me, table, segment_ids, text_rows, text_c, text_y, text_d, gain_one, weight)

    beside = to_core(found, "prompt_core")

    context_shapes = [shape((2, head_lanes, rows), bf16), shape((2, head_lanes, rows), f32), shape((2, heads, rows), f32)]
    score_buffer = pltpu.VMEM((heads, length + rows, rows), f32)
    forward_scratch = [pltpu.VMEM((length, lanes), bf16), score_buffer]
    joined = shape((2 * right_state.shape[0], width // 2), bf16)
    prompt, proj, right_near, ctx_near, exact_near, log_near = pl.pallas_call(
        functools.partial(forward_first, (3, 1)),
        out_shape=[shape((slots, width), bf16), proj_shape, joined] + context_shapes,
        in_specs=[SMEM] + [VMEM] * 11,
        out_specs=[VMEM] * 6,
        scratch_shapes=forward_scratch,
        compiler_params=params(24),
        cost_estimate=cost(4.5),
        name="attend",
    )(
        me, found, beside, gain_one, weight, onehot, text_proj, key_mark, query_mark, band,
        right_near, right_far,
    )
    got_d = to_across(ctx_near, "context_across")
    got_c = to_core(ctx_near, "context_core")
    out_pair, ctx_far, exact_far, log_far = pl.pallas_call(
        functools.partial(forward_second, (2, 0)),
        out_shape=[shape((2 * head_lanes, width), bf16)] + context_shapes,
        in_specs=[SMEM] + [VMEM] * 6,
        out_specs=[VMEM] * 4,
        scratch_shapes=forward_scratch,
        compiler_params=params(24),
        cost_estimate=cost(4.5),
        name="attend",
    )(me, proj, key_mark, query_mark, band, out_weight, out_y)
    out_pair = to_core(out_pair, "out_core")
    got_y = to_y(ctx_far, "context_y")
    right_far = swap(right_near, "dp", dp_size, dp_bits[1], "right_z")

    units = ffn_in_weight.shape[1]
    wide = (rows, width)

    half = rows // 2

    def far_first(*refs):
        join(refs[11], refs[12], refs[15])
        ffn_kernel(2, slice(0, half), *refs[:11], refs[13], None, refs[14])

    def far_second(*refs):
        ffn_kernel(2, slice(half, rows), *refs[:11], refs[11], None, refs[12])

    def ffn(body, start, cot, out_shape, *extra):
        return pl.pallas_call(
            body,
            out_shape=out_shape,
            in_specs=[VMEM] * (11 + len(extra)),
            out_specs=[VMEM] * len(out_shape),
            compiler_params=params(24),
            cost_estimate=cost(4.5),
            name="ffn",
        )(
            start, gain_two, cot, ctx_far, got_y, out_weight, out_y,
            ffn_in_weight, up_c, ffn_out_weight, down_c, *extra,
        )

    start, start_y, cot_y = pl.pallas_call(
        middle_kernel,
        out_shape=[shape(wide, f32)] * 2 + [shape(wide, bf16)],
        in_specs=[SMEM] + [VMEM] * 8,
        out_specs=[VMEM] * 3,
        compiler_params=params(16),
        cost_estimate=cost(2),
        name="middle",
    )(me, text_rows, text_y, prompt, onehot, got_c, got_d, out_pair, cot_y)
    half_rows = shape((rows // 2, width), bf16)
    joined = shape((4 * right_state.shape[0], width // 2), bf16)
    result_a, grad_a, right_near = ffn(
        far_first, start_y, cot_y, [half_rows, half_rows, joined], right_near, right_far
    )
    result_b, grad_b = ffn(far_second, start_y, cot_y, [half_rows, half_rows])
    right_far = swap(right_near, "dp", dp_size, dp_bits[2], "right_far")
    got_grad = [to_y(piece, "grad_second_y") for piece in (grad_a, grad_b)]
    own_result, middle, own_grad = ffn(
        functools.partial(ffn_kernel, 0, slice(0, rows)), start, cotangent, [shape(wide, f32)] * 3
    )

    send_shape = shape((head_lanes, rows), bf16)
    grad_middle, prompt_part, send_0, send_1, send_2, send_3 = pl.pallas_call(
        post_kernel,
        out_shape=[shape(wide, f32), shape((slots, width), f32)] + [send_shape] * 4,
        in_specs=[SMEM] + [VMEM] * 10,
        out_specs=[VMEM] * 6,
        compiler_params=params(16),
        cost_estimate=cost(2.2),
        name="post",
    )(me, middle, gain_two, cotangent, onehot, own_grad, *got_grad, out_weight, out_y, out_pair)
    back_2, back_3 = to_y(send_2, "grad_context_y"), to_across(send_3, "grad_context_across")
    back_1 = to_core(send_1, "grad_context_core")

    back_scratch = [
        pltpu.VMEM((length, lanes), bf16),
        pltpu.VMEM((length, heads * rows), bf16),
        pltpu.VMEM((length, heads * rows), bf16),
        pltpu.VMEM((heads * rows, lanes), bf16),
        pltpu.VMEM((heads * rows, lanes), bf16),
        score_buffer,
    ]
    sum_shape = shape((length, lanes), f32)
    exact_a, log_a = jnp.stack([exact_far[1], exact_near[1]]), jnp.stack([log_far[1], log_near[1]])
    exact_b, log_b = jnp.stack([exact_far[0], exact_near[0]]), jnp.stack([log_far[0], log_near[0]])
    query_a, key_a, value_a = pl.pallas_call(
        functools.partial(back_first, (0, 1)),
        out_shape=[shape((2, rows, lanes), bf16), sum_shape, sum_shape],
        in_specs=[SMEM] + [VMEM] * 8,
        out_specs=[VMEM] * 3,
        scratch_shapes=back_scratch,
        compiler_params=params(32),
        cost_estimate=cost(6.5),
        name="attend_back",
    )(me, proj, key_mark, query_mark, band, send_0, back_1, exact_a, log_a)
    grad_proj, part, part_other, right_far = pl.pallas_call(
        functools.partial(back_second, (2, 3)),
        out_shape=[proj_shape] + [shape((kept, width // 2), f32)] * 2 + [shape(right_far.shape, bf16)],
        in_specs=[SMEM] + [VMEM] * 17,
        out_specs=[VMEM] * 4,
        scratch_shapes=[pltpu.VMEM((length, lanes), f32)] * 2 + [pltpu.VMEM((slots, width), f32)] + back_scratch,
        compiler_params=params(36),
        cost_estimate=cost(6.5),
        name="attend_back",
    )(
        me, proj, key_mark, query_mark, band, back_2, back_3, exact_b, log_b, query_a, key_a, value_a,
        onehot_t, prompt, gain_one, weight, prompt_part, right_far,
    )

    for bit in dp_bits[3:]:
        right_near = jnp.concatenate([right_near, right_far])
        right_far = swap(right_near, "dp", dp_size, bit, "right_far")
    if right_state.shape[0] % 16:
        blocks = jnp.concatenate([right_near, right_far]).reshape(dp_size, -1, width // 2)
        blocks = jnp.take(blocks, jnp.arange(dp_size) ^ dp_index, axis=0).reshape(width, width // 2)
        right_near, right_far = blocks[: width // 2], blocks[width // 2 :]
    right_beside = [to_core(right_near, "right_core"), to_core(right_far, "right_core")]

    part = part + to_core(part_other, "prompt_grad_core")

    def add_pair(values, axis, size, bit):
        sent = values.astype(bf16)
        return sent.astype(f32) + swap(sent, axis, size, bit, "prompt_grad_sum").astype(f32)

    sent = part.astype(bf16)
    beyond = lax.ppermute(
        sent, ("dp", "mp"),
        [(i, i ^ (mp_size + 2)) for i in range(dp_size * mp_size)],
    ).astype(f32)
    over_y = swap(sent, "mp", mp_size, 2, "prompt_grad_y").astype(f32)
    over_x = swap(sent, "dp", dp_size, dp_bits[0], "prompt_grad_x").astype(f32)
    part = (beyond + over_x) + (over_y + sent.astype(f32))
    for bit in dp_bits[1:]:
        part = add_pair(part, "dp", dp_size, bit)
    part_beside = to_core(part, "prompt_grad_other")

    first = pl.pallas_call(
        first_kernel,
        out_shape=[shape(wide, bf16)] * 4,
        in_specs=[SMEM] + [VMEM] * 2,
        out_specs=[VMEM] * 4,
        compiler_params=params(16),
        cost_estimate=cost(1.5),
        name="grad_first",
    )(me, grad_proj, weight)
    near = first[0] + to_core(first[1], "grad_first_core")
    outgoing = pl.pallas_call(
        outgoing_kernel,
        out_shape=shape((2 * rows, width), bf16),
        in_specs=[VMEM] * 4 + [ANY] * 2,
        out_specs=VMEM,
        compiler_params=params(8),
        cost_estimate=cost(0.5),
        name="outgoing",
    )(result_a, result_b, first[2], to_core(first[3], "grad_first_across"), *right_beside)
    received = to_y(outgoing, "result_and_grad_first_y")
    input_grad, result = pl.pallas_call(
        finish_kernel,
        out_shape=[shape(wide, f32), shape(wide, bf16)],
        in_specs=[SMEM] + [VMEM] * 9,
        out_specs=[VMEM] * 2,
        compiler_params=params(16),
        cost_estimate=cost(1.5),
        name="finish",
    )(me, text_rows, prompt, onehot, gain_one, grad_middle, near, received, middle, own_result)

    band_rows = right_state.shape[0]
    prompt_grad, left_new, right_new, new_prompt = pl.pallas_call(
        update_kernel,
        out_shape=[
            shape((prompt_rows, width), f32),
            shape((prompt_rows, prompt_rows), f32),
            shape((band_rows, width), f32),
            shape((prompt_rows, width), f32),
        ],
        in_specs=[SMEM] + [VMEM] * 9,
        out_specs=[VMEM] * 4,
        scratch_shapes=[
            pltpu.VMEM((slots, width), f32),
            pltpu.VMEM((slots, slots), f32),
            pltpu.VMEM((width, width), bf16),
            pltpu.VMEM((slots + width, width), bf16),
            pltpu.VMEM((width, width), bf16),
            pltpu.VMEM((width, width), bf16),
        ],
        compiler_params=params(40),
        cost_estimate=cost(16),
        name="update",
    )(
        place, part, part_beside, prompt, left_state, right_near, right_far, *right_beside,
        right_state,
    )
    return result, input_grad, prompt_grad, left_new, right_new, new_prompt


def solution(mesh):
    sizes = dict(mesh.shape)
    return jax.shard_map(
        functools.partial(local, dp_size=sizes["dp"], mp_size=sizes["mp"]),
        mesh=mesh,
        in_specs=(
            P(("dp", "mp"), None),
            P("dp", None),
            P(),
            P("dp", None),
            P(),
            P(),
            P(None, None, "mp"),
            P("mp", None),
            P(None, "mp"),
            P("mp", None),
            P(None, "mp"),
            P(("dp", "mp"), None),
            P(),
            P("dp", None),
        ),
        out_specs=(P(("dp", "mp"), None), P(("dp", "mp"), None), P(), P(), P("dp", None), P()),
        check_vma=False,
    )
```

```python
import functools

import jax
import jax.numpy as jnp
from jax import lax
from jax.experimental import pallas as pl
from jax.experimental.pallas import tpu as pltpu
from jax.sharding import PartitionSpec as P

ROOT_STEPS = 5
HEAD = 64
SEGMENTS = 8
PENALTY = -1000000000.0

norm_epsilon = 1e-06
step_rate = 0.5
bucket_edges = (12, 16, 23, 32, 46, 64, 91)
bf16 = jnp.bfloat16
f32 = jnp.float32
MIB = 1024 * 1024
TILE = 256

VMEM = pl.BlockSpec(memory_space=pltpu.VMEM)
ANY = pl.BlockSpec(memory_space=pl.ANY)
SMEM = pl.BlockSpec(memory_space=pltpu.SMEM)


def dot(left, right):
    return lax.dot_general(left, right, (((1,), (0,)), ((), ())), preferred_element_type=f32)


def dot_t(left, right):
    return lax.dot_general(left, right, (((1,), (1,)), ((), ())), preferred_element_type=f32)


def dot_rows(left, right):
    return lax.dot_general(left, right, (((0,), (0,)), ((), ())), preferred_element_type=f32)


def split(values):
    high = values.astype(bf16)
    return high, (values - high.astype(f32)).astype(bf16)


def swap(array, axis, count, bit, name):
    with jax.named_scope(name):
        return lax.ppermute(array, axis, [(i, i ^ bit) for i in range(count)])


def rms_scale(values):
    return lax.rsqrt(jnp.mean(values * values, axis=-1, keepdims=True) + norm_epsilon)


def norm_back(values, gain, grad):
    scale = rms_scale(values)
    inner = gain * grad
    mean = jnp.mean(values * inner, axis=-1, keepdims=True)
    return scale * inner - values * (scale * scale * scale * mean)


def params(limit=56):
    return pltpu.CompilerParams(vmem_limit_bytes=limit * MIB)


def cost(time):
    return pl.CostEstimate(flops=int(time), bytes_accessed=int(time * 3.5e6), transcendentals=0)


def cast_kernel(member, right, _, out):
    half = out.shape[1]
    columns = pl.ds(pl.multiple_of((member[0] & 1) * half, half), half)
    out[...] = right[:, columns].astype(bf16)


def relay_kernel(
    table, found, received, text, right, _cotangent, _up, _down, out, text_out
):
    out[...] = found[...] + received[...]
    text_out[...] = text[...]


def prep_kernel(
    member, table, segments, x0, x1, x2, x3, gain, weight,
    onehot, onehot_t, key_mark, query_mark, band, out,
):
    length = segments.shape[1]
    slots = onehot_t.shape[0]
    heads, tall, wide = band.shape
    tile = tall // 4
    segment = segments[...]
    first = jnp.zeros_like(segment)
    for number in range(1, SEGMENTS):
        before = jnp.sum(jnp.where(segment < number, 1.0, 0.0), axis=-1, keepdims=True)
        first = jnp.where(segment == number, before.astype(jnp.int32), first)
    offset = lax.broadcasted_iota(jnp.int32, segment.shape, 1) - first
    slot = jnp.where(offset < table[0, heads].astype(jnp.int32), offset, -1)
    placed = lax.broadcasted_iota(jnp.int32, (slots, length), 0) == slot
    placed = jnp.where(placed, 1.0, 0.0)
    onehot_t[...] = placed.astype(bf16)
    onehot[...] = jnp.transpose(placed).astype(bf16)
    lanes = key_mark.shape[1]
    spare = heads * HEAD % lanes
    segment_t = jnp.transpose(jnp.broadcast_to(segment.astype(f32), (lanes, length)))
    lane = lax.broadcasted_iota(jnp.int32, (length, lanes), 1) - spare
    tile_at = lax.broadcasted_iota(jnp.int32, (length, lanes), 0) // tile
    in_segment = (lane >= 0) & (lane < SEGMENTS)
    in_tile = (lane >= SEGMENTS) & (lane < SEGMENTS + length // tile)
    same = segment_t == lane.astype(f32)
    other_tile = lane - SEGMENTS
    key_mark[...] = jnp.where(
        (in_segment & ~same) | (in_tile & (tile_at == other_tile)), 1.0, 0.0
    ).astype(bf16)
    for head in range(heads):
        values = jnp.where(in_segment & same, PENALTY, 0.0)
        values = jnp.where(in_tile & (other_tile < tile_at - 1), table[15, head], values)
        values = jnp.where(in_tile & (other_tile > tile_at + 1), table[31, head], values)
        query_mark[head] = values.astype(bf16)
    rows = lax.broadcasted_iota(jnp.int32, (tile, tile), 0)
    columns = lax.broadcasted_iota(jnp.int32, (tile, tile), 1)
    zero = jnp.zeros((tile, tile), f32)
    for head in range(heads):
        band[head, :tile, tile:] = zero
        band[head, 3 * tile :, :tile] = zero
    for shift in (-1, 0, 1):
        relative = rows - columns + shift * tile
        distance = jnp.abs(relative)
        bucket = jnp.full((tile, tile), 8, jnp.int32)
        for edge in bucket_edges:
            bucket = bucket + jnp.where(distance >= edge, 1, 0)
        bucket = jnp.where(distance < 8, distance, bucket) + jnp.where(relative > 0, 16, 0)
        numbers = {-1: range(1, 16), 0: (*range(0, 16), *range(17, 32)), 1: range(17, 32)}[shift]
        values = [zero] * heads
        for number in numbers:
            here = bucket == number
            values = [jnp.where(here, table[number, head], values[head]) for head in range(heads)]
        for head in range(heads):
            for half in range(2):
                at = (shift + 1 + half) * tile
                band[head, at : at + tile, half * tile : half * tile + tile] = values[head]

    me = member[0]
    rows = x0.shape[0]
    used = weight.shape[1]
    out[:, :, used:] = jnp.zeros((3, out.shape[1], out.shape[2] - used), bf16)
    for step, ref in enumerate((x0, x1, x2, x3)):
        place = pl.ds(pl.multiple_of((me ^ step) * rows, rows), rows)
        values = ref[...].astype(f32)
        inside = jnp.max(onehot[place, :].astype(f32), axis=-1, keepdims=True) > 0.0
        scale = jnp.where(inside, 0.0, rms_scale(values))
        normed = (values * scale * gain[...].reshape(1, -1)).astype(bf16)
        for part in range(3):
            out[part, place, :used] = dot_t(normed, weight[part]).astype(bf16)


def lane_head(rows, lanes):
    return lax.broadcasted_iota(jnp.int32, (rows, lanes), 1) // HEAD


def marked_keys(keys, key, key_mark):
    lanes = key_mark.shape[1]
    keys[:, :lanes] = key[:, :lanes]
    keys[:, lanes:] = key[:, lanes:] + key_mark[...]


def block_scores(scores, keys, queries, marks, which, head, band, block):
    rows = queries.shape[0]
    length = keys.shape[0]
    mine = jnp.where(which == head, queries, marks)
    margin = rows // 2
    scores[margin : margin + length, :] = dot_t(keys[...], mine)
    near = pl.ds(pl.multiple_of(block * rows, rows), 2 * rows)
    scores[near, :] += band[head]
    return scores[margin : margin + length, :]


def padded_marks(query_mark, head, place, lanes):
    marks = query_mark[head, place, :]
    return jnp.concatenate([jnp.zeros((marks.shape[0], lanes - marks.shape[1]), bf16), marks], axis=1)


def attend_blocks(steps, member, proj, key_mark, query_mark, band, refs):
    contexts, exact, log_rows, keys, scores_buf = refs
    rows = contexts.shape[2]
    used = contexts.shape[1]
    heads = used // HEAD
    lanes = proj.shape[2]
    marked_keys(keys, proj[1], key_mark)
    which = lane_head(rows, lanes)
    for at, step in enumerate(steps):
        block = member[0] ^ step
        place = pl.ds(pl.multiple_of(block * rows, rows), rows)
        queries = proj[0, place, :]
        mixed = jnp.zeros((rows, lanes), f32)
        sums = []
        for head in range(heads):
            marks = padded_marks(query_mark, head, place, lanes)
            scores = block_scores(
                scores_buf.at[head], keys, queries, marks, which, head, band, block
            )
            row_max = jnp.max(scores, axis=0, keepdims=True)
            exponent = jnp.exp(scores - row_max)
            row_sum = jnp.sum(exponent, axis=0, keepdims=True)
            mixed = jnp.where(which == head, dot_rows(exponent.astype(bf16), proj[2]), mixed)
            log_rows[at, head : head + 1, :] = row_max + jnp.log(row_sum)
            sums.append(jnp.broadcast_to(1.0 / row_sum, (HEAD, rows)))
        context = jnp.transpose(mixed)[:used] * jnp.concatenate(sums, axis=0)
        contexts[at] = context.astype(bf16)
        exact[at] = context


def join(near, far, out):
    count = near.shape[0]
    out[:count] = near[...]
    out[count:] = far[...]


def forward_first(
    steps, member, found, beside, gain, weight, onehot, text, key_mark, query_mark, band,
    near, far, prompt, proj, joined, *refs
):
    join(near, far, joined)
    share = found.shape[0]
    core = member[0] & 1
    prompt[pl.ds(pl.multiple_of(core * share, share), share), :] = found[...]
    prompt[pl.ds(pl.multiple_of((1 - core) * share, share), share), :] = beside[...]
    values = prompt[...].astype(f32)
    normed = (values * rms_scale(values) * gain[...].reshape(1, -1)).astype(bf16)
    used = weight.shape[1]
    for part in range(3):
        projected = dot_t(normed, weight[part]).astype(bf16)
        proj[part, :, :used] = text[part, :, :used] + dot(onehot[...], projected).astype(bf16)
    proj[:, :, used:] = text[:, :, used:]
    attend_blocks(steps, member, proj, key_mark, query_mark, band, refs)


def forward_second(steps, member, proj, key_mark, query_mark, band, near, far, joined, *refs):
    join(near, far, joined)
    attend_blocks(steps, member, proj, key_mark, query_mark, band, refs)


def own_input(member, step, text, prompt, onehot):
    rows = text.shape[0]
    mine = onehot[pl.ds(pl.multiple_of((member[0] ^ step) * rows, rows), rows), :]
    inside = jnp.max(mine.astype(f32), axis=-1, keepdims=True) > 0.0
    return mine, inside, jnp.where(inside, dot(mine, prompt[...]), text[...].astype(f32))


def middle_kernel(
    member, text, text_y, prompt, onehot, left, across, weights, cotangent, out, out_y, cot_out
):
    cot_out[...] = cotangent[...]
    for step, rows, result in ((0, text, out), (2, text_y, out_y)):
        at = step // 2
        layer_in = own_input(member, step, rows, prompt, onehot)[2]
        part = left.shape[1]
        added = dot(jnp.transpose(left[1 - at]), weights[:part])
        added = added + dot(jnp.transpose(across[at]), weights[part:])
        result[...] = layer_in + added


def ffn_kernel(step, place, start, gain, cotangent, near, far, *refs):
    outs_w, ups, downs = refs[:2], refs[2:4], refs[4:6]
    result, middle_out, grad_second = refs[6:9]
    at = step // 2
    added = dot(jnp.transpose(near[1 - at, :, place]), outs_w[0][...])
    added = added + dot(jnp.transpose(far[at, :, place]), outs_w[1][...])
    middle = start[place, :] + added
    if middle_out is not None:
        middle_out[...] = middle
    second = (middle * rms_scale(middle) * gain[...].reshape(1, -1)).astype(bf16)
    cot = cotangent[place, :]
    total = jnp.zeros_like(middle)
    grad = jnp.zeros_like(middle)
    root = 0.7978845608028654
    for up, down in zip(ups, downs):
        hidden = dot(second, up[...])
        square = hidden * hidden
        tanh = jnp.tanh(root * hidden * (1.0 + 0.044715 * square))
        half = 0.5 + 0.5 * tanh
        active = (hidden * half).astype(bf16)
        slope = half + (0.5 * root) * hidden * (1.0 - tanh * tanh) * (1.0 + 0.134145 * square)
        grad_hidden = (dot_t(cot, down[...]) * slope).astype(bf16)
        grad = grad + dot_t(grad_hidden, up[...])
        total = total + dot(active, down[...])
    grad_second[...] = grad.astype(grad_second.dtype)
    result[...] = total.astype(result.dtype)


def post_kernel(member, middle, gain, cotangent, onehot, own, received, received_b, *refs):
    weight, weight_y, pair, grad_middle_out, prompt_part = refs[:5]
    sends = refs[5:]
    part = weight.shape[0]
    outs_w = (weight, pair.at[:part], weight_y, pair.at[part:])
    rows, half = own.shape[0], received.shape[0]
    received = jnp.concatenate([received[...], received_b[...]]).astype(f32)
    grad_second = own[...] + received
    grad_middle = cotangent[...].astype(f32) + norm_back(middle[...], gain[...].reshape(1, -1), grad_second)
    grad_middle_out[...] = grad_middle
    send = grad_middle.astype(bf16)
    for out, weight in zip(sends, outs_w):
        out[...] = dot_t(weight[...], send).astype(bf16)
    mine_t = jnp.transpose(onehot[pl.ds(pl.multiple_of(member[0] * rows, rows), rows), :])
    high, low = split(grad_middle)
    prompt_part[...] = dot(mine_t, high) + dot(mine_t, low)


def back_blocks(steps, member, proj, key_mark, query_mark, band, grads, exact, log_rows, grad_query, sums, started, buffers):
    keys, prob_buf, grad_buf, query_all, out_all, scores_buf = buffers
    key_sum, value_sum = sums
    rows = grads[0].shape[1]
    heads = grads[0].shape[0] // HEAD
    lanes = proj.shape[2]
    marked_keys(keys, proj[1], key_mark)
    which = lane_head(rows, lanes)
    for at, step in enumerate(steps):
        block = member[0] ^ step
        place = pl.ds(pl.multiple_of(block * rows, rows), rows)
        queries = proj[0, place, :]
        grad_t = jnp.concatenate(
            [grads[at][...], jnp.zeros((lanes - heads * HEAD, rows), bf16)], axis=0
        )
        grad_out = jnp.transpose(grad_t)
        mixed = jnp.zeros((rows, lanes), f32)
        for head in range(heads):
            near = which == head
            own_grad = jnp.where(near, grad_out, jnp.zeros_like(grad_out))
            part = slice(head * HEAD, head * HEAD + HEAD)
            stack = slice(head * rows, head * rows + rows)
            query_all[stack, :] = jnp.where(near, queries, jnp.zeros_like(queries))
            out_all[stack, :] = own_grad
            marks = padded_marks(query_mark, head, place, lanes)
            scores = block_scores(
                scores_buf.at[head], keys, queries, marks, which, head, band, block
            )
            probs = jnp.exp(scores - log_rows[at, head : head + 1, :])
            prob_buf[:, stack] = probs.astype(bf16)
            grad_probs = dot_t(proj[2], own_grad)
            inner = jnp.sum(grads[at][part, :].astype(f32) * exact[at, part, :], axis=0, keepdims=True)
            grad_scores = (probs * (grad_probs - inner)).astype(bf16)
            grad_buf[:, stack] = grad_scores
            mixed = jnp.where(near, dot_rows(grad_scores, proj[1]), mixed)
        grad_query(step, place, mixed.astype(bf16))
        more_keys = dot(grad_buf[...], query_all[...])
        more_values = dot(prob_buf[...], out_all[...])
        if at == 0 and not started:
            key_sum[...] = more_keys
            value_sum[...] = more_values
        else:
            key_sum[...] += more_keys
            value_sum[...] += more_values


def back_first(steps, member, proj, key_mark, query_mark, band, *refs):
    grads, exact, log_rows = refs[0:2], refs[2], refs[3]
    query_out, key_sum, value_sum = refs[4:7]

    def store(step, place, values):
        query_out[steps.index(step)] = values

    back_blocks(steps, member, proj, key_mark, query_mark, band, grads, exact, log_rows, store,
                (key_sum, value_sum), False, refs[7:])


def back_second(steps, member, proj, key_mark, query_mark, band, *refs):
    grads, exact, log_rows = refs[0:2], refs[2], refs[3]
    query_in, key_in, value_in = refs[4:7]
    onehot_t, prompt, gain, weight, prompt_part, far, out, part_mine, part_other, far_out = refs[7:17]
    key_sum, value_sum, total_buf = refs[17:20]
    rows = grads[0].shape[1]
    far_out[...] = far[...]
    key_sum[...] = key_in[...]
    value_sum[...] = value_in[...]

    def store(step, place, values):
        out[0, place, :] = values

    for at in range(2):
        out[0, pl.ds(pl.multiple_of((member[0] ^ at) * rows, rows), rows), :] = query_in[at]
    back_blocks(steps, member, proj, key_mark, query_mark, band, grads, exact, log_rows, store,
                (key_sum, value_sum), True, refs[20:])
    out[1] = key_sum[...].astype(bf16)
    out[2] = value_sum[...].astype(bf16)
    grad = jnp.zeros((prompt.shape[0], prompt.shape[1]), f32)
    for part in range(3):
        high, low = split(dot(onehot_t[...], out[part])[:, : weight.shape[1]])
        grad = grad + dot(high, weight[part]) + dot(low, weight[part])
    total_buf[...] = prompt_part[...] + norm_back(prompt[...].astype(f32), gain[...].reshape(1, -1), grad)
    kept, half = part_mine.shape
    core = member[0] & 1
    part_mine[...] = total_buf[:kept, pl.ds(pl.multiple_of(core * half, half), half)]
    part_other[...] = total_buf[:kept, pl.ds(pl.multiple_of((1 - core) * half, half), half)]


def first_kernel(member, grad_proj, weight, *outs):
    rows = outs[0].shape[0]
    used = weight.shape[1]
    for step, out in enumerate(outs):
        place = pl.ds(pl.multiple_of((member[0] ^ step) * rows, rows), rows)
        total = dot(grad_proj[0, place, :used], weight[0])
        for part in (1, 2):
            total = total + dot(grad_proj[part, place, :used], weight[part])
        out[...] = total.astype(out.dtype)


def outgoing_kernel(result_a, result_b, own, other, _near, _far, out):
    rows = own.shape[0]
    out[: rows // 2] = result_a[...]
    out[rows // 2 : rows] = result_b[...]
    out[rows:] = own[...] + other[...]


def finish_kernel(
    member, text, prompt, onehot, gain, grad_middle, own, received, middle, own_result, out, result
):
    rows = text.shape[0]
    _, inside, layer_in = own_input(member, 0, text, prompt, onehot)
    grad_first = own[...].astype(f32) + received[rows:].astype(f32)
    start = grad_middle[...] + norm_back(layer_in, gain[...].reshape(1, -1), grad_first)
    out[...] = jnp.where(inside, 0.0, start)
    result[...] = (middle[...] + own_result[...] + received[:rows].astype(f32)).astype(bf16)


def newton_step(current):
    low = current.astype(bf16)
    inner = -0.625 * current + 0.0625 * dot(low, low)
    inner_low = inner.astype(bf16)
    outer = 3.125 * inner + dot(inner_low, inner_low)
    return 2.44140625 * current + dot(outer.astype(bf16), low)


def put_columns(target, first, block, values):
    low = values.astype(bf16)
    begin = block * TILE
    lanes = slice(begin, begin + TILE)
    target[first : first + begin + TILE, lanes] = low
    if block:
        target[first + begin : first + begin + TILE, :begin] = jnp.transpose(low[:begin])


def update_kernel(
    place, mine, other, prompt, left, near_a, far_a, near_b, far_b, band_state,
    grad_out, left_out, band_out, prompt_out, grad, left_pad, right, matrix, inner_buf, outer_buf,
):
    kept, half = mine.shape
    count, width = prompt_out.shape
    band = band_state.shape[0]
    size = grad.shape[0]
    core = place[0]
    half_rows = width // 2
    grad[...] = jnp.zeros_like(grad)
    for side, pieces in ((core, (near_a, far_a)), (1 - core, (near_b, far_b))):
        columns = pl.ds(pl.multiple_of(side * half, half), half)
        for at in range(width // band):
            source = pieces[at * band // half_rows]
            begin = at * band % half_rows
            target = at * band
            if band % 16 == 0:
                target = pl.multiple_of((place[1] ^ at) * band, 16)
            elif at * band % half_rows:
                continue
            count_rows = band if band % 16 == 0 else half_rows
            right[pl.ds(target, count_rows), columns] = source[begin : begin + count_rows, :]
    grad[:kept, pl.ds(pl.multiple_of(core * half, half), half)] = mine[...]
    grad[:kept, pl.ds(pl.multiple_of((1 - core) * half, half), half)] = other[...]
    value = grad[...]
    grad_out[...] = value[:count]
    high, low = split(value)
    high_t, low_t = jnp.transpose(high), jnp.transpose(low)
    left_gram = dot(high, high_t) + dot(high, low_t) + dot(low, high_t)
    left_new = 0.5 * left[...] + 0.5 * left_gram[:count, :count]
    left_out[...] = left_new

    tops = [begin + TILE for begin in range(0, width, TILE)]
    columns = []
    total = 0.0
    for top in tops:
        lanes = slice(top - TILE, top)
        values = 0.5 * right[:top, lanes].astype(f32) + 0.5 * dot(high_t[:top], high[:, lanes])
        squares = values * values
        if top > TILE:
            total = total + 2.0 * jnp.sum(squares[: top - TILE])
        total = total + jnp.sum(squares[top - TILE :])
        columns.append(values)
    right_scale = 1.25 * lax.rsqrt(total)
    pick = (
        lax.broadcasted_iota(jnp.int32, (band, width), 1)
        == lax.broadcasted_iota(jnp.int32, (band, width), 0) + place[1] * band
    )
    pick = jnp.where(pick, 1.0, 0.0).astype(bf16)
    pick_high, pick_low = dot_t(pick, high).astype(bf16), dot_t(pick, low).astype(bf16)
    band_out[...] = 0.5 * band_state[...] + 0.5 * (
        dot(pick_high, high) + dot(pick_high, low) + dot(pick_low, high)
    )

    left_pad[...] = jnp.zeros_like(left_pad)
    left_pad[:count, :count] = left_new
    left_mat = left_pad[...]
    left_scale = 1.25 * lax.rsqrt(jnp.sum(left_mat * left_mat))
    left_mat = left_mat * left_scale
    root = jnp.where(
        lax.broadcasted_iota(jnp.int32, (size, size), 0)
        == lax.broadcasted_iota(jnp.int32, (size, size), 1),
        1.0,
        0.0,
    )
    thin = value
    columns = [values * right_scale for values in columns]
    for block, values in enumerate(columns):
        put_columns(matrix, size, block, values)
    for repeat in range(ROOT_STEPS - 2):
        matrix[:size, :] = thin.astype(bf16)
        inner, thin_parts = [], []
        for block, top in enumerate(tops):
            lanes = slice(top - TILE, top)
            product = dot(matrix[: size + top, :], matrix[size:, lanes])
            thin_parts.append(product[:size])
            inner.append(-0.625 * columns[block] + 0.0625 * product[size:])
            put_columns(inner_buf, 0, block, inner[block])
        thin = 1.25 * thin - 0.25 * jnp.concatenate(thin_parts, axis=1)
        root = 1.25 * root - 0.25 * dot(root.astype(bf16), left_mat.astype(bf16))
        left_mat = newton_step(left_mat)
        for block, top in enumerate(tops):
            lanes = slice(top - TILE, top)
            outer = 3.125 * inner[block] + dot(inner_buf[:top, :], inner_buf[:, lanes])
            put_columns(outer_buf, 0, block, outer)
        for block, top in enumerate(tops):
            lanes = slice(top - TILE, top)
            columns[block] = 2.44140625 * columns[block] + dot(
                outer_buf[:top, :], matrix[size:, lanes]
            )
        for block, values in enumerate(columns):
            put_columns(matrix, size, block, values)

    def thin_dot(values):
        return dot(values.astype(bf16), matrix[size:, :])

    root = 1.25 * root - 0.25 * dot(root.astype(bf16), left_mat.astype(bf16))
    left_mat = newton_step(left_mat)
    thin = 1.25 * thin - 0.25 * thin_dot(thin)
    power = thin
    for repeat in range(4):
        power = 1.25 * power - 0.25 * thin_dot(power)
    thin = 1.25 * thin - 0.25 * thin_dot(power)
    root = 1.25 * root - 0.25 * dot(root.astype(bf16), left_mat.astype(bf16))
    direction = dot(root.astype(bf16), thin.astype(bf16))
    scale = jnp.sqrt(jnp.sqrt(left_scale)) * jnp.sqrt(jnp.sqrt(right_scale))
    direction = (direction * scale)[:count]
    prompt_value = prompt[...].astype(f32)[:count]
    cells = 1.0 / (count * width)
    ratio = jnp.sqrt(jnp.sum(prompt_value * prompt_value) * cells + norm_epsilon) * lax.rsqrt(
        jnp.sum(direction * direction) * cells + norm_epsilon
    )
    prompt_out[...] = prompt_value - step_rate * ratio * direction


def local(
    text_rows, segment_ids, vocab_ids, embed_table, gain_one, gain_two, qkv_weight, out_weight,
    ffn_in_weight, ffn_out_weight, rel_table, cotangent, left_state, right_state,
    *, dp_size, mp_size,
):
    member = lax.axis_index("mp")
    dp_index = lax.axis_index("dp")
    core = member % 2
    rows, width = text_rows.shape
    length = segment_ids.shape[1]
    prompt_rows = vocab_ids.shape[0]
    table_rows = embed_table.shape[0]
    heads = rel_table.shape[1]
    head_lanes = heads * HEAD
    lanes = -(-(head_lanes + SEGMENTS + length // 128) // 128) * 128
    slots = 128
    kept = -(-prompt_rows // 8) * 8
    me = jnp.reshape(member, (1,))
    dp_bits = [1 << bit for bit in range(dp_size.bit_length() - 1)]
    shape = jax.ShapeDtypeStruct

    def to_core(array, name):
        return swap(array, "mp", mp_size, 1, name)

    def to_y(array, name):
        return swap(array, "mp", mp_size, 2, name)

    def to_across(array, name):
        return swap(array, "mp", mp_size, 3, name)

    place = jnp.stack([core, dp_index]).astype(jnp.int32)

    text_y, cot_y = to_y(text_rows, "text_y"), to_y(cotangent, "cotangent_y")
    up_c = to_core(ffn_in_weight, "up_core")
    down_c = to_core(ffn_out_weight, "down_core")
    right_near = pl.pallas_call(
        cast_kernel,
        out_shape=shape((right_state.shape[0], width // 2), bf16),
        in_specs=[SMEM, VMEM, ANY],
        out_specs=VMEM,
        compiler_params=params(4),
        cost_estimate=cost(1),
        name="cast",
    )(me, right_state, text_y)
    right_far = swap(right_near, "dp", dp_size, dp_bits[0], "right_x")
    text_c = to_core(text_rows, "text_core")

    share = slots // 2
    padded = jnp.pad(vocab_ids, (0, slots - prompt_rows), constant_values=-1)
    ids = lax.dynamic_slice_in_dim(padded, core * share, share)
    local_ids = jnp.where(ids >= 0, ids - dp_index * table_rows, -1)
    picked = local_ids[:, None] == jnp.arange(table_rows, dtype=jnp.int32)[None, :]
    found = dot(picked.astype(bf16), embed_table).astype(bf16)

    table = jnp.concatenate(
        [rel_table.astype(f32), jnp.full((rel_table.shape[0], 1), prompt_rows, f32)], axis=1
    )
    weight = jnp.transpose(qkv_weight, (1, 2, 0))
    found = found + swap(found, "dp", dp_size, dp_bits[0], "prompt_x")
    found = found + swap(found, "dp", dp_size, dp_bits[1], "prompt_z")
    for bit in dp_bits[2:-1]:
        found = found + swap(found, "dp", dp_size, bit, "prompt_far")
    found, text_y = pl.pallas_call(
        relay_kernel,
        out_shape=[
            shape(found.shape, bf16),
            shape((rows, width), bf16),
        ],
        in_specs=[SMEM] + [VMEM] * 4 + [ANY] * 3,
        out_specs=[VMEM] * 2,
        compiler_params=params(8),
        cost_estimate=cost(0.5),
        name="relay",
    )(
        table, found, swap(found, "dp", dp_size, dp_bits[-1], "prompt_far"), text_y,
        right_far, cot_y, up_c, down_c,
    )
    text_d = to_core(text_y, "text_across")
    out_y = to_y(out_weight, "out_y")

    proj_shape = shape((3, length, lanes), bf16)
    onehot, onehot_t, key_mark, query_mark, band, text_proj = pl.pallas_call(
        prep_kernel,
        out_shape=[
            shape((length, slots), bf16),
            shape((slots, length), bf16),
            shape((length, 128), bf16),
            shape((heads, length, 128), bf16),
            shape((heads, 512, 256), f32),
            proj_shape,
        ],
        in_specs=[SMEM, SMEM] + [VMEM] * 7,
        out_specs=[VMEM] * 6,
        compiler_params=params(16),
        cost_estimate=cost(3.5),
        name="project",
    )(me, table, segment_ids, text_rows, text_c, text_y, text_d, gain_one, weight)

    beside = to_core(found, "prompt_core")

    context_shapes = [shape((2, head_lanes, rows), bf16), shape((2, head_lanes, rows), f32), shape((2, heads, rows), f32)]
    score_buffer = pltpu.VMEM((heads, length + rows, rows), f32)
    forward_scratch = [pltpu.VMEM((length, lanes), bf16), score_buffer]
    joined = shape((2 * right_state.shape[0], width // 2), bf16)
    prompt, proj, right_near, ctx_near, exact_near, log_near = pl.pallas_call(
        functools.partial(forward_first, (3, 1)),
        out_shape=[shape((slots, width), bf16), proj_shape, joined] + context_shapes,
        in_specs=[SMEM] + [VMEM] * 11,
        out_specs=[VMEM] * 6,
        scratch_shapes=forward_scratch,
        compiler_params=params(24),
        cost_estimate=cost(4.5),
        name="attend",
    )(
        me, found, beside, gain_one, weight, onehot, text_proj, key_mark, query_mark, band,
        right_near, right_far,
    )
    got_d = to_across(ctx_near, "context_across")
    got_c = to_core(ctx_near, "context_core")
    out_pair, ctx_far, exact_far, log_far = pl.pallas_call(
        functools.partial(forward_second, (2, 0)),
        out_shape=[shape((2 * head_lanes, width), bf16)] + context_shapes,
        in_specs=[SMEM] + [VMEM] * 6,
        out_specs=[VMEM] * 4,
        scratch_shapes=forward_scratch,
        compiler_params=params(24),
        cost_estimate=cost(4.5),
        name="attend",
    )(me, proj, key_mark, query_mark, band, out_weight, out_y)
    out_pair = to_core(out_pair, "out_core")
    got_y = to_y(ctx_far, "context_y")
    right_far = swap(right_near, "dp", dp_size, dp_bits[1], "right_z")

    units = ffn_in_weight.shape[1]
    wide = (rows, width)

    half = rows // 2

    def far_first(*refs):
        join(refs[11], refs[12], refs[15])
        ffn_kernel(2, slice(0, half), *refs[:11], refs[13], None, refs[14])

    def far_second(*refs):
        ffn_kernel(2, slice(half, rows), *refs[:11], refs[11], None, refs[12])

    def ffn(body, start, cot, out_shape, *extra):
        return pl.pallas_call(
            body,
            out_shape=out_shape,
            in_specs=[VMEM] * (11 + len(extra)),
            out_specs=[VMEM] * len(out_shape),
            compiler_params=params(24),
            cost_estimate=cost(4.5),
            name="ffn",
        )(
            start, gain_two, cot, ctx_far, got_y, out_weight, out_y,
            ffn_in_weight, up_c, ffn_out_weight, down_c, *extra,
        )

    start, start_y, cot_y = pl.pallas_call(
        middle_kernel,
        out_shape=[shape(wide, f32)] * 2 + [shape(wide, bf16)],
        in_specs=[SMEM] + [VMEM] * 8,
        out_specs=[VMEM] * 3,
        compiler_params=params(16),
        cost_estimate=cost(2),
        name="middle",
    )(me, text_rows, text_y, prompt, onehot, got_c, got_d, out_pair, cot_y)
    half_rows = shape((rows // 2, width), bf16)
    joined = shape((4 * right_state.shape[0], width // 2), bf16)
    result_a, grad_a, right_near = ffn(
        far_first, start_y, cot_y, [half_rows, half_rows, joined], right_near, right_far
    )
    result_b, grad_b = ffn(far_second, start_y, cot_y, [half_rows, half_rows])
    right_far = swap(right_near, "dp", dp_size, dp_bits[2], "right_far")
    got_grad = [to_y(piece, "grad_second_y") for piece in (grad_a, grad_b)]
    own_result, middle, own_grad = ffn(
        functools.partial(ffn_kernel, 0, slice(0, rows)), start, cotangent, [shape(wide, f32)] * 3
    )

    send_shape = shape((head_lanes, rows), bf16)
    grad_middle, prompt_part, send_0, send_1, send_2, send_3 = pl.pallas_call(
        post_kernel,
        out_shape=[shape(wide, f32), shape((slots, width), f32)] + [send_shape] * 4,
        in_specs=[SMEM] + [VMEM] * 10,
        out_specs=[VMEM] * 6,
        compiler_params=params(16),
        cost_estimate=cost(2.2),
        name="post",
    )(me, middle, gain_two, cotangent, onehot, own_grad, *got_grad, out_weight, out_y, out_pair)
    back_2, back_3 = to_y(send_2, "grad_context_y"), to_across(send_3, "grad_context_across")
    back_1 = to_core(send_1, "grad_context_core")

    back_scratch = [
        pltpu.VMEM((length, lanes), bf16),
        pltpu.VMEM((length, heads * rows), bf16),
        pltpu.VMEM((length, heads * rows), bf16),
        pltpu.VMEM((heads * rows, lanes), bf16),
        pltpu.VMEM((heads * rows, lanes), bf16),
        score_buffer,
    ]
    sum_shape = shape((length, lanes), f32)
    exact_a, log_a = jnp.stack([exact_far[1], exact_near[1]]), jnp.stack([log_far[1], log_near[1]])
    exact_b, log_b = jnp.stack([exact_far[0], exact_near[0]]), jnp.stack([log_far[0], log_near[0]])
    query_a, key_a, value_a = pl.pallas_call(
        functools.partial(back_first, (0, 1)),
        out_shape=[shape((2, rows, lanes), bf16), sum_shape, sum_shape],
        in_specs=[SMEM] + [VMEM] * 8,
        out_specs=[VMEM] * 3,
        scratch_shapes=back_scratch,
        compiler_params=params(32),
        cost_estimate=cost(6.5),
        name="attend_back",
    )(me, proj, key_mark, query_mark, band, send_0, back_1, exact_a, log_a)
    grad_proj, part, part_other, right_far = pl.pallas_call(
        functools.partial(back_second, (2, 3)),
        out_shape=[proj_shape] + [shape((kept, width // 2), f32)] * 2 + [shape(right_far.shape, bf16)],
        in_specs=[SMEM] + [VMEM] * 17,
        out_specs=[VMEM] * 4,
        scratch_shapes=[pltpu.VMEM((length, lanes), f32)] * 2 + [pltpu.VMEM((slots, width), f32)] + back_scratch,
        compiler_params=params(36),
        cost_estimate=cost(6.5),
        name="attend_back",
    )(
        me, proj, key_mark, query_mark, band, back_2, back_3, exact_b, log_b, query_a, key_a, value_a,
        onehot_t, prompt, gain_one, weight, prompt_part, right_far,
    )

    for bit in dp_bits[3:]:
        right_near = jnp.concatenate([right_near, right_far])
        right_far = swap(right_near, "dp", dp_size, bit, "right_far")
    if right_state.shape[0] % 16:
        blocks = jnp.concatenate([right_near, right_far]).reshape(dp_size, -1, width // 2)
        blocks = jnp.take(blocks, jnp.arange(dp_size) ^ dp_index, axis=0).reshape(width, width // 2)
        right_near, right_far = blocks[: width // 2], blocks[width // 2 :]
    right_beside = [to_core(right_near, "right_core"), to_core(right_far, "right_core")]

    part = part + to_core(part_other, "prompt_grad_core")

    def add_pair(values, axis, size, bit):
        sent = values.astype(bf16)
        return sent.astype(f32) + swap(sent, axis, size, bit, "prompt_grad_sum").astype(f32)

    sent = part.astype(bf16)
    beyond = lax.ppermute(
        sent, ("dp", "mp"),
        [(i, i ^ (mp_size + 2)) for i in range(dp_size * mp_size)],
    ).astype(f32)
    over_y = swap(sent, "mp", mp_size, 2, "prompt_grad_y").astype(f32)
    over_x = swap(sent, "dp", dp_size, dp_bits[0], "prompt_grad_x").astype(f32)
    part = (beyond + over_x) + (over_y + sent.astype(f32))
    for bit in dp_bits[1:]:
        part = add_pair(part, "dp", dp_size, bit)
    part_beside = to_core(part, "prompt_grad_other")

    first = pl.pallas_call(
        first_kernel,
        out_shape=[shape(wide, bf16)] * 4,
        in_specs=[SMEM] + [VMEM] * 2,
        out_specs=[VMEM] * 4,
        compiler_params=params(16),
        cost_estimate=cost(1.5),
        name="grad_first",
    )(me, grad_proj, weight)
    near = first[0] + to_core(first[1], "grad_first_core")
    outgoing = pl.pallas_call(
        outgoing_kernel,
        out_shape=shape((2 * rows, width), bf16),
        in_specs=[VMEM] * 4 + [ANY] * 2,
        out_specs=VMEM,
        compiler_params=params(8),
        cost_estimate=cost(0.5),
        name="outgoing",
    )(result_a, result_b, first[2], to_core(first[3], "grad_first_across"), *right_beside)
    received = to_y(outgoing, "result_and_grad_first_y")
    input_grad, result = pl.pallas_call(
        finish_kernel,
        out_shape=[shape(wide, f32), shape(wide, bf16)],
        in_specs=[SMEM] + [VMEM] * 9,
        out_specs=[VMEM] * 2,
        compiler_params=params(16),
        cost_estimate=cost(1.5),
        name="finish",
    )(me, text_rows, prompt, onehot, gain_one, grad_middle, near, received, middle, own_result)

    band_rows = right_state.shape[0]
    prompt_grad, left_new, right_new, new_prompt = pl.pallas_call(
        update_kernel,
        out_shape=[
            shape((prompt_rows, width), f32),
            shape((prompt_rows, prompt_rows), f32),
            shape((band_rows, width), f32),
            shape((prompt_rows, width), f32),
        ],
        in_specs=[SMEM] + [VMEM] * 9,
        out_specs=[VMEM] * 4,
        scratch_shapes=[
            pltpu.VMEM((slots, width), f32),
            pltpu.VMEM((slots, slots), f32),
            pltpu.VMEM((width, width), bf16),
            pltpu.VMEM((slots + width, width), bf16),
            pltpu.VMEM((width, width), bf16),
            pltpu.VMEM((width, width), bf16),
        ],
        compiler_params=params(40),
        cost_estimate=cost(16),
        name="update",
    )(
        place, part, part_beside, prompt, left_state, right_near, right_far, *right_beside,
        right_state,
    )
    return result, input_grad, prompt_grad, left_new, right_new, new_prompt


def solution(mesh):
    sizes = dict(mesh.shape)
    return jax.shard_map(
        functools.partial(local, dp_size=sizes["dp"], mp_size=sizes["mp"]),
        mesh=mesh,
        in_specs=(
            P(("dp", "mp"), None),
            P("dp", None),
            P(),
            P("dp", None),
            P(),
            P(),
            P(None, None, "mp"),
            P("mp", None),
            P(None, "mp"),
            P("mp", None),
            P(None, "mp"),
            P(("dp", "mp"), None),
            P(),
            P("dp", None),
        ),
        out_specs=(P(("dp", "mp"), None), P(("dp", "mp"), None), P(), P(), P("dp", None), P()),
        check_vma=False,
    )
```

```python
import functools

import jax
import jax.numpy as jnp
from jax import lax
from jax.experimental import pallas as pl
from jax.experimental.pallas import tpu as pltpu
from jax.sharding import PartitionSpec as P

ROOT_STEPS = 5
HEAD = 64
SEGMENTS = 8
PENALTY = -1000000000.0

norm_epsilon = 1e-06
step_rate = 0.5
bucket_edges = (12, 16, 23, 32, 46, 64, 91)
bf16 = jnp.bfloat16
f32 = jnp.float32
MIB = 1024 * 1024
TILE = 256

VMEM = pl.BlockSpec(memory_space=pltpu.VMEM)
ANY = pl.BlockSpec(memory_space=pl.ANY)
SMEM = pl.BlockSpec(memory_space=pltpu.SMEM)


def dot(left, right):
    return lax.dot_general(left, right, (((1,), (0,)), ((), ())), preferred_element_type=f32)


def dot_t(left, right):
    return lax.dot_general(left, right, (((1,), (1,)), ((), ())), preferred_element_type=f32)


def dot_rows(left, right):
    return lax.dot_general(left, right, (((0,), (0,)), ((), ())), preferred_element_type=f32)


def split(values):
    high = values.astype(bf16)
    return high, (values - high.astype(f32)).astype(bf16)


def swap(array, axis, count, bit, name):
    with jax.named_scope(name):
        return lax.ppermute(array, axis, [(i, i ^ bit) for i in range(count)])


def rms_scale(values):
    return lax.rsqrt(jnp.mean(values * values, axis=-1, keepdims=True) + norm_epsilon)


def norm_back(values, gain, grad):
    scale = rms_scale(values)
    inner = gain * grad
    mean = jnp.mean(values * inner, axis=-1, keepdims=True)
    return scale * inner - values * (scale * scale * scale * mean)


def params(limit=56):
    return pltpu.CompilerParams(vmem_limit_bytes=limit * MIB)


def cost(time):
    return pl.CostEstimate(flops=int(time), bytes_accessed=int(time * 3.5e6), transcendentals=0)


def cast_kernel(member, right, _, out):
    half = out.shape[1]
    columns = pl.ds(pl.multiple_of((member[0] & 1) * half, half), half)
    out[...] = right[:, columns].astype(bf16)


def relay_kernel(
    table, found, received, text, right, _cotangent, _up, _down, out, text_out
):
    out[...] = found[...] + received[...]
    text_out[...] = text[...]


def prep_kernel(
    member, table, segments, x0, x1, x2, x3, gain, weight,
    onehot, onehot_t, key_mark, query_mark, band, out,
):
    length = segments.shape[1]
    slots = onehot_t.shape[0]
    heads, tall, wide = band.shape
    tile = tall // 4
    segment = segments[...]
    first = jnp.zeros_like(segment)
    for number in range(1, SEGMENTS):
        before = jnp.sum(jnp.where(segment < number, 1.0, 0.0), axis=-1, keepdims=True)
        first = jnp.where(segment == number, before.astype(jnp.int32), first)
    offset = lax.broadcasted_iota(jnp.int32, segment.shape, 1) - first
    slot = jnp.where(offset < table[0, heads].astype(jnp.int32), offset, -1)
    placed = lax.broadcasted_iota(jnp.int32, (slots, length), 0) == slot
    placed = jnp.where(placed, 1.0, 0.0)
    onehot_t[...] = placed.astype(bf16)
    onehot[...] = jnp.transpose(placed.astype(bf16))
    lanes = key_mark.shape[1]
    spare = heads * HEAD % lanes
    spread = jnp.broadcast_to(segment.astype(f32), (lanes, length)).astype(bf16)
    segment_t = jnp.transpose(spread).astype(f32)
    lane = lax.broadcasted_iota(jnp.int32, (length, lanes), 1) - spare
    tile_at = lax.broadcasted_iota(jnp.int32, (length, lanes), 0) // tile
    in_segment = (lane >= 0) & (lane < SEGMENTS)
    in_tile = (lane >= SEGMENTS) & (lane < SEGMENTS + length // tile)
    same = segment_t == lane.astype(f32)
    other_tile = lane - SEGMENTS
    key_mark[...] = jnp.where(
        (in_segment & ~same) | (in_tile & (tile_at == other_tile)), 1.0, 0.0
    ).astype(bf16)
    for head in range(heads):
        values = jnp.where(in_segment & same, PENALTY, 0.0)
        values = jnp.where(in_tile & (other_tile < tile_at - 1), table[15, head], values)
        values = jnp.where(in_tile & (other_tile > tile_at + 1), table[31, head], values)
        query_mark[head] = values.astype(bf16)
    rows = lax.broadcasted_iota(jnp.int32, (tile, tile), 0)
    columns = lax.broadcasted_iota(jnp.int32, (tile, tile), 1)
    zero = jnp.zeros((tile, tile), f32)
    for head in range(heads):
        band[head, :tile, tile:] = zero
        band[head, 3 * tile :, :tile] = zero
    for shift in (-1, 0, 1):
        relative = rows - columns + shift * tile
        distance = jnp.abs(relative)
        bucket = jnp.full((tile, tile), 8, jnp.int32)
        for edge in bucket_edges:
            bucket = bucket + jnp.where(distance >= edge, 1, 0)
        bucket = jnp.where(distance < 8, distance, bucket) + jnp.where(relative > 0, 16, 0)
        numbers = {-1: range(1, 16), 0: (*range(0, 16), *range(17, 32)), 1: range(17, 32)}[shift]
        values = [zero] * heads
        for number in numbers:
            here = bucket == number
            values = [jnp.where(here, table[number, head], values[head]) for head in range(heads)]
        for head in range(heads):
            for half in range(2):
                at = (shift + 1 + half) * tile
                band[head, at : at + tile, half * tile : half * tile + tile] = values[head]

    me = member[0]
    rows = x0.shape[0]
    used = weight.shape[1]
    out[:, :, used:] = jnp.zeros((3, out.shape[1], out.shape[2] - used), bf16)
    for step, ref in enumerate((x0, x1, x2, x3)):
        place = pl.ds(pl.multiple_of((me ^ step) * rows, rows), rows)
        values = ref[...].astype(f32)
        inside = jnp.max(onehot[place, :].astype(f32), axis=-1, keepdims=True) > 0.0
        scale = jnp.where(inside, 0.0, rms_scale(values))
        normed = (values * scale * gain[...].reshape(1, -1)).astype(bf16)
        for part in range(3):
            out[part, place, :used] = dot_t(normed, weight[part]).astype(bf16)


def lane_head(rows, lanes):
    return lax.broadcasted_iota(jnp.int32, (rows, lanes), 1) // HEAD


def marked_keys(keys, key, key_mark):
    lanes = key_mark.shape[1]
    keys[:, :lanes] = key[:, :lanes]
    keys[:, lanes:] = key[:, lanes:] + key_mark[...]


def block_scores(scores, keys, queries, marks, which, head, band, block):
    rows = queries.shape[0]
    length = keys.shape[0]
    mine = jnp.where(which == head, queries, marks)
    margin = rows // 2
    scores[margin : margin + length, :] = dot_t(keys[...], mine)
    near = pl.ds(pl.multiple_of(block * rows, rows), 2 * rows)
    scores[near, :] += band[head]
    return scores[margin : margin + length, :]


def padded_marks(query_mark, head, place, lanes):
    marks = query_mark[head, place, :]
    return jnp.concatenate([jnp.zeros((marks.shape[0], lanes - marks.shape[1]), bf16), marks], axis=1)


def attend_blocks(steps, member, proj, key_mark, query_mark, band, refs):
    contexts, exact, log_rows, keys, scores_buf = refs
    rows = contexts.shape[2]
    used = contexts.shape[1]
    heads = used // HEAD
    lanes = proj.shape[2]
    marked_keys(keys, proj[1], key_mark)
    which = lane_head(rows, lanes)
    for at, step in enumerate(steps):
        block = member[0] ^ step
        place = pl.ds(pl.multiple_of(block * rows, rows), rows)
        queries = proj[0, place, :]
        mixed = jnp.zeros((rows, lanes), f32)
        sums = []
        for head in range(heads):
            marks = padded_marks(query_mark, head, place, lanes)
            scores = block_scores(
                scores_buf.at[head], keys, queries, marks, which, head, band, block
            )
            row_max = jnp.max(scores, axis=0, keepdims=True)
            exponent = jnp.exp(scores - row_max)
            row_sum = jnp.sum(exponent, axis=0, keepdims=True)
            mixed = jnp.where(which == head, dot_rows(exponent.astype(bf16), proj[2]), mixed)
            log_rows[at, head : head + 1, :] = row_max + jnp.log(row_sum)
            sums.append(jnp.broadcast_to(1.0 / row_sum, (HEAD, rows)))
        context = jnp.transpose(mixed)[:used] * jnp.concatenate(sums, axis=0)
        contexts[at] = context.astype(bf16)
        exact[at] = context


def join(near, far, out):
    count = near.shape[0]
    out[:count] = near[...]
    out[count:] = far[...]


def forward_first(
    steps, member, found, beside, gain, weight, onehot, text, key_mark, query_mark, band,
    near, far, prompt, proj, joined, *refs
):
    join(near, far, joined)
    share = found.shape[0]
    core = member[0] & 1
    prompt[pl.ds(pl.multiple_of(core * share, share), share), :] = found[...]
    prompt[pl.ds(pl.multiple_of((1 - core) * share, share), share), :] = beside[...]
    values = prompt[...].astype(f32)
    normed = (values * rms_scale(values) * gain[...].reshape(1, -1)).astype(bf16)
    used = weight.shape[1]
    for part in range(3):
        projected = dot_t(normed, weight[part]).astype(bf16)
        proj[part, :, :used] = text[part, :, :used] + dot(onehot[...], projected).astype(bf16)
    proj[:, :, used:] = text[:, :, used:]
    attend_blocks(steps, member, proj, key_mark, query_mark, band, refs)


def forward_second(steps, member, proj, key_mark, query_mark, band, near, far, joined, *refs):
    join(near, far, joined)
    attend_blocks(steps, member, proj, key_mark, query_mark, band, refs)


def own_input(member, step, text, prompt, onehot):
    rows = text.shape[0]
    mine = onehot[pl.ds(pl.multiple_of((member[0] ^ step) * rows, rows), rows), :]
    inside = jnp.max(mine.astype(f32), axis=-1, keepdims=True) > 0.0
    return mine, inside, jnp.where(inside, dot(mine, prompt[...]), text[...].astype(f32))


def middle_kernel(
    member, text, text_y, prompt, onehot, left, across, weights, cotangent, out, out_y, cot_out
):
    cot_out[...] = cotangent[...]
    for step, rows, result in ((0, text, out), (2, text_y, out_y)):
        at = step // 2
        layer_in = own_input(member, step, rows, prompt, onehot)[2]
        part = left.shape[1]
        added = dot(jnp.transpose(left[1 - at]), weights[:part])
        added = added + dot(jnp.transpose(across[at]), weights[part:])
        result[...] = layer_in + added


def ffn_kernel(step, place, start, gain, cotangent, near, far, *refs):
    outs_w, ups, downs = refs[:2], refs[2:4], refs[4:6]
    result, middle_out, grad_second = refs[6:9]
    at = step // 2
    added = dot(jnp.transpose(near[1 - at, :, place]), outs_w[0][...])
    added = added + dot(jnp.transpose(far[at, :, place]), outs_w[1][...])
    middle = start[place, :] + added
    if middle_out is not None:
        middle_out[...] = middle
    second = (middle * rms_scale(middle) * gain[...].reshape(1, -1)).astype(bf16)
    cot = cotangent[place, :]
    total = jnp.zeros_like(middle)
    grad = jnp.zeros_like(middle)
    root = 0.7978845608028654
    for up, down in zip(ups, downs):
        hidden = dot(second, up[...])
        square = hidden * hidden
        tanh = jnp.tanh(root * hidden * (1.0 + 0.044715 * square))
        half = 0.5 + 0.5 * tanh
        active = (hidden * half).astype(bf16)
        slope = half + (0.5 * root) * hidden * (1.0 - tanh * tanh) * (1.0 + 0.134145 * square)
        grad_hidden = (dot_t(cot, down[...]) * slope).astype(bf16)
        grad = grad + dot_t(grad_hidden, up[...])
        total = total + dot(active, down[...])
    grad_second[...] = grad.astype(grad_second.dtype)
    result[...] = total.astype(result.dtype)


def post_kernel(member, middle, gain, cotangent, onehot, own, received, received_b, *refs):
    weight, weight_y, pair, grad_middle_out, prompt_part = refs[:5]
    sends = refs[5:]
    part = weight.shape[0]
    outs_w = (weight, pair.at[:part], weight_y, pair.at[part:])
    rows, half = own.shape[0], received.shape[0]
    received = jnp.concatenate([received[...], received_b[...]]).astype(f32)
    grad_second = own[...] + received
    grad_middle = cotangent[...].astype(f32) + norm_back(middle[...], gain[...].reshape(1, -1), grad_second)
    grad_middle_out[...] = grad_middle
    send = grad_middle.astype(bf16)
    for out, weight in zip(sends, outs_w):
        out[...] = dot_t(weight[...], send).astype(bf16)
    mine_t = jnp.transpose(onehot[pl.ds(pl.multiple_of(member[0] * rows, rows), rows), :])
    high, low = split(grad_middle)
    prompt_part[...] = dot(mine_t, high) + dot(mine_t, low)


def back_blocks(steps, member, proj, key_mark, query_mark, band, grads, exact, log_rows, grad_query, sums, started, buffers):
    keys, prob_buf, grad_buf, query_all, out_all, scores_buf = buffers
    key_sum, value_sum = sums
    rows = grads[0].shape[1]
    heads = grads[0].shape[0] // HEAD
    lanes = proj.shape[2]
    marked_keys(keys, proj[1], key_mark)
    which = lane_head(rows, lanes)
    for at, step in enumerate(steps):
        block = member[0] ^ step
        place = pl.ds(pl.multiple_of(block * rows, rows), rows)
        queries = proj[0, place, :]
        grad_t = jnp.concatenate(
            [grads[at][...], jnp.zeros((lanes - heads * HEAD, rows), bf16)], axis=0
        )
        grad_out = jnp.transpose(grad_t)
        mixed = jnp.zeros((rows, lanes), f32)
        for head in range(heads):
            near = which == head
            own_grad = jnp.where(near, grad_out, jnp.zeros_like(grad_out))
            part = slice(head * HEAD, head * HEAD + HEAD)
            stack = slice(head * rows, head * rows + rows)
            query_all[stack, :] = jnp.where(near, queries, jnp.zeros_like(queries))
            out_all[stack, :] = own_grad
            marks = padded_marks(query_mark, head, place, lanes)
            scores = block_scores(
                scores_buf.at[head], keys, queries, marks, which, head, band, block
            )
            probs = jnp.exp(scores - log_rows[at, head : head + 1, :])
            prob_buf[:, stack] = probs.astype(bf16)
            grad_probs = dot_t(proj[2], own_grad)
            inner = jnp.sum(grads[at][part, :].astype(f32) * exact[at, part, :], axis=0, keepdims=True)
            grad_scores = (probs * (grad_probs - inner)).astype(bf16)
            grad_buf[:, stack] = grad_scores
            mixed = jnp.where(near, dot_rows(grad_scores, proj[1]), mixed)
        grad_query(step, place, mixed.astype(bf16))
        more_keys = dot(grad_buf[...], query_all[...])
        more_values = dot(prob_buf[...], out_all[...])
        if at == 0 and not started:
            key_sum[...] = more_keys
            value_sum[...] = more_values
        else:
            key_sum[...] += more_keys
            value_sum[...] += more_values


def back_first(steps, member, proj, key_mark, query_mark, band, *refs):
    grads, exact, log_rows = refs[0:2], refs[2], refs[3]
    query_out, key_sum, value_sum = refs[4:7]

    def store(step, place, values):
        query_out[steps.index(step)] = values

    back_blocks(steps, member, proj, key_mark, query_mark, band, grads, exact, log_rows, store,
                (key_sum, value_sum), False, refs[7:])


def back_second(steps, member, proj, key_mark, query_mark, band, *refs):
    grads, exact, log_rows = refs[0:2], refs[2], refs[3]
    query_in, key_in, value_in = refs[4:7]
    onehot_t, prompt, gain, weight, prompt_part, far, out, part_mine, part_other, far_out = refs[7:17]
    key_sum, value_sum, total_buf = refs[17:20]
    rows = grads[0].shape[1]
    far_out[...] = far[...]
    key_sum[...] = key_in[...]
    value_sum[...] = value_in[...]

    def store(step, place, values):
        out[0, place, :] = values

    for at in range(2):
        out[0, pl.ds(pl.multiple_of((member[0] ^ at) * rows, rows), rows), :] = query_in[at]
    back_blocks(steps, member, proj, key_mark, query_mark, band, grads, exact, log_rows, store,
                (key_sum, value_sum), True, refs[20:])
    out[1] = key_sum[...].astype(bf16)
    out[2] = value_sum[...].astype(bf16)
    grad = jnp.zeros((prompt.shape[0], prompt.shape[1]), f32)
    for part in range(3):
        high, low = split(dot(onehot_t[...], out[part])[:, : weight.shape[1]])
        grad = grad + dot(high, weight[part]) + dot(low, weight[part])
    total_buf[...] = prompt_part[...] + norm_back(prompt[...].astype(f32), gain[...].reshape(1, -1), grad)
    kept, half = part_mine.shape
    core = member[0] & 1
    part_mine[...] = total_buf[:kept, pl.ds(pl.multiple_of(core * half, half), half)]
    part_other[...] = total_buf[:kept, pl.ds(pl.multiple_of((1 - core) * half, half), half)]


def first_kernel(member, grad_proj, weight, *outs):
    rows = outs[0].shape[0]
    used = weight.shape[1]
    for step, out in enumerate(outs):
        place = pl.ds(pl.multiple_of((member[0] ^ step) * rows, rows), rows)
        total = dot(grad_proj[0, place, :used], weight[0])
        for part in (1, 2):
            total = total + dot(grad_proj[part, place, :used], weight[part])
        out[...] = total.astype(out.dtype)


def outgoing_kernel(result_a, result_b, own, other, _near, _far, out):
    rows = own.shape[0]
    out[: rows // 2] = result_a[...]
    out[rows // 2 : rows] = result_b[...]
    out[rows:] = own[...] + other[...]


def finish_kernel(
    member, text, prompt, onehot, gain, grad_middle, own, received, middle, own_result, out, result
):
    rows = text.shape[0]
    _, inside, layer_in = own_input(member, 0, text, prompt, onehot)
    grad_first = own[...].astype(f32) + received[rows:].astype(f32)
    start = grad_middle[...] + norm_back(layer_in, gain[...].reshape(1, -1), grad_first)
    out[...] = jnp.where(inside, 0.0, start)
    result[...] = (middle[...] + own_result[...] + received[:rows].astype(f32)).astype(bf16)


def newton_step(current):
    low = current.astype(bf16)
    inner = -0.625 * current + 0.0625 * dot(low, low)
    inner_low = inner.astype(bf16)
    outer = 3.125 * inner + dot(inner_low, inner_low)
    return 2.44140625 * current + dot(outer.astype(bf16), low)


def put_columns(target, first, block, values):
    low = values.astype(bf16)
    begin = block * TILE
    lanes = slice(begin, begin + TILE)
    target[first : first + begin + TILE, lanes] = low
    if block:
        target[first + begin : first + begin + TILE, :begin] = jnp.transpose(low[:begin])


def update_kernel(
    place, mine, other, prompt, left, near_a, far_a, near_b, far_b, band_state,
    grad_out, left_out, band_out, prompt_out, grad, left_pad, right, matrix, inner_buf, outer_buf,
):
    kept, half = mine.shape
    count, width = prompt_out.shape
    band = band_state.shape[0]
    size = grad.shape[0]
    core = place[0]
    half_rows = width // 2
    grad[kept:, :] = jnp.zeros((size - kept, width), f32)
    for side, pieces in ((core, (near_a, far_a)), (1 - core, (near_b, far_b))):
        columns = pl.ds(pl.multiple_of(side * half, half), half)
        for at in range(width // band):
            source = pieces[at * band // half_rows]
            begin = at * band % half_rows
            target = at * band
            if band % 16 == 0:
                target = pl.multiple_of((place[1] ^ at) * band, 16)
            elif at * band % half_rows:
                continue
            count_rows = band if band % 16 == 0 else half_rows
            right[pl.ds(target, count_rows), columns] = source[begin : begin + count_rows, :]
    grad[:kept, pl.ds(pl.multiple_of(core * half, half), half)] = mine[...]
    grad[:kept, pl.ds(pl.multiple_of((1 - core) * half, half), half)] = other[...]
    value = grad[...]
    grad_out[...] = value[:count]
    high, low = split(value)
    high_t, low_t = jnp.transpose(high), jnp.transpose(low)
    left_gram = dot(high, high_t) + dot(high, low_t) + dot(low, high_t)
    left_new = 0.5 * left[...] + 0.5 * left_gram[:count, :count]
    left_out[...] = left_new

    tops = [begin + TILE for begin in range(0, width, TILE)]
    columns = []
    total = 0.0
    for top in tops:
        lanes = slice(top - TILE, top)
        values = 0.5 * right[:top, lanes].astype(f32) + 0.5 * dot(high_t[:top], high[:, lanes])
        squares = values * values
        if top > TILE:
            total = total + 2.0 * jnp.sum(squares[: top - TILE])
        total = total + jnp.sum(squares[top - TILE :])
        columns.append(values)
    right_scale = 1.25 * lax.rsqrt(total)
    pick = (
        lax.broadcasted_iota(jnp.int32, (band, width), 1)
        == lax.broadcasted_iota(jnp.int32, (band, width), 0) + place[1] * band
    )
    pick = jnp.where(pick, 1.0, 0.0).astype(bf16)
    pick_high, pick_low = dot_t(pick, high).astype(bf16), dot_t(pick, low).astype(bf16)
    band_out[...] = 0.5 * band_state[...] + 0.5 * (
        dot(pick_high, high) + dot(pick_high, low) + dot(pick_low, high)
    )

    left_pad[...] = jnp.zeros_like(left_pad)
    left_pad[:count, :count] = left_new
    left_mat = left_pad[...]
    left_scale = 1.25 * lax.rsqrt(jnp.sum(left_mat * left_mat))
    left_mat = left_mat * left_scale
    root = jnp.where(
        lax.broadcasted_iota(jnp.int32, (size, size), 0)
        == lax.broadcasted_iota(jnp.int32, (size, size), 1),
        1.0,
        0.0,
    )
    thin = value
    columns = [values * right_scale for values in columns]
    for block, values in enumerate(columns):
        put_columns(matrix, size, block, values)
    for repeat in range(ROOT_STEPS - 2):
        matrix[:size, :] = thin.astype(bf16)
        inner, thin_parts = [], []
        for block, top in enumerate(tops):
            lanes = slice(top - TILE, top)
            product = dot(matrix[: size + top, :], matrix[size:, lanes])
            thin_parts.append(product[:size])
            inner.append(-0.625 * columns[block] + 0.0625 * product[size:])
            put_columns(inner_buf, 0, block, inner[block])
        thin = 1.25 * thin - 0.25 * jnp.concatenate(thin_parts, axis=1)
        root = 1.25 * root - 0.25 * dot(root.astype(bf16), left_mat.astype(bf16))
        left_mat = newton_step(left_mat)
        for block, top in enumerate(tops):
            lanes = slice(top - TILE, top)
            outer = 3.125 * inner[block] + dot(inner_buf[:top, :], inner_buf[:, lanes])
            put_columns(outer_buf, 0, block, outer)
        for block, top in enumerate(tops):
            lanes = slice(top - TILE, top)
            columns[block] = 2.44140625 * columns[block] + dot(
                outer_buf[:top, :], matrix[size:, lanes]
            )
        for block, values in enumerate(columns):
            put_columns(matrix, size, block, values)

    def thin_dot(values):
        return dot(values.astype(bf16), matrix[size:, :])

    root = 1.25 * root - 0.25 * dot(root.astype(bf16), left_mat.astype(bf16))
    left_mat = newton_step(left_mat)
    thin = 1.25 * thin - 0.25 * thin_dot(thin)
    power = thin
    for repeat in range(4):
        power = 1.25 * power - 0.25 * thin_dot(power)
    thin = 1.25 * thin - 0.25 * thin_dot(power)
    root = 1.25 * root - 0.25 * dot(root.astype(bf16), left_mat.astype(bf16))
    direction = dot(root.astype(bf16), thin.astype(bf16))
    scale = jnp.sqrt(jnp.sqrt(left_scale)) * jnp.sqrt(jnp.sqrt(right_scale))
    direction = (direction * scale)[:count]
    prompt_value = prompt[...].astype(f32)[:count]
    cells = 1.0 / (count * width)
    ratio = jnp.sqrt(jnp.sum(prompt_value * prompt_value) * cells + norm_epsilon) * lax.rsqrt(
        jnp.sum(direction * direction) * cells + norm_epsilon
    )
    prompt_out[...] = prompt_value - step_rate * ratio * direction


def local(
    text_rows, segment_ids, vocab_ids, embed_table, gain_one, gain_two, qkv_weight, out_weight,
    ffn_in_weight, ffn_out_weight, rel_table, cotangent, left_state, right_state,
    *, dp_size, mp_size,
):
    member = lax.axis_index("mp")
    dp_index = lax.axis_index("dp")
    core = member % 2
    rows, width = text_rows.shape
    length = segment_ids.shape[1]
    prompt_rows = vocab_ids.shape[0]
    table_rows = embed_table.shape[0]
    heads = rel_table.shape[1]
    head_lanes = heads * HEAD
    lanes = -(-(head_lanes + SEGMENTS + length // 128) // 128) * 128
    slots = 128
    kept = -(-prompt_rows // 8) * 8
    me = jnp.reshape(member, (1,))
    dp_bits = [1 << bit for bit in range(dp_size.bit_length() - 1)]
    shape = jax.ShapeDtypeStruct

    def to_core(array, name):
        return swap(array, "mp", mp_size, 1, name)

    def to_y(array, name):
        return swap(array, "mp", mp_size, 2, name)

    def to_across(array, name):
        return swap(array, "mp", mp_size, 3, name)

    place = jnp.stack([core, dp_index]).astype(jnp.int32)

    text_y, cot_y = to_y(text_rows, "text_y"), to_y(cotangent, "cotangent_y")
    up_c = to_core(ffn_in_weight, "up_core")
    down_c = to_core(ffn_out_weight, "down_core")
    right_near = pl.pallas_call(
        cast_kernel,
        out_shape=shape((right_state.shape[0], width // 2), bf16),
        in_specs=[SMEM, VMEM, ANY],
        out_specs=VMEM,
        compiler_params=params(4),
        cost_estimate=cost(1),
        name="cast",
    )(me, right_state, text_y)
    right_far = swap(right_near, "dp", dp_size, dp_bits[0], "right_x")
    text_c = to_core(text_rows, "text_core")

    share = slots // 2
    padded = jnp.pad(vocab_ids, (0, slots - prompt_rows), constant_values=-1)
    ids = lax.dynamic_slice_in_dim(padded, core * share, share)
    local_ids = jnp.where(ids >= 0, ids - dp_index * table_rows, -1)
    picked = local_ids[:, None] == jnp.arange(table_rows, dtype=jnp.int32)[None, :]
    found = dot(picked.astype(bf16), embed_table).astype(bf16)

    table = jnp.concatenate(
        [rel_table.astype(f32), jnp.full((rel_table.shape[0], 1), prompt_rows, f32)], axis=1
    )
    weight = jnp.transpose(qkv_weight, (1, 2, 0))
    found = found + swap(found, "dp", dp_size, dp_bits[0], "prompt_x")
    found = found + swap(found, "dp", dp_size, dp_bits[1], "prompt_z")
    for bit in dp_bits[2:-1]:
        found = found + swap(found, "dp", dp_size, bit, "prompt_far")
    found, text_y = pl.pallas_call(
        relay_kernel,
        out_shape=[
            shape(found.shape, bf16),
            shape((rows, width), bf16),
        ],
        in_specs=[SMEM] + [VMEM] * 4 + [ANY] * 3,
        out_specs=[VMEM] * 2,
        compiler_params=params(8),
        cost_estimate=cost(0.5),
        name="relay",
    )(
        table, found, swap(found, "dp", dp_size, dp_bits[-1], "prompt_far"), text_y,
        right_far, cot_y, up_c, down_c,
    )
    text_d = to_core(text_y, "text_across")
    out_y = to_y(out_weight, "out_y")

    proj_shape = shape((3, length, lanes), bf16)
    onehot, onehot_t, key_mark, query_mark, band, text_proj = pl.pallas_call(
        prep_kernel,
        out_shape=[
            shape((length, slots), bf16),
            shape((slots, length), bf16),
            shape((length, 128), bf16),
            shape((heads, length, 128), bf16),
            shape((heads, 512, 256), f32),
            proj_shape,
        ],
        in_specs=[SMEM, SMEM] + [VMEM] * 7,
        out_specs=[VMEM] * 6,
        compiler_params=params(16),
        cost_estimate=cost(3.5),
        name="project",
    )(me, table, segment_ids, text_rows, text_c, text_y, text_d, gain_one, weight)

    beside = to_core(found, "prompt_core")

    context_shapes = [shape((2, head_lanes, rows), bf16), shape((2, head_lanes, rows), f32), shape((2, heads, rows), f32)]
    score_buffer = pltpu.VMEM((heads, length + rows, rows), f32)
    forward_scratch = [pltpu.VMEM((length, lanes), bf16), score_buffer]
    joined = shape((2 * right_state.shape[0], width // 2), bf16)
    prompt, proj, right_near, ctx_near, exact_near, log_near = pl.pallas_call(
        functools.partial(forward_first, (3, 1)),
        out_shape=[shape((slots, width), bf16), proj_shape, joined] + context_shapes,
        in_specs=[SMEM] + [VMEM] * 11,
        out_specs=[VMEM] * 6,
        scratch_shapes=forward_scratch,
        compiler_params=params(24),
        cost_estimate=cost(4.5),
        name="attend",
    )(
        me, found, beside, gain_one, weight, onehot, text_proj, key_mark, query_mark, band,
        right_near, right_far,
    )
    got_d = to_across(ctx_near, "context_across")
    got_c = to_core(ctx_near, "context_core")
    out_pair, ctx_far, exact_far, log_far = pl.pallas_call(
        functools.partial(forward_second, (2, 0)),
        out_shape=[shape((2 * head_lanes, width), bf16)] + context_shapes,
        in_specs=[SMEM] + [VMEM] * 6,
        out_specs=[VMEM] * 4,
        scratch_shapes=forward_scratch,
        compiler_params=params(24),
        cost_estimate=cost(4.5),
        name="attend",
    )(me, proj, key_mark, query_mark, band, out_weight, out_y)
    out_pair = to_core(out_pair, "out_core")
    got_y = to_y(ctx_far, "context_y")
    right_far = swap(right_near, "dp", dp_size, dp_bits[1], "right_z")

    units = ffn_in_weight.shape[1]
    wide = (rows, width)

    half = rows // 2

    def far_first(*refs):
        join(refs[11], refs[12], refs[15])
        ffn_kernel(2, slice(0, half), *refs[:11], refs[13], None, refs[14])

    def far_second(*refs):
        ffn_kernel(2, slice(half, rows), *refs[:11], refs[11], None, refs[12])

    def ffn(body, start, cot, out_shape, *extra):
        return pl.pallas_call(
            body,
            out_shape=out_shape,
            in_specs=[VMEM] * (11 + len(extra)),
            out_specs=[VMEM] * len(out_shape),
            compiler_params=params(24),
            cost_estimate=cost(4.5),
            name="ffn",
        )(
            start, gain_two, cot, ctx_far, got_y, out_weight, out_y,
            ffn_in_weight, up_c, ffn_out_weight, down_c, *extra,
        )

    start, start_y, cot_y = pl.pallas_call(
        middle_kernel,
        out_shape=[shape(wide, f32)] * 2 + [shape(wide, bf16)],
        in_specs=[SMEM] + [VMEM] * 8,
        out_specs=[VMEM] * 3,
        compiler_params=params(16),
        cost_estimate=cost(2),
        name="middle",
    )(me, text_rows, text_y, prompt, onehot, got_c, got_d, out_pair, cot_y)
    half_rows = shape((rows // 2, width), bf16)
    joined = shape((4 * right_state.shape[0], width // 2), bf16)
    result_a, grad_a, right_near = ffn(
        far_first, start_y, cot_y, [half_rows, half_rows, joined], right_near, right_far
    )
    result_b, grad_b = ffn(far_second, start_y, cot_y, [half_rows, half_rows])
    right_far = swap(right_near, "dp", dp_size, dp_bits[2], "right_far")
    got_grad = [to_y(piece, "grad_second_y") for piece in (grad_a, grad_b)]
    own_result, middle, own_grad = ffn(
        functools.partial(ffn_kernel, 0, slice(0, rows)), start, cotangent, [shape(wide, f32)] * 3
    )

    send_shape = shape((head_lanes, rows), bf16)
    grad_middle, prompt_part, send_0, send_1, send_2, send_3 = pl.pallas_call(
        post_kernel,
        out_shape=[shape(wide, f32), shape((slots, width), f32)] + [send_shape] * 4,
        in_specs=[SMEM] + [VMEM] * 10,
        out_specs=[VMEM] * 6,
        compiler_params=params(16),
        cost_estimate=cost(2.2),
        name="post",
    )(me, middle, gain_two, cotangent, onehot, own_grad, *got_grad, out_weight, out_y, out_pair)
    back_2, back_3 = to_y(send_2, "grad_context_y"), to_across(send_3, "grad_context_across")
    back_1 = to_core(send_1, "grad_context_core")

    back_scratch = [
        pltpu.VMEM((length, lanes), bf16),
        pltpu.VMEM((length, heads * rows), bf16),
        pltpu.VMEM((length, heads * rows), bf16),
        pltpu.VMEM((heads * rows, lanes), bf16),
        pltpu.VMEM((heads * rows, lanes), bf16),
        score_buffer,
    ]
    sum_shape = shape((length, lanes), f32)
    exact_a, log_a = jnp.stack([exact_far[1], exact_near[1]]), jnp.stack([log_far[1], log_near[1]])
    exact_b, log_b = jnp.stack([exact_far[0], exact_near[0]]), jnp.stack([log_far[0], log_near[0]])
    query_a, key_a, value_a = pl.pallas_call(
        functools.partial(back_first, (0, 1)),
        out_shape=[shape((2, rows, lanes), bf16), sum_shape, sum_shape],
        in_specs=[SMEM] + [VMEM] * 8,
        out_specs=[VMEM] * 3,
        scratch_shapes=back_scratch,
        compiler_params=params(32),
        cost_estimate=cost(6.5),
        name="attend_back",
    )(me, proj, key_mark, query_mark, band, send_0, back_1, exact_a, log_a)
    grad_proj, part, part_other, right_far = pl.pallas_call(
        functools.partial(back_second, (2, 3)),
        out_shape=[proj_shape] + [shape((kept, width // 2), f32)] * 2 + [shape(right_far.shape, bf16)],
        in_specs=[SMEM] + [VMEM] * 17,
        out_specs=[VMEM] * 4,
        scratch_shapes=[pltpu.VMEM((length, lanes), f32)] * 2 + [pltpu.VMEM((slots, width), f32)] + back_scratch,
        compiler_params=params(36),
        cost_estimate=cost(6.5),
        name="attend_back",
    )(
        me, proj, key_mark, query_mark, band, back_2, back_3, exact_b, log_b, query_a, key_a, value_a,
        onehot_t, prompt, gain_one, weight, prompt_part, right_far,
    )

    for bit in dp_bits[3:]:
        right_near = jnp.concatenate([right_near, right_far])
        right_far = swap(right_near, "dp", dp_size, bit, "right_far")
    if right_state.shape[0] % 16:
        blocks = jnp.concatenate([right_near, right_far]).reshape(dp_size, -1, width // 2)
        blocks = jnp.take(blocks, jnp.arange(dp_size) ^ dp_index, axis=0).reshape(width, width // 2)
        right_near, right_far = blocks[: width // 2], blocks[width // 2 :]
    right_beside = [to_core(right_near, "right_core"), to_core(right_far, "right_core")]

    part = part + to_core(part_other, "prompt_grad_core")

    def add_pair(values, axis, size, bit):
        sent = values.astype(bf16)
        return sent.astype(f32) + swap(sent, axis, size, bit, "prompt_grad_sum").astype(f32)

    sent = part.astype(bf16)
    beyond = lax.ppermute(
        sent, ("dp", "mp"),
        [(i, i ^ (mp_size + 2)) for i in range(dp_size * mp_size)],
    ).astype(f32)
    over_y = swap(sent, "mp", mp_size, 2, "prompt_grad_y").astype(f32)
    over_x = swap(sent, "dp", dp_size, dp_bits[0], "prompt_grad_x").astype(f32)
    part = (beyond + over_x) + (over_y + sent.astype(f32))
    for bit in dp_bits[1:]:
        part = add_pair(part, "dp", dp_size, bit)
    part_beside = to_core(part, "prompt_grad_other")

    first = pl.pallas_call(
        first_kernel,
        out_shape=[shape(wide, bf16)] * 4,
        in_specs=[SMEM] + [VMEM] * 2,
        out_specs=[VMEM] * 4,
        compiler_params=params(16),
        cost_estimate=cost(1.5),
        name="grad_first",
    )(me, grad_proj, weight)
    near = first[0] + to_core(first[1], "grad_first_core")
    outgoing = pl.pallas_call(
        outgoing_kernel,
        out_shape=shape((2 * rows, width), bf16),
        in_specs=[VMEM] * 4 + [ANY] * 2,
        out_specs=VMEM,
        compiler_params=params(8),
        cost_estimate=cost(0.5),
        name="outgoing",
    )(result_a, result_b, first[2], to_core(first[3], "grad_first_across"), *right_beside)
    received = to_y(outgoing, "result_and_grad_first_y")
    input_grad, result = pl.pallas_call(
        finish_kernel,
        out_shape=[shape(wide, f32), shape(wide, bf16)],
        in_specs=[SMEM] + [VMEM] * 9,
        out_specs=[VMEM] * 2,
        compiler_params=params(16),
        cost_estimate=cost(1.5),
        name="finish",
    )(me, text_rows, prompt, onehot, gain_one, grad_middle, near, received, middle, own_result)

    band_rows = right_state.shape[0]
    prompt_grad, left_new, right_new, new_prompt = pl.pallas_call(
        update_kernel,
        out_shape=[
            shape((prompt_rows, width), f32),
            shape((prompt_rows, prompt_rows), f32),
            shape((band_rows, width), f32),
            shape((prompt_rows, width), f32),
        ],
        in_specs=[SMEM] + [VMEM] * 9,
        out_specs=[VMEM] * 4,
        scratch_shapes=[
            pltpu.VMEM((slots, width), f32),
            pltpu.VMEM((slots, slots), f32),
            pltpu.VMEM((width, width), bf16),
            pltpu.VMEM((slots + width, width), bf16),
            pltpu.VMEM((width, width), bf16),
            pltpu.VMEM((width, width), bf16),
        ],
        compiler_params=params(40),
        cost_estimate=cost(16),
        name="update",
    )(
        place, part, part_beside, prompt, left_state, right_near, right_far, *right_beside,
        right_state,
    )
    return result, input_grad, prompt_grad, left_new, right_new, new_prompt


def solution(mesh):
    sizes = dict(mesh.shape)
    return jax.shard_map(
        functools.partial(local, dp_size=sizes["dp"], mp_size=sizes["mp"]),
        mesh=mesh,
        in_specs=(
            P(("dp", "mp"), None),
            P("dp", None),
            P(),
            P("dp", None),
            P(),
            P(),
            P(None, None, "mp"),
            P("mp", None),
            P(None, "mp"),
            P("mp", None),
            P(None, "mp"),
            P(("dp", "mp"), None),
            P(),
            P("dp", None),
        ),
        out_specs=(P(("dp", "mp"), None), P(("dp", "mp"), None), P(), P(), P("dp", None), P()),
        check_vma=False,
    )
```
